32 devices in a mesh: dp: 16 (over z, y, core), mp: 2 (over x).
Axes of the slice: x: 2, y: 2, z: 4, core: 2. Of those that a mesh axis runs over, the one named last changes fastest.
Arguments:
- tokens: float32 [128, 256, 1152], P(('dp', 'mp')), may hold values from -6 to 6
- cotangent: float32 [128, 256, 1152], P(('dp', 'mp')), may hold values from -6 to 6
- bucket: int32 [128], P('dp'), may hold values from 0 to 63
- counts: int32 [16], replicated, may hold values from 1 to 8, as said below
- first_gain: float32 [1152], replicated, may hold values from 0.5 to 1.5
- first_shift: float32 [1152], replicated, may hold values from -1.75 to 1.75
- attend_weight: float32 [3, 1152, 1152], P(None, None, 'mp'), may hold values from -0.1875 to 0.1875
- time_weight: float32 [3, 1152, 1152], P(None, None, 'mp'), may hold values from -0.1875 to 0.1875
- time_table: float32 [64, 1152], replicated, may hold values from -6 to 6
- bias_table: float32 [16, 961], P('mp'), may hold values from -3 to 3
- output_weight: float32 [1152, 1152], P('mp'), may hold values from -0.5 to 0.5
- output_bias: float32 [1152], replicated, may hold values from -1.75 to 1.75
- second_gain: float32 [1152], replicated, may hold values from 0.5 to 1.5
- second_shift: float32 [1152], replicated, may hold values from -1.75 to 1.75
- hidden_weight: float32 [1152, 4608], P(None, 'mp'), may hold values from -0.1875 to 0.1875
- hidden_bias: float32 [4608], P('mp'), may hold values from -3 to 3
- return_weight: float32 [4608, 1152], P('mp'), may hold values from -0.09375 to 0.09375
- return_bias: float32 [1152], replicated, may hold values from -1.75 to 1.75
Outputs:
- result: float32 [128, 256, 1152], P(('dp', 'mp'))
- tokens_grad: float32 [128, 256, 1152], P(('dp', 'mp'))
- first_gain_grad: float32 [1152], replicated
- first_shift_grad: float32 [1152], replicated
- attend_weight_grad: float32 [3, 1152, 1152], P(None, None, 'mp')
- time_weight_grad: float32 [3, 1152, 1152], P(None, None, 'mp')
- time_table_grad: float32 [64, 1152], replicated
- bias_table_grad: float32 [16, 961], P('mp')
- output_weight_grad: float32 [1152, 1152], P('mp')
- output_bias_grad: float32 [1152], replicated
- second_gain_grad: float32 [1152], replicated
- second_shift_grad: float32 [1152], replicated
- hidden_weight_grad: float32 [1152, 4608], P(None, 'mp')
- hidden_bias_grad: float32 [4608], P('mp')
- return_weight_grad: float32 [4608, 1152], P('mp')
- return_bias_grad: float32 [1152], replicated
The draws below stay inside these ranges and needn't reach their ends.
Inputs may be any that keep to these rules, and one draw needn't show every extreme that they name: Group g holds its live images in its first counts[g] slots; some group has all 8 slots live.
All inputs are finite; a program needn't handle non-finite values.
Results may differ from the reference program's by a relative error of at most 0.0003.
Values sent between devices are 32-bit elements; how exact they have to be, the bound alone decides.
No kernel may reach another device: no remote copies, remote signals or barrier semaphores. Data moves between devices by JAX's collectives and lax.ppermute only.
A program may use at most 384 MiB of HBM per device.

```python
import jax
import jax.numpy as jnp
from jax import lax

D = 1152
HEADS = 16
HEAD_DIM = 72
FF = 4608
SIDE = 16
BUCKETS = 64
SLOT_DEV = 8
PATCHES = 256
REL = 961
GROUPS = 16
SLOTS = 128


def draw_counts(key, part):
    key = jax.random.fold_in(key, 1)
    values = jax.random.randint(key, (GROUPS,), 1, SLOT_DEV + 1)
    chosen = jax.random.randint(jax.random.fold_in(key, 2), (), 0, GROUPS)
    return jnp.where(jnp.arange(GROUPS) == chosen, SLOT_DEV, values).astype(jnp.int32)


def touch_ends(array, own_key, smallest, largest):
    longest = array.shape.index(max(array.shape))
    spots = []
    for shift in (0, 1):
        where = [jax.random.randint(jax.random.fold_in(own_key, axis), (), 0, length) for axis, length in enumerate(array.shape)]
        where[longest] = (where[longest] + shift) % array.shape[longest]
        spots.append(tuple(where))
    return array.at[spots[0]].set(smallest).at[spots[1]].set(largest)


def levels(own_key, extent, cuts, smallest, top_value):
    factor_of = 1.0
    for position, blocks in cuts:
        draws = jax.random.uniform(jax.random.fold_in(jax.random.fold_in(own_key, 6), position), (blocks,), jnp.float32, smallest / len(cuts), top_value / len(cuts))
        factor_of = factor_of * jnp.repeat(jnp.exp(draws), extent[position] // blocks).reshape((-1,) + (1,) * (len(extent) - 1 - position))
    return factor_of


def bell_draw(stream_key, shape, spread, most, shards=(), held_as=jnp.bfloat16):
    drawn = jax.random.normal(stream_key, shape, jnp.float32) * spread
    if len(shards) > 0:
        drawn = levels(stream_key, shape, shards, -0.22, 0.18) * drawn
    return jnp.clip(drawn, min=-most, max=most).astype(held_as)


def setup_inputs(seed: int = 0) -> dict:
    keys = jax.random.split(jax.random.key(seed), 19)
    return {
        "tokens": bell_draw(keys[0], (SLOTS, PATCHES, D), 1.0, 6.0, ((0, 32),), jnp.float32),
        "cotangent": bell_draw(keys[1], (SLOTS, PATCHES, D), 1.0, 6.0, ((0, 32),), jnp.float32),
        "bucket": touch_ends(jax.random.randint(keys[2], (SLOTS,), 0, BUCKETS), jax.random.fold_in(keys[2], 1), 0, BUCKETS - 1).astype(jnp.int32),
        "counts": draw_counts(jax.random.fold_in(keys[18], 71), 0),
        "first_gain": jnp.clip(1.0 + 0.1 * jax.random.normal(keys[4], (D,), jnp.float32), 0.5, 1.5),
        "first_shift": bell_draw(keys[5], (D,), 0.3, 1.75, (), jnp.float32),
        "attend_weight": bell_draw(keys[6], (3, D, D), D ** -0.5, 0.1875, ((2, 2),), jnp.float32),
        "time_weight": bell_draw(keys[7], (3, D, D), D ** -0.5, 0.1875, ((2, 2),), jnp.float32),
        "time_table": bell_draw(keys[8], (BUCKETS, D), 1.0, 6.0, (), jnp.float32),
        "bias_table": bell_draw(keys[9], (HEADS, REL), 0.5, 3.0, ((0, 2),), jnp.float32),
        "output_weight": bell_draw(keys[10], (D, D), (D // 8) ** -0.5, 0.5, ((0, 2),), jnp.float32),
        "output_bias": bell_draw(keys[11], (D,), 0.3, 1.75, (), jnp.float32),
        "second_gain": jnp.clip(1.0 + 0.1 * jax.random.normal(keys[12], (D,), jnp.float32), 0.5, 1.5),
        "second_shift": bell_draw(keys[13], (D,), 0.3, 1.75, (), jnp.float32),
        "hidden_weight": bell_draw(keys[14], (D, FF), D ** -0.5, 0.1875, ((1, 2),), jnp.float32),
        "hidden_bias": bell_draw(keys[15], (FF,), 0.5, 3.0, ((0, 2),), jnp.float32),
        "return_weight": bell_draw(keys[16], (FF, D), FF ** -0.5, 0.09375, ((0, 2),), jnp.float32),
        "return_bias": bell_draw(keys[17], (D,), 0.3, 1.75, (), jnp.float32),
    }


HIGH = lax.Precision.HIGHEST
EPS = 1e-05

def layer_norm(values, gain, shift):
    centre = values - lax.optimization_barrier(jnp.mean(values, -1, keepdims=True))
    scaled = centre * lax.rsqrt(lax.optimization_barrier(jnp.mean(centre * centre, -1, keepdims=True)) + EPS)
    return scaled * gain + shift

def relative_index(side):
    place = jnp.arange(side * side, dtype=jnp.int32)
    rows = place // side
    cols = place % side
    return ((rows[:, None] - rows[None, :] + side - 1) * (2 * side - 1) + cols[:, None] - cols[None, :] + side - 1).astype(jnp.int32)

def block(images, buckets, params):
    first_gain, first_shift, attend_weight, time_weight, time_table, bias_table, output_weight, output_bias, second_gain, second_shift, hidden_weight, hidden_bias, return_weight, return_bias = params
    normed = layer_norm(images, first_gain, first_shift)
    onehot = (buckets[:, None] == jnp.arange(BUCKETS)[None, :]).astype(jnp.float32)
    time_vec = jnp.dot(onehot, time_table, precision=HIGH)
    proj = jnp.einsum('spd,cde->cspe', normed, attend_weight, precision=HIGH)
    proj = proj + jnp.einsum('sd,cde->cse', time_vec, time_weight, precision=HIGH)[:, :, None, :]
    split = proj.reshape(3, SLOT_DEV, PATCHES, HEADS, HEAD_DIM)
    bias = bias_table[:, relative_index(SIDE)]
    scores = jnp.einsum('sphe,sqhe->shpq', split[0], split[1], precision=HIGH) * HEAD_DIM ** (-0.5) + bias[None]
    prob = jax.nn.softmax(scores, axis=-1)
    mixed = jnp.einsum('shpq,sqhe->sphe', prob, split[2], precision=HIGH).reshape(SLOT_DEV, PATCHES, D)
    middle = images + jnp.einsum('spe,ed->spd', mixed, output_weight, precision=HIGH) + output_bias
    normed_second = layer_norm(middle, second_gain, second_shift)
    hidden = jnp.einsum('spd,df->spf', normed_second, hidden_weight, precision=HIGH) + hidden_bias
    active = jax.nn.gelu(hidden, approximate=False)
    return middle + jnp.einsum('spf,fd->spd', active, return_weight, precision=HIGH) + return_bias

def reference(tokens, cotangent, bucket, counts, first_gain, first_shift, attend_weight, time_weight, time_table, bias_table, output_weight, output_bias, second_gain, second_shift, hidden_weight, hidden_bias, return_weight, return_bias):
    params = (first_gain, first_shift, attend_weight, time_weight, time_table, bias_table, output_weight, output_bias, second_gain, second_shift, hidden_weight, hidden_bias, return_weight, return_bias)
    slot = jnp.arange(SLOTS, dtype=jnp.int32)
    live = (slot % SLOT_DEV < counts[slot // SLOT_DEV]).astype(jnp.float32)
    total = jnp.sum(counts).astype(jnp.float32)
    group_buckets = bucket.reshape(GROUPS, SLOT_DEV)

    def forward(inputs, weights):
        grouped = inputs.reshape(GROUPS, SLOT_DEV, PATCHES, D)
        step = jax.checkpoint(lambda pair: block(pair[0], pair[1], weights))
        return lax.map(step, (grouped, group_buckets)).reshape(SLOTS, PATCHES, D)
    result, pull = jax.vjp(forward, tokens, params)
    tokens_grad, weight_grads = pull(cotangent * live[:, None, None])
    scaled = tuple((grad / total for grad in weight_grads))
    return (result, tokens_grad) + scaled
```

```python
import functools
import math

import jax
import jax.numpy as jnp
from jax import lax
from jax.experimental import pallas as pl
from jax.experimental.pallas import tpu as pltpu
from jax.sharding import PartitionSpec as P

HEAD_DIM = 72
SIDE = 16
PATCHES = SIDE * SIDE
STRIP = 2 * SIDE - 1
EPS = 1e-05
SCALE = HEAD_DIM ** (-0.5)
MIB = 1024 * 1024
HIGHEST = lax.Precision.HIGHEST
HIGH = lax.Precision.HIGH


def dot_nn(a, b):
    return lax.dot_general(a, b, (((1,), (0,)), ((), ())), precision=HIGH, preferred_element_type=jnp.float32)


def dot_nt(a, b):
    return lax.dot_general(a, b, (((1,), (1,)), ((), ())), precision=HIGH, preferred_element_type=jnp.float32)


def dot_tn(a, b):
    return lax.dot_general(a, b, (((0,), (0,)), ((), ())), precision=HIGH, preferred_element_type=jnp.float32)


def standardize(values):
    centre = values - jnp.mean(values, -1, keepdims=True)
    inverse = lax.rsqrt(jnp.mean(centre * centre, -1, keepdims=True) + EPS)
    return centre * inverse, inverse


def norm_back(grad_hat, scaled, inverse):
    return inverse * (
        grad_hat
        - jnp.mean(grad_hat, -1, keepdims=True)
        - scaled * jnp.mean(grad_hat * scaled, -1, keepdims=True)
    )


def head_window(head, width):
    first = head * HEAD_DIM
    start = first // 128 * 128
    stop = min(-(-(first + HEAD_DIM) // 128) * 128, width)
    return start, stop, first - start


def head_mask(head, width):
    start, stop, offset = head_window(head, width)
    lane = lax.broadcasted_iota(jnp.int32, (1, stop - start), 1)
    return (lane >= offset) & (lane < offset + HEAD_DIM)


def fixed(shape, **kw):
    return pl.BlockSpec(shape, lambda i: (0,) * len(shape), pipeline_mode=pl.Buffered(1), **kw)


def rows(count, width):
    return pl.BlockSpec((count, width), lambda i: (i, 0))


def params(limit):
    return pltpu.CompilerParams(dimension_semantics=("arbitrary",), vmem_limit_bytes=limit * MIB)


def cost(flops, nbytes, trans=0):
    return pl.CostEstimate(flops=int(flops) // 1000, bytes_accessed=int(nbytes) // 1000, transcendentals=0)


def halves(value):
    high = value.astype(jnp.bfloat16)
    return high, (value - high.astype(jnp.float32)).astype(jnp.bfloat16)


def mul(a, b, left, right):
    return lax.dot_general(a, b, (((left,), (right,)), ((), ())), preferred_element_type=jnp.float32)


def scalars():
    return pl.BlockSpec(memory_space=pltpu.SMEM)


def build_bias(strip_ref, bias_ref, heads):
    def one(head, carry):
        strip = strip_ref[head]
        for row in range(SIDE):
            shift = (SIDE - 1 - row) * SIDE
            bias_ref[head, row * SIDE : (row + 1) * SIDE, :] = strip[:, shift : shift + PATCHES]
        return carry

    lax.fori_loop(0, heads, one, 0)


def attend_forward_kernel(
    heads, tokens_ref, gain_ref, shift_ref, weight_ref, time_ref, strip_ref,
    query_ref, keys_ref, values_ref, mixed_ref, flipped_ref, lse_ref, normed_ref, bias_ref,
):
    width = query_ref.shape[1]

    @pl.when(pl.program_id(0) == 0)
    def _():
        build_bias(strip_ref, bias_ref, heads)

    scaled, _ = standardize(tokens_ref[...])
    normed = scaled * gain_ref[...] + shift_ref[...]
    normed_ref[...] = normed
    proj = dot_nt(normed, weight_ref[...]) + time_ref[0]
    query_ref[...] = proj[:, :width] * SCALE
    keys_ref[...] = proj[:, width : 2 * width]
    values_ref[...] = proj[:, 2 * width :]
    mixed_ref[...] = jnp.zeros_like(mixed_ref)
    columns = lax.broadcasted_iota(jnp.int32, (1, heads), 1)
    stats = jnp.zeros((PATCHES, heads), jnp.float32)
    for head in range(heads):
        start, stop, _ = head_window(head, width)
        mask = head_mask(head, width)
        query = jnp.where(mask, query_ref[:, start:stop], 0.0)
        scores = dot_nt(query, keys_ref[:, start:stop]) + bias_ref[head]
        peak = jnp.max(scores, -1, keepdims=True)
        weights = jnp.exp(scores - peak)
        total = jnp.sum(weights, -1, keepdims=True)
        values = jnp.where(mask, values_ref[:, start:stop], 0.0)
        mixed_ref[:, start:stop] += dot_nn(weights, values) * (1.0 / total)
        stats = jnp.where(columns == head, peak + jnp.log(total), stats)
    lse_ref[...] = stats
    flipped_ref[...] = mixed_ref[...].T


def attend_forward(tokens, gain, shift, weight, time_proj, strips):
    count, dim = tokens.shape
    heads = strips.shape[0]
    width = weight.shape[0] // 3
    images = count // PATCHES
    piece = jax.ShapeDtypeStruct((count, width), jnp.float32)
    return pl.pallas_call(
        functools.partial(attend_forward_kernel, heads),
        grid=(images,),
        in_specs=[
            rows(PATCHES, dim),
            fixed((1, dim)),
            fixed((1, dim)),
            fixed((3 * width, dim)),
            pl.BlockSpec((1, 1, 3 * width), lambda i: (i, 0, 0)),
            fixed(strips.shape),
        ],
        out_specs=[rows(PATCHES, width)] * 4
        + [pl.BlockSpec((width, PATCHES), lambda i: (0, i)), rows(PATCHES, heads), rows(PATCHES, dim)],
        out_shape=[piece] * 4
        + [
            jax.ShapeDtypeStruct((width, count), jnp.float32),
            jax.ShapeDtypeStruct((count, heads), jnp.float32),
            jax.ShapeDtypeStruct((count, dim), jnp.float32),
        ],
        scratch_shapes=[pltpu.VMEM((heads, PATCHES, PATCHES), jnp.float32)],
        compiler_params=params(56),
        cost_estimate=cost(6 * count * dim * width * 3 + 24 * count * PATCHES * 256 * heads // 2, 4 * (weight.size + 6 * count * width)),
    )(tokens, gain, shift, weight, time_proj, strips)


def output_kernel(parts, *refs):
    live_ref, tokens_ref, cotangent_ref = refs[:3]
    mixed_refs = refs[3 : 3 + parts]
    weight_refs = refs[3 + parts : 3 + 2 * parts]
    bias_ref, gain_ref, shift_ref, middle_ref, pair_ref, flip_ref, grad_pair_ref, grad_flip_ref = refs[3 + 2 * parts :]
    dim = tokens_ref.shape[1]
    middle = tokens_ref[...] + bias_ref[...]
    for mixed_ref, weight_ref in zip(mixed_refs, weight_refs):
        middle = middle + dot_nn(mixed_ref[...], weight_ref[...])
    middle_ref[...] = middle
    scaled, _ = standardize(middle)
    normed = scaled * gain_ref[...] + shift_ref[...]
    grad = cotangent_ref[...] * live_ref[pl.program_id(0)]
    for value, pair_out, flip_out in ((normed, pair_ref, flip_ref), (grad, grad_pair_ref, grad_flip_ref)):
        pair_out[:, :dim], pair_out[:, dim:] = halves(value)
        flip_out[:dim], flip_out[dim:] = halves(value.T)


def output_forward(live, tokens, cotangent, mixed, weights, bias, gain, shift):
    count, dim = tokens.shape
    parts = len(mixed)
    pair = jax.ShapeDtypeStruct((count, 2 * dim), jnp.bfloat16)
    return pl.pallas_call(
        functools.partial(output_kernel, parts),
        grid=(count // PATCHES,),
        in_specs=[scalars()]
        + [rows(PATCHES, dim)] * 2
        + [rows(PATCHES, m.shape[1]) for m in mixed]
        + [fixed(w.shape) for w in weights]
        + [fixed((1, dim))] * 3,
        out_specs=[rows(PATCHES, dim)]
        + [rows(PATCHES, 2 * dim), pl.BlockSpec((2 * dim, PATCHES), lambda i: (0, i))] * 2,
        out_shape=[jax.ShapeDtypeStruct((count, dim), jnp.float32)]
        + [
            jax.ShapeDtypeStruct((count, 2 * dim), jnp.bfloat16),
            jax.ShapeDtypeStruct((2 * dim, count), jnp.bfloat16),
        ]
        * 2,
        compiler_params=params(48),
        cost_estimate=cost(6 * count * dim * dim, 4 * (dim * dim + 5 * count * dim)),
    )(live, tokens, cotangent, *mixed, *weights, bias, gain, shift)


BLOCK = 256
PIECE = BLOCK // 16


def feed_kernel(
    split, core_ref, pair_ref, flip_ref, grad_pair_ref, grad_flip_ref, hidden_ref, bias_ref, return_ref, *refs
):
    result_ref, second_ref, d_bias_ref = refs[:3]
    outs = refs[3:-7]
    up_ref, down_ref, hidden3_ref, return3_ref, active3_ref, slope3_ref, block_ref = refs[-7:]
    count = pair_ref.shape[0]
    dim = pair_ref.shape[1] // 2
    chunk = min(512, count)

    @pl.when(pl.program_id(0) == 0)
    def _():
        result_ref[...] = jnp.zeros_like(result_ref)
        second_ref[...] = jnp.zeros_like(second_ref)

    d_bias_ref[...] = jnp.zeros_like(d_bias_ref)

    def triple_columns(ref, value, size):
        high, low = halves(value)
        ref[:, :size] = high
        ref[:, size : 2 * size] = high
        ref[:, 2 * size :] = low

    def triple_rows(ref, part, value):
        high, low = halves(value)
        ref[:BLOCK, part] = high
        ref[BLOCK : 2 * BLOCK, part] = low
        ref[2 * BLOCK :, part] = high

    triple_columns(down_ref, return_ref[...], dim)
    triple_columns(up_ref, hidden_ref[...].T, dim)
    triple_columns(hidden3_ref, hidden_ref[...], BLOCK)
    triple_columns(return3_ref, return_ref[...].T, BLOCK)

    def tokens_step(step, carry):
        part = pl.ds(pl.multiple_of(step * chunk, chunk), chunk)
        d_active = mul(down_ref[:, : 2 * dim], grad_flip_ref[:, part], 1, 0) + mul(
            down_ref[:, 2 * dim :], grad_flip_ref[:dim, part], 1, 0
        )
        hidden = (
            mul(up_ref[:, : 2 * dim], flip_ref[:, part], 1, 0)
            + mul(up_ref[:, 2 * dim :], flip_ref[:dim, part], 1, 0)
            + bias_ref[...]
        )
        cumul = 0.5 * (1.0 + lax.erf(hidden * 2.0 ** (-0.5)))
        triple_rows(active3_ref, part, hidden * cumul)
        density = hidden * jnp.exp(-0.5 * hidden * hidden) * (1.0 / math.sqrt(2.0 * math.pi))
        d_hidden = d_active * (cumul + density)
        triple_rows(slope3_ref, part, d_hidden)
        d_bias_ref[...] += jnp.sum(d_hidden, 1, keepdims=True)
        result_ref[:, part] += mul(return3_ref[...], active3_ref[:, part], 1, 0)
        second_ref[:, part] += mul(hidden3_ref[...], slope3_ref[:, part], 1, 0)
        return carry

    lax.fori_loop(0, count // chunk, tokens_step, 0)

    def weight_grad(left_ref, right_ref):
        wide = mul(left_ref[:BLOCK], right_ref[...], 1, 0)
        return wide[:, :dim] + wide[:, dim:] + mul(left_ref[BLOCK : 2 * BLOCK], right_ref[:, :dim], 1, 0)

    if split:
        hidden_keep, hidden_send, return_keep, return_send = outs
        block_ref[...] = weight_grad(active3_ref, grad_pair_ref)

        def place_return(even_ref, odd_ref):
            for pair in range(8):
                even_ref[0, pair] = block_ref[2 * pair * PIECE : (2 * pair + 1) * PIECE]
                odd_ref[0, pair] = block_ref[(2 * pair + 1) * PIECE : (2 * pair + 2) * PIECE]

        pl.when(core_ref[0] == 0)(lambda: place_return(return_keep, return_send))
        pl.when(core_ref[0] == 1)(lambda: place_return(return_send, return_keep))
        value = weight_grad(slope3_ref, pair_ref).T
        piece = dim // 16

        def place_hidden(even_ref, odd_ref):
            for pair in range(8):
                even_ref[pair] = value[2 * pair * piece : (2 * pair + 1) * piece]
                odd_ref[pair] = value[(2 * pair + 1) * piece : (2 * pair + 2) * piece]

        pl.when(core_ref[0] == 0)(lambda: place_hidden(hidden_keep, hidden_send))
        pl.when(core_ref[0] == 1)(lambda: place_hidden(hidden_send, hidden_keep))
    else:
        outs[1][...] = weight_grad(active3_ref, grad_pair_ref)
        outs[0][...] = weight_grad(slope3_ref, pair_ref).T


def feed(split, core, tokens_forms, hidden_weight, hidden_bias, return_weight, first, blocks):
    pair, flip = tokens_forms[:2]
    count = pair.shape[0]
    dim = pair.shape[1] // 2
    units = blocks * BLOCK
    whole = jax.ShapeDtypeStruct((dim, count), jnp.float32)
    if split:
        hidden_out = jax.ShapeDtypeStruct((8, dim // 16, units), jnp.float32)
        return_out = jax.ShapeDtypeStruct((blocks, 8, PIECE, dim), jnp.float32)
        out_specs = [pl.BlockSpec((8, dim // 16, BLOCK), lambda i: (0, 0, i))] * 2 + [
            pl.BlockSpec((1, 8, PIECE, dim), lambda i: (i, 0, 0, 0))
        ] * 2
        out_shape = [hidden_out] * 2 + [return_out] * 2
    else:
        out_specs = [pl.BlockSpec((dim, BLOCK), lambda i: (0, i)), rows(BLOCK, dim)]
        out_shape = [
            jax.ShapeDtypeStruct((dim, units), jnp.float32),
            jax.ShapeDtypeStruct((units, dim), jnp.float32),
        ]
    wide = pltpu.VMEM((BLOCK, 3 * dim), jnp.bfloat16)
    tall = pltpu.VMEM((dim, 3 * BLOCK), jnp.bfloat16)
    return pl.pallas_call(
        functools.partial(feed_kernel, split),
        grid=(blocks,),
        in_specs=[scalars()]
        + [fixed(form.shape) for form in tokens_forms]
        + [
            pl.BlockSpec((dim, BLOCK), lambda i: (0, first + i)),
            pl.BlockSpec((BLOCK, 1), lambda i: (first + i, 0)),
            pl.BlockSpec((BLOCK, dim), lambda i: (first + i, 0)),
        ],
        out_specs=[fixed((dim, count)), fixed((dim, count)), rows(BLOCK, 1)] + out_specs,
        out_shape=[whole, whole, jax.ShapeDtypeStruct((units, 1), jnp.float32)] + out_shape,
        scratch_shapes=[
            wide,
            wide,
            tall,
            tall,
            pltpu.VMEM((3 * BLOCK, count), jnp.bfloat16),
            pltpu.VMEM((3 * BLOCK, count), jnp.bfloat16),
            pltpu.VMEM((BLOCK, dim), jnp.float32),
        ],
        compiler_params=params(62),
        cost_estimate=cost(36 * count * dim * units, 4 * (4 * dim * units + 5 * count * dim), 2 * count * units),
    )(core, *tokens_forms, hidden_weight, hidden_bias, return_weight)


def middle_kernel(parts, feeds, *refs):
    live_ref, middle_ref, cotangent_ref, gain_ref, bias_ref = refs[:5]
    result_parts = refs[5 : 5 + feeds]
    second_parts = refs[5 + feeds : 5 + 2 * feeds]
    weight_refs = refs[5 + 2 * feeds : 5 + 2 * feeds + parts]
    result_ref, d_middle_ref, sums_ref = refs[5 + 2 * feeds + parts : 8 + 2 * feeds + parts]
    mix_refs = refs[8 + 2 * feeds + parts :]
    middle = middle_ref[...]
    grad = cotangent_ref[...] * live_ref[pl.program_id(0)]
    result = result_parts[0][...]
    second = second_parts[0][...]
    for part in result_parts[1:]:
        result = result + part[...]
    for part in second_parts[1:]:
        second = second + part[...]
    result_ref[...] = middle + bias_ref[...] + result.T
    second = second.T
    scaled, inverse = standardize(middle)
    d_middle = grad + norm_back(second * gain_ref[...], scaled, inverse)
    d_middle_ref[...] = d_middle

    @pl.when(pl.program_id(0) == 0)
    def _():
        sums_ref[...] = jnp.zeros_like(sums_ref)

    sums_ref[0:1, :] += jnp.sum(second * scaled, 0, keepdims=True)
    sums_ref[1:2, :] += jnp.sum(second, 0, keepdims=True)
    sums_ref[2:3, :] += jnp.sum(d_middle, 0, keepdims=True)
    sums_ref[3:4, :] += jnp.sum(grad, 0, keepdims=True)
    for weight_ref, mix_ref in zip(weight_refs, mix_refs):
        mix_ref[...] = dot_nt(d_middle, weight_ref[...])


def middle_backward(live, middle, cotangent, gain, bias, results, seconds, weights):
    count, dim = middle.shape
    parts = len(weights)
    block = jax.ShapeDtypeStruct((count, dim), jnp.float32)
    return pl.pallas_call(
        functools.partial(middle_kernel, parts, len(results)),
        grid=(count // PATCHES,),
        in_specs=[scalars()]
        + [rows(PATCHES, dim)] * 2
        + [fixed((1, dim))] * 2
        + [pl.BlockSpec((dim, PATCHES), lambda i: (0, i))] * (2 * len(results))
        + [fixed(w.shape) for w in weights],
        out_specs=[rows(PATCHES, dim)] * 2 + [fixed((8, dim))] + [rows(PATCHES, w.shape[0]) for w in weights],
        out_shape=[block, block, jax.ShapeDtypeStruct((8, dim), jnp.float32)]
        + [jax.ShapeDtypeStruct((count, w.shape[0]), jnp.float32) for w in weights],
        compiler_params=params(60),
        cost_estimate=cost(6 * count * dim * dim, 4 * (dim * dim + 9 * count * dim)),
    )(live, middle, cotangent, gain, bias, *results, *seconds, *weights)


def attend_backward_kernel(
    heads, query_ref, keys_ref, values_ref, mixed_ref, grad_ref, lse_ref, strip_ref,
    d_proj_ref, flipped_ref, d_strip_ref, d_time_ref, bias_ref, total_ref, d_query_ref, d_keys_ref, d_values_ref,
):
    width = query_ref.shape[1]
    image = pl.program_id(0)

    @pl.when(image == 0)
    def _():
        build_bias(strip_ref, bias_ref, heads)
        total_ref[...] = jnp.zeros_like(total_ref)

    d_query_ref[...] = jnp.zeros_like(d_query_ref)
    d_keys_ref[...] = jnp.zeros_like(d_keys_ref)
    d_values_ref[...] = jnp.zeros_like(d_values_ref)
    for head in range(heads):
        start, stop, _ = head_window(head, width)
        mask = head_mask(head, width)
        query = jnp.where(mask, query_ref[:, start:stop], 0.0)
        keys = jnp.where(mask, keys_ref[:, start:stop], 0.0)
        grad = jnp.where(mask, grad_ref[:, start:stop], 0.0)
        scores = dot_nt(query, keys) + bias_ref[head]
        prob = jnp.exp(scores - lse_ref[:, head : head + 1])
        d_prob = dot_nt(grad, values_ref[:, start:stop])
        delta = jnp.sum(grad * mixed_ref[:, start:stop], -1, keepdims=True)
        d_scores = prob * (d_prob - delta)
        total_ref[head] += d_scores
        d_values_ref[:, start:stop] += dot_tn(prob, grad)
        d_query_ref[:, start:stop] += dot_nn(d_scores, keys)
        d_keys_ref[:, start:stop] += dot_tn(d_scores, query)
    d_proj_ref[:, :width] = d_query_ref[...] * SCALE
    d_proj_ref[:, width : 2 * width] = d_keys_ref[...]
    d_proj_ref[:, 2 * width :] = d_values_ref[...]
    d_time_ref[0] = jnp.sum(d_proj_ref[...], 0, keepdims=True)
    flipped_ref[:width] = (d_query_ref[...] * SCALE).T
    flipped_ref[width : 2 * width] = d_keys_ref[...].T
    flipped_ref[2 * width :] = d_values_ref[...].T

    @pl.when(image == pl.num_programs(0) - 1)
    def _():
        d_strip_ref[...] = jnp.zeros_like(d_strip_ref)

        def one(head, carry):
            for row in range(SIDE):
                shift = (SIDE - 1 - row) * SIDE
                d_strip_ref[head, :, shift : shift + PATCHES] += total_ref[head, row * SIDE : (row + 1) * SIDE, :]
            return carry

        lax.fori_loop(0, heads, one, 0)


def attend_backward(query, keys, values, mixed, grad, lse, strips):
    count, width = query.shape
    heads = strips.shape[0]
    images = count // PATCHES
    return pl.pallas_call(
        functools.partial(attend_backward_kernel, heads),
        grid=(images,),
        in_specs=[rows(PATCHES, width)] * 5 + [rows(PATCHES, heads), fixed(strips.shape)],
        out_specs=[
            rows(PATCHES, 3 * width),
            pl.BlockSpec((3 * width, PATCHES), lambda i: (0, i)),
            fixed(strips.shape),
            pl.BlockSpec((1, 1, 3 * width), lambda i: (i, 0, 0)),
        ],
        out_shape=[
            jax.ShapeDtypeStruct((count, 3 * width), jnp.float32),
            jax.ShapeDtypeStruct((3 * width, count), jnp.float32),
            jax.ShapeDtypeStruct(strips.shape, jnp.float32),
            jax.ShapeDtypeStruct((images, 1, 3 * width), jnp.float32),
        ],
        scratch_shapes=[pltpu.VMEM((heads, PATCHES, PATCHES), jnp.float32)] * 2
        + [pltpu.VMEM((PATCHES, width), jnp.float32)] * 3,
        compiler_params=params(56),
        cost_estimate=cost(30 * count * PATCHES * 256 * heads, 4 * 9 * count * width),
    )(query, keys, values, mixed, grad, lse, strips)


STEP = 576


def attend_weights_kernel(split, steps, core_ref, *refs):
    lefts, rights = refs[: len(steps)], refs[len(steps) : 2 * len(steps)]
    outs = refs[2 * len(steps) :]
    step = pl.program_id(0)
    piece = STEP // 8
    begin = 0
    for left_ref, right_ref, count in zip(lefts, rights, steps):

        @pl.when((step >= begin) & (step < begin + count))
        def _(left_ref=left_ref, right_ref=right_ref):
            value = dot_nn(left_ref[...], right_ref[...])
            if split:

                def store(even_ref, odd_ref):
                    for pair in range(4):
                        even_ref[pair] = value[2 * pair * piece : (2 * pair + 1) * piece]
                        odd_ref[pair] = value[(2 * pair + 1) * piece : (2 * pair + 2) * piece]

                pl.when(core_ref[0] == 0)(lambda: store(outs[0], outs[1]))
                pl.when(core_ref[0] == 1)(lambda: store(outs[1], outs[0]))
            else:
                outs[0][...] = value

        begin += count


def attend_weights(split, core, lefts, rights, firsts, steps):
    count, dim = rights[0].shape
    total = sum(steps)
    starts = [sum(steps[:i]) for i in range(len(steps))]

    def left_spec(start, first, size):
        return pl.BlockSpec((STEP, count), lambda i: (first + jnp.clip(i - start, 0, size - 1), 0))

    if split:
        out_specs = [pl.BlockSpec((4, STEP // 8, dim), lambda i: (i, 0, 0))] * 2
        out_shape = [jax.ShapeDtypeStruct((4 * total, STEP // 8, dim), jnp.float32)] * 2
    else:
        out_specs = [rows(STEP, dim)]
        out_shape = [jax.ShapeDtypeStruct((STEP * total, dim), jnp.float32)]
    return pl.pallas_call(
        functools.partial(attend_weights_kernel, split, steps),
        grid=(total,),
        in_specs=[scalars()]
        + [left_spec(a, b, c) for a, b, c in zip(starts, firsts, steps)]
        + [fixed((count, dim)) for _ in rights],
        out_specs=out_specs,
        out_shape=out_shape,
        compiler_params=params(60),
        cost_estimate=cost(6 * count * dim * STEP * total, 4 * (dim * STEP * total + count * 3 * dim)),
    )(core, *lefts, *rights)


def first_kernel(parts, *refs):
    tokens_ref, d_middle_ref, gain_ref = refs[:3]
    d_proj_refs = refs[3 : 3 + parts]
    weight_refs = refs[3 + parts : 3 + 2 * parts]
    out_ref, sums_ref = refs[3 + 2 * parts :]
    first = dot_nn(d_proj_refs[0][...], weight_refs[0][...])
    for d_proj_ref, weight_ref in zip(d_proj_refs[1:], weight_refs[1:]):
        first = first + dot_nn(d_proj_ref[...], weight_ref[...])
    scaled, inverse = standardize(tokens_ref[...])
    out_ref[...] = d_middle_ref[...] + norm_back(first * gain_ref[...], scaled, inverse)

    @pl.when(pl.program_id(0) == 0)
    def _():
        sums_ref[...] = jnp.zeros_like(sums_ref)

    sums_ref[0:1, :] += jnp.sum(first * scaled, 0, keepdims=True)
    sums_ref[1:2, :] += jnp.sum(first, 0, keepdims=True)


def first_backward(tokens, d_middle, gain, d_projs, weights, begin, images):
    dim = tokens.shape[1]
    count = images * PATCHES

    def some(width):
        return pl.BlockSpec((PATCHES, width), lambda i: (begin + i, 0))

    parts = len(d_projs)
    return pl.pallas_call(
        functools.partial(first_kernel, parts),
        grid=(count // PATCHES,),
        in_specs=[some(dim)] * 2
        + [fixed((1, dim))]
        + [some(d.shape[1]) for d in d_projs]
        + [fixed(w.shape) for w in weights],
        out_specs=[rows(PATCHES, dim), fixed((8, dim))],
        out_shape=[jax.ShapeDtypeStruct((count, dim), jnp.float32), jax.ShapeDtypeStruct((8, dim), jnp.float32)],
        compiler_params=params(60),
        cost_estimate=cost(18 * count * dim * dim, 4 * (3 * dim * dim + 6 * count * dim)),
    )(tokens, d_middle, gain, *d_projs, *weights)


def offset_matrix():
    place = jnp.arange(PATCHES)
    offset = place // SIDE - place % SIDE + SIDE - 1
    return (jnp.arange(STRIP)[:, None] == offset[None, :]).astype(jnp.float32)


def make_strips(table):
    heads = table.shape[0]
    grid = table.reshape(heads, STRIP, STRIP)[:, ::-1]
    wide = jnp.einsum("hmo,op->hmp", grid, offset_matrix(), precision=HIGHEST)
    wide = wide.reshape(heads, STRIP, SIDE, SIDE).transpose(0, 2, 1, 3).reshape(heads, SIDE, STRIP * SIDE)
    return jnp.pad(wide, ((0, 0), (0, 0), (0, 512 - STRIP * SIDE)))


def table_gradient(d_strips):
    heads = d_strips.shape[0]
    wide = d_strips[:, :, : STRIP * SIDE].reshape(heads, SIDE, STRIP, SIDE).transpose(0, 2, 1, 3)
    grid = jnp.einsum("hmp,op->hmo", wide.reshape(heads, STRIP, PATCHES), offset_matrix(), precision=HIGHEST)
    return grid[:, ::-1].reshape(heads, STRIP * STRIP)


def pick(array, index, axis):
    return lax.dynamic_index_in_dim(array, index, axis, keepdims=False)


def join(*values):
    return lax.optimization_barrier(values)


class Ring:
    def __init__(self):
        place = lax.axis_index("dp")
        self.place = place
        self.bits = [place & 1, (place >> 1) & 1, (place >> 2) & 1, (place >> 3) & 1]

    def across(self, value):
        return lax.ppermute(value, "mp", [(0, 1), (1, 0)])

    def along(self, value, bit):
        return lax.ppermute(value, "dp", [(i, i ^ (1 << bit)) for i in range(16)])

    def ordered(self, mine, theirs, bit, axis=0):
        flag = self.bits[bit] == 0
        return jnp.concatenate([jnp.where(flag, mine, theirs), jnp.where(flag, theirs, mine)], axis)

    def core_half(self, weight, base, count):
        half = count // 2
        return lax.dynamic_slice(weight, (base + self.bits[0] * half, 0), (half, weight.shape[1]))

    def share(self, weight, count, first, width):
        part = count // 16
        return lax.dynamic_slice(weight, (self.place * part, first), (part, width))

    def spread(self, part):
        return lax.all_gather(part, "dp", axis=0, tiled=True)

    def all_sum(self, value):
        value = value + self.along(value, 0)
        value = value + self.across(value)
        for bit in (1, 2, 3):
            value = value + self.along(value, bit)
        return value

    def all_rows(self, value):
        for bit in range(4):
            value = self.ordered(value, self.along(value, bit), bit)
        return value


class Reduction:
    def __init__(self, ring, axis):
        self.ring = ring
        self.axis = axis
        self.terms = {}
        self.level = {}

    def begin(self, side, keep, send):
        self.terms[side] = [keep, self.ring.along(send, 0)]
        self.level[side] = 1

    def value(self, side):
        out = self.terms[side][0]
        for term in self.terms[side][1:]:
            out = out + term
        return out

    def send(self, side):
        bit = self.ring.bits[self.level[side]]
        kept = []
        out = 0.0
        for term in self.terms[side]:
            shape = term.shape
            axis = self.axis
            cut = term.reshape(shape[:axis] + (shape[axis] // 2, 2) + shape[axis + 1 :])
            kept.append(pick(cut, bit, axis + 1))
            out = out + pick(cut, 1 - bit, axis + 1)
        self.terms[side] = kept
        return out

    def pass_on(self, side, value):
        self.terms[side].append(self.ring.along(value, self.level[side]))
        self.level[side] += 1

    def cross(self, value):
        self.terms["own"].append(self.ring.across(value))

    def gather(self, value):
        return lax.all_gather(value, "dp", axis=self.axis, tiled=True)

    def back(self, value, bit):
        axis = self.axis
        got = self.ring.along(value, bit)
        value, got = (v.reshape(v.shape[: axis + 1] + (1,) + v.shape[axis + 1 :]) for v in (value, got))
        out = self.ring.ordered(value, got, bit, axis + 1)
        return out.reshape(out.shape[:axis] + (-1,) + out.shape[axis + 2 :])


def body(split, *args):
    (
        tokens, cotangent, bucket, counts, first_gain, first_shift, attend_weight, time_weight, time_table,
        bias_table, output_weight, output_bias, second_gain, second_shift, hidden_weight, hidden_bias,
        return_weight, return_bias,
    ) = args
    own_images, patches, dim = tokens.shape
    images = bucket.shape[0]
    buckets = time_table.shape[0]
    heads_local = bias_table.shape[0]
    width = attend_weight.shape[2]
    units = hidden_bias.shape[0]
    group = lax.axis_index("dp")
    rank = lax.axis_index("mp")
    first_own = rank * own_images
    live = (first_own + jnp.arange(own_images) < counts[group]).astype(jnp.float32)
    inv_total = 1.0 / jnp.sum(counts).astype(jnp.float32)
    core = (group & 1).reshape(1)

    def row(vector):
        return vector.reshape(1, -1)

    def column(vector):
        return vector.reshape(-1, 1)

    tokens2 = tokens.reshape(own_images * patches, dim)
    cotangent2 = cotangent.reshape(own_images * patches, dim)
    onehot = (bucket[:, None] == jnp.arange(buckets)[None, :]).astype(jnp.float32)
    time_vec = jnp.dot(onehot, time_table, precision=HIGHEST)
    time_proj = jnp.einsum("sd,ced->sce", time_vec, time_weight.transpose(0, 2, 1), precision=HIGH)
    attend_own = attend_weight.transpose(0, 2, 1).reshape(3 * width, dim)
    norm_first = (row(first_gain), row(first_shift))
    norm_second = (row(second_gain), row(second_shift))

    def times_of(value):
        return value.reshape(own_images, 1, -1)

    if split:
        ring = Ring()
        more = (units // BLOCK + 1) // 2
        cuts = [(0, more), (more, units // BLOCK - more)]
        qk = ring.across(ring.share(attend_own, 2 * width, 0, dim))
        qk_full = ring.spread(qk)
        values_half = ring.core_half(attend_own, 2 * width, width)
        values_half, qk = join(values_half, qk)
        values_mine = ring.across(values_half)
        time_mine = lax.dynamic_slice_in_dim(time_proj, first_own, own_images, 0)
        time_theirs = lax.dynamic_slice_in_dim(time_proj, (1 - rank) * own_images, own_images, 0)
        strips_own = make_strips(bias_table)
        tokens_a, qk, time_theirs = join(tokens2, qk, time_theirs)
        own = attend_forward(tokens_a, *norm_first, attend_own, times_of(time_mine), strips_own)
        own, values_mine, time_theirs, bias_table_b = join(own, values_mine, time_theirs, bias_table)
        time_other = ring.across(time_theirs)
        table_other = ring.across(bias_table_b)
        bias_other = column(ring.across(hidden_bias))
        output_mine = ring.across(ring.core_half(output_weight, 0, width))
        values_theirs = ring.along(values_mine, 0)
        hidden_other = []
        for first, blocks in cuts:
            part = ring.share(hidden_weight, dim, first * BLOCK, blocks * BLOCK)
            part, values_mine = join(part, values_mine)
            hidden_other.append(ring.spread(ring.across(part)))
        attend_other = jnp.concatenate([qk_full, ring.ordered(values_mine, values_theirs, 0)], 0)
        attend_other, output_mine = join(attend_other, output_mine)
        first_half = ring.core_half(return_weight, 0, cuts[0][1] * BLOCK)
        first_half, output_mine = join(first_half, output_mine)
        return_mine = ring.across(first_half)
        output_other = ring.ordered(output_mine, ring.along(output_mine, 0), 0)
        other = attend_forward(
            tokens2, *norm_first, attend_other, times_of(time_other), make_strips(table_other)
        )
        strips_other = make_strips(table_other)
        attend = [attend_own, attend_other]
        output = [output_weight, output_other]
        middle, *forms = output_forward(
            live, tokens2, cotangent2, [own[3], other[3]], output, row(output_bias), *norm_second
        )
        second_half = ring.core_half(return_weight, cuts[1][0] * BLOCK, cuts[1][1] * BLOCK)
        return_1, second_half = join(ring.ordered(return_mine, ring.along(return_mine, 0), 0), second_half)
        return_mine = ring.across(second_half)

        def feed_other(forms, index, hidden, back):
            first, blocks = cuts[index]
            bias = bias_other[first * BLOCK : (first + blocks) * BLOCK]
            return feed(True, core, forms, hidden, bias, back, 0, blocks)

        def feed_own(forms, index):
            return feed(True, core, forms, hidden_weight, column(hidden_bias), return_weight, *cuts[index])

        h1, h2, r1, r2, qa, qb = (Reduction(ring, axis) for axis in (0, 0, 1, 1, 0, 0))
        other_1 = feed_other(forms, 0, hidden_other[0], return_1)
        forms, other_1, return_mine = join(forms, other_1, return_mine)
        h1.begin("other", *other_1[3:5])
        r1.begin("other", *other_1[5:7])
        return_2 = ring.ordered(return_mine, ring.along(return_mine, 0), 0)
        other_2 = feed_other(forms, 1, hidden_other[1], return_2)
        forms, other_2, a, b = join(forms, other_2, h1.value("other"), r1.send("other"))
        h1_cross, r1_y = a, b
        h2.begin("other", *other_2[3:5])
        r2.begin("other", *other_2[5:7])
        h1_crossed = ring.across(h1_cross)
        r1.pass_on("other", r1_y)
        own_1 = feed_own(forms, 0)
        forms, own_1, a, b, h1_crossed, r1.terms["other"] = join(
            forms, own_1, h2.value("other"), r2.send("other"), h1_crossed, r1.terms["other"]
        )
        h1.begin("own", *own_1[3:5])
        r1.begin("own", *own_1[5:7])
        h1.terms["own"].append(h1_crossed)
        h2_crossed = ring.across(a)
        r2.pass_on("other", b)
        own_2 = feed_own(forms, 1)
        middle, own_2, a, b, h2_crossed = join(middle, own_2, r1.send("own"), r1.value("other"), h2_crossed)
        h2.begin("own", *own_2[3:5])
        r2.begin("own", *own_2[5:7])
        h2.terms["own"].append(h2_crossed)
        r1.pass_on("own", a)
        r1.cross(b)
        fed = [other_1, own_1, other_2, own_2]
        result, d_middle, second_sums, d_mixed_own, d_mixed_other = middle_backward(
            live, middle, cotangent2, row(second_gain), row(return_bias), [f[0] for f in fed], [f[1] for f in fed], output
        )
        d_mixed_other, a, b, c = join(d_mixed_other, h1.send("own"), r2.value("other"), r1.send("own"))
        h1.pass_on("own", a)
        r2_crossed = ring.across(b)
        r1.pass_on("own", c)
        attended_other = attend_backward(*other[:4], d_mixed_other, other[5], strips_other)
        attended_other, a, b, c, r2_crossed = join(
            attended_other, h1.send("own"), r1.send("own"), h2.send("own"), r2_crossed
        )
        h1.pass_on("own", a)
        r1.pass_on("own", b)
        h2.pass_on("own", c)

        def weights_a(attended, normed):
            return attend_weights(True, core, [attended[1]], [normed], [0], [2])

        def weights_b(attended, normed, flipped_mixed):
            return attend_weights(True, core, [attended[1], flipped_mixed], [normed, d_middle], [2, 0], [1, 1])

        normed_first = own[6]
        part = weights_a(attended_other, normed_first)
        part, normed_first = join(part, normed_first)
        qa.begin("other", *part)
        part = weights_b(attended_other, normed_first, other[4])
        part, d_mixed_own, a, b, c, d, e = join(
            part, d_mixed_own, qa.value("other"), h1.send("own"), r2.send("own"), h2.send("own"), r1.value("own")
        )
        qb.begin("other", *part)
        qa_first = ring.across(a[:4])
        h1.pass_on("own", b)
        r2.pass_on("own", c)
        r2.terms["own"].append(r2_crossed)
        h2.pass_on("own", d)
        return_1 = r1.gather(e)
        attended_own = attend_backward(*own[:4], d_mixed_own, own[5], strips_own)
        attended_own, a, b, c, d, e, qa_first = join(
            attended_own, qb.send("other"), h1.value("own"), r2.send("own"), h2.send("own"), a[4:], qa_first
        )
        qb.pass_on("other", a)
        hidden_1 = h1.gather(b)
        r2.pass_on("own", c)
        h2.pass_on("own", d)
        qa_second = ring.across(e)
        part = weights_b(attended_own, normed_first, own[4])
        part, normed_first = join(part, normed_first)
        qb.begin("own", *part)
        part = weights_a(attended_own, normed_first)
        part, d_projs, a, b, c, d, qa_second = join(
            part, [attended_own[0], attended_other[0]], qb.send("own"), qb.value("other"), r2.send("own"),
            h2.value("own"), qa_second,
        )
        qa.begin("own", *part)
        qa.terms["own"].append(jnp.concatenate([qa_first, qa_second], 0))
        qb.pass_on("own", a)
        qb.cross(b)
        r2.pass_on("own", c)
        hidden_2 = h2.back(d, 3)
        half = own_images // 2
        tokens_a, sums_a = first_backward(tokens2, d_middle, row(first_gain), d_projs, attend, 0, half)
        tokens_a, d_projs, a, b, c, hidden_2 = join(
            tokens_a, d_projs, qa.send("own"), qb.send("own"), r2.value("own"), hidden_2
        )
        qa.pass_on("own", a)
        qb.pass_on("own", b)
        return_2 = r2.back(c, 3)
        hidden_2 = h2.back(hidden_2, 2)
        tokens_b, sums_b = first_backward(
            tokens2, d_middle, row(first_gain), d_projs, attend, half, own_images - half
        )
        tokens_b, a, b, hidden_2, return_2 = join(tokens_b, qa.send("own"), qb.send("own"), hidden_2, return_2)
        qa.pass_on("own", a)
        qb.pass_on("own", b)
        hidden_2 = h2.back(hidden_2, 1)
        return_2 = r2.back(return_2, 2)
        a, b, hidden_2, return_2 = join(qa.send("own"), qb.value("own"), hidden_2, return_2)
        qa.pass_on("own", a)
        attend_b = qb.gather(b)
        hidden_2 = h2.back(hidden_2, 0)
        return_2 = r2.back(return_2, 1)
        a, hidden_2, return_2 = join(qa.value("own"), hidden_2, return_2)
        attend_a = qa.back(a, 3)
        return_2 = r2.back(return_2, 0)
        hidden_grad = jnp.concatenate([g.reshape(dim, -1) for g in (hidden_1, hidden_2)], 1) * inv_total
        attend_a, hidden_grad, return_2 = join(attend_a, hidden_grad, return_2)
        attend_a = qa.back(attend_a, 2)
        return_grad = jnp.concatenate([g.reshape(-1, dim) for g in (return_1, return_2)], 0) * inv_total
        attend_a, return_grad = join(attend_a, return_grad)
        attend_a = qa.back(qa.back(attend_a, 1), 0)
        tokens_grad = jnp.concatenate([tokens_a, tokens_b], 0)
        first_sums = sums_a + sums_b
        attend_a = attend_a.reshape(2, width, dim)
        attend_b = attend_b.reshape(2, width, dim)
        attend_weight_grad = (jnp.concatenate([attend_a, attend_b[:1]], 0) * inv_total).transpose(0, 2, 1)
        output_weight_grad = attend_b[1] * inv_total

        def absolute(own, other):
            flag = rank == 0
            return jnp.concatenate([jnp.where(flag, own, other), jnp.where(flag, other, own)], 0)

        table_full = absolute(table_gradient(attended_own[2]), table_gradient(attended_other[2]))
        bias_own = jnp.concatenate([own_1[2][:, 0], own_2[2][:, 0]])
        hidden_bias_full = absolute(bias_own, jnp.concatenate([other_1[2][:, 0], other_2[2][:, 0]]))
        d_time_got = ring.across(attended_other[3].reshape(own_images, 3, width))
        d_time = absolute(attended_own[3].reshape(own_images, 3, width), d_time_got)
        gather_rows = ring.all_rows
        all_sum = ring.all_sum
    else:
        attend = [lax.all_gather(attend_weight, "mp", axis=2, tiled=True).transpose(0, 2, 1).reshape(-1, dim)]
        output = [lax.all_gather(output_weight, "mp", axis=0, tiled=True)]
        hidden_full = lax.all_gather(hidden_weight, "mp", axis=1, tiled=True)
        return_full = lax.all_gather(return_weight, "mp", axis=0, tiled=True)
        bias_full = lax.all_gather(hidden_bias, "mp", axis=0, tiled=True)
        strips = make_strips(lax.all_gather(bias_table, "mp", axis=0, tiled=True))
        full = lax.all_gather(time_proj, "mp", axis=2, tiled=True)
        times = times_of(lax.dynamic_slice_in_dim(full, first_own, own_images, 0))
        all_of = attend_forward(tokens2, *norm_first, attend[0], times, strips)
        middle, *forms = output_forward(
            live, tokens2, cotangent2, [all_of[3]], output, row(output_bias), *norm_second
        )
        fed = feed(False, core, forms, hidden_full, column(bias_full), return_full, 0, hidden_full.shape[1] // BLOCK)
        result, d_middle, second_sums, d_mixed = middle_backward(
            live, middle, cotangent2, row(second_gain), row(return_bias), [fed[0]], [fed[1]], output
        )
        attended = attend_backward(*all_of[:4], d_mixed, all_of[5], strips)
        (attend_full,) = attend_weights(
            False, core, [attended[1]], [all_of[6]], [0], [attended[1].shape[0] // STEP]
        )
        (output_full,) = attend_weights(False, core, [all_of[4]], [d_middle], [0], [dim // STEP])
        tokens_grad, first_sums = first_backward(
            tokens2, d_middle, row(first_gain), [attended[0]], attend, 0, own_images
        )

        def settle(value, axis):
            return lax.psum(lax.psum_scatter(value * inv_total, "mp", scatter_dimension=axis, tiled=True), "dp")

        hidden_grad = settle(fed[3], 1)
        return_grad = settle(fed[4], 0)
        attend_weight_grad = settle(attend_full.reshape(3, -1, dim), 1).transpose(0, 2, 1)
        output_weight_grad = settle(output_full, 0)
        table_full = table_gradient(attended[2])
        hidden_bias_full = fed[2][:, 0]
        d_time = lax.all_gather(attended[3].reshape(own_images, 3, -1), "mp", axis=0, tiled=True)
        d_time = lax.dynamic_slice_in_dim(d_time, rank * width, width, 2)

        def gather_rows(value):
            return lax.all_gather(value, "dp", axis=0, tiled=True)

        def all_sum(value):
            return lax.psum(value, ("dp", "mp"))

    packed = jnp.concatenate([d_time.reshape(images, -1), bucket.astype(jnp.float32)[:, None]], 1)
    packed = gather_rows(packed)
    d_time_all = packed[:, :-1].reshape(-1, 3, width)
    bucket_all = packed[:, -1].astype(jnp.int32)
    onehot_all = (bucket_all[:, None] == jnp.arange(buckets)[None, :]).astype(jnp.float32)
    time_all = jnp.dot(onehot_all, time_table, precision=HIGHEST)
    time_weight_grad = jnp.einsum("sce,sd->ced", d_time_all * inv_total, time_all, precision=HIGH).transpose(0, 2, 1)
    d_time_vec = jnp.einsum("sce,ced->sd", d_time, time_weight.transpose(0, 2, 1), precision=HIGH)
    time_table_part = jnp.dot(onehot.T, d_time_vec, precision=HIGHEST)

    small = [
        first_sums[0], first_sums[1], time_table_part, second_sums[2], second_sums[0], second_sums[1],
        second_sums[3], table_full, hidden_bias_full,
    ]
    flat = jnp.concatenate([s.reshape(-1) for s in small]) * inv_total
    size = flat.shape[0]
    flat = all_sum(jnp.pad(flat, (0, -size % 1024)).reshape(-1, 128)).reshape(-1)[:size]
    sums = []
    start = 0
    for s in small:
        sums.append(flat[start : start + s.size].reshape(s.shape))
        start += s.size
    bias_table_grad = lax.dynamic_slice_in_dim(sums[7], rank * heads_local, heads_local, 0)
    hidden_bias_grad = lax.dynamic_slice_in_dim(sums[8], rank * units, units, 0)
    return (
        result.reshape(tokens.shape),
        tokens_grad.reshape(tokens.shape),
        sums[0],
        sums[1],
        attend_weight_grad,
        time_weight_grad,
        sums[2],
        bias_table_grad,
        output_weight_grad,
        sums[3],
        sums[4],
        sums[5],
        hidden_grad,
        hidden_bias_grad,
        return_grad,
        sums[6],
    )


def solution(mesh):
    in_specs = (
        P(("dp", "mp"), None, None),
        P(("dp", "mp"), None, None),
        P("dp"),
        P(),
        P(),
        P(),
        P(None, None, "mp"),
        P(None, None, "mp"),
        P(),
        P("mp", None),
        P("mp", None),
        P(),
        P(),
        P(),
        P(None, "mp"),
        P("mp"),
        P("mp", None),
        P(),
    )
    out_specs = (
        P(("dp", "mp"), None, None),
        P(("dp", "mp"), None, None),
        P(),
        P(),
        P(None, None, "mp"),
        P(None, None, "mp"),
        P(),
        P("mp", None),
        P("mp", None),
        P(),
        P(),
        P(),
        P(None, "mp"),
        P("mp"),
        P("mp", None),
        P(),
    )
    split = mesh.shape["dp"] == 16 and mesh.shape["mp"] == 2
    return jax.shard_map(
        functools.partial(body, split), mesh=mesh, in_specs=in_specs, out_specs=out_specs, check_vma=False
    )
```

```python
import functools
import math

import jax
import jax.numpy as jnp
from jax import lax
from jax.experimental import pallas as pl
from jax.experimental.pallas import tpu as pltpu
from jax.sharding import PartitionSpec as P

HEAD_DIM = 72
SIDE = 16
PATCHES = SIDE * SIDE
STRIP = 2 * SIDE - 1
EPS = 1e-05
SCALE = HEAD_DIM ** (-0.5)
MIB = 1024 * 1024
HIGHEST = lax.Precision.HIGHEST
HIGH = lax.Precision.HIGH


def dot_nn(a, b):
    return lax.dot_general(a, b, (((1,), (0,)), ((), ())), precision=HIGH, preferred_element_type=jnp.float32)


def dot_nt(a, b):
    return lax.dot_general(a, b, (((1,), (1,)), ((), ())), precision=HIGH, preferred_element_type=jnp.float32)


def dot_tn(a, b):
    return lax.dot_general(a, b, (((0,), (0,)), ((), ())), precision=HIGH, preferred_element_type=jnp.float32)


def standardize(values):
    centre = values - jnp.mean(values, -1, keepdims=True)
    inverse = lax.rsqrt(jnp.mean(centre * centre, -1, keepdims=True) + EPS)
    return centre * inverse, inverse


def norm_back(grad_hat, scaled, inverse):
    return inverse * (
        grad_hat
        - jnp.mean(grad_hat, -1, keepdims=True)
        - scaled * jnp.mean(grad_hat * scaled, -1, keepdims=True)
    )


def head_window(head, width):
    first = head * HEAD_DIM
    start = first // 128 * 128
    stop = min(-(-(first + HEAD_DIM) // 128) * 128, width)
    return start, stop, first - start


def head_mask(head, width):
    start, stop, offset = head_window(head, width)
    lane = lax.broadcasted_iota(jnp.int32, (1, stop - start), 1)
    return (lane >= offset) & (lane < offset + HEAD_DIM)


def fixed(shape, **kw):
    return pl.BlockSpec(shape, lambda i: (0,) * len(shape), pipeline_mode=pl.Buffered(1), **kw)


def rows(count, width):
    return pl.BlockSpec((count, width), lambda i: (i, 0))


def params(limit):
    return pltpu.CompilerParams(dimension_semantics=("arbitrary",), vmem_limit_bytes=limit * MIB)


def cost(flops, nbytes, trans=0):
    return pl.CostEstimate(flops=int(flops) // 1000, bytes_accessed=int(nbytes) // 1000, transcendentals=0)


def halves(value):
    high = value.astype(jnp.bfloat16)
    return high, (value - high.astype(jnp.float32)).astype(jnp.bfloat16)


def mul(a, b, left, right):
    return lax.dot_general(a, b, (((left,), (right,)), ((), ())), preferred_element_type=jnp.float32)


def scalars():
    return pl.BlockSpec(memory_space=pltpu.SMEM)


def build_bias(strip_ref, bias_ref, heads):
    def one(head, carry):
        strip = strip_ref[head]
        for row in range(SIDE):
            shift = (SIDE - 1 - row) * SIDE
            bias_ref[head, row * SIDE : (row + 1) * SIDE, :] = strip[:, shift : shift + PATCHES]
        return carry

    lax.fori_loop(0, heads, one, 0)


def attend_forward_kernel(
    heads, tokens_ref, gain_ref, shift_ref, weight_ref, time_ref, strip_ref,
    query_ref, keys_ref, values_ref, mixed_ref, flipped_ref, lse_ref, normed_ref, bias_ref,
):
    width = query_ref.shape[1]

    @pl.when(pl.program_id(0) == 0)
    def _():
        build_bias(strip_ref, bias_ref, heads)

    scaled, _ = standardize(tokens_ref[...])
    normed = scaled * gain_ref[...] + shift_ref[...]
    normed_ref[...] = normed
    proj = dot_nt(normed, weight_ref[...]) + time_ref[0]
    query_ref[...] = proj[:, :width] * SCALE
    keys_ref[...] = proj[:, width : 2 * width]
    values_ref[...] = proj[:, 2 * width :]
    mixed_ref[...] = jnp.zeros_like(mixed_ref)
    columns = lax.broadcasted_iota(jnp.int32, (1, heads), 1)
    stats = jnp.zeros((PATCHES, heads), jnp.float32)
    for head in range(heads):
        start, stop, _ = head_window(head, width)
        mask = head_mask(head, width)
        query = jnp.where(mask, query_ref[:, start:stop], 0.0)
        scores = dot_nt(query, keys_ref[:, start:stop]) + bias_ref[head]
        peak = jnp.max(scores, -1, keepdims=True)
        weights = jnp.exp(scores - peak)
        total = jnp.sum(weights, -1, keepdims=True)
        values = jnp.where(mask, values_ref[:, start:stop], 0.0)
        mixed_ref[:, start:stop] += dot_nn(weights, values) * (1.0 / total)
        stats = jnp.where(columns == head, peak + jnp.log(total), stats)
    lse_ref[...] = stats
    flipped_ref[...] = mixed_ref[...].T


def attend_forward(tokens, gain, shift, weight, time_proj, strips):
    count, dim = tokens.shape
    heads = strips.shape[0]
    width = weight.shape[0] // 3
    images = count // PATCHES
    piece = jax.ShapeDtypeStruct((count, width), jnp.float32)
    return pl.pallas_call(
        functools.partial(attend_forward_kernel, heads),
        grid=(images,),
        in_specs=[
            rows(PATCHES, dim),
            fixed((1, dim)),
            fixed((1, dim)),
            fixed((3 * width, dim)),
            pl.BlockSpec((1, 1, 3 * width), lambda i: (i, 0, 0)),
            fixed(strips.shape),
        ],
        out_specs=[rows(PATCHES, width)] * 4
        + [pl.BlockSpec((width, PATCHES), lambda i: (0, i)), rows(PATCHES, heads), rows(PATCHES, dim)],
        out_shape=[piece] * 4
        + [
            jax.ShapeDtypeStruct((width, count), jnp.float32),
            jax.ShapeDtypeStruct((count, heads), jnp.float32),
            jax.ShapeDtypeStruct((count, dim), jnp.float32),
        ],
        scratch_shapes=[pltpu.VMEM((heads, PATCHES, PATCHES), jnp.float32)],
        compiler_params=params(56),
        cost_estimate=cost(6 * count * dim * width * 3 + 24 * count * PATCHES * 256 * heads // 2, 4 * (weight.size + 6 * count * width)),
    )(tokens, gain, shift, weight, time_proj, strips)


def output_kernel(parts, *refs):
    live_ref, tokens_ref, cotangent_ref = refs[:3]
    mixed_refs = refs[3 : 3 + parts]
    weight_refs = refs[3 + parts : 3 + 2 * parts]
    bias_ref, gain_ref, shift_ref, middle_ref, pair_ref, grad_ref = refs[3 + 2 * parts :]
    dim = tokens_ref.shape[1]
    middle = tokens_ref[...] + bias_ref[...]
    for mixed_ref, weight_ref in zip(mixed_refs, weight_refs):
        middle = middle + dot_nn(mixed_ref[...], weight_ref[...])
    middle_ref[...] = middle
    scaled, _ = standardize(middle)
    normed = scaled * gain_ref[...] + shift_ref[...]
    pair_ref[:, :dim], pair_ref[:, dim:] = halves(normed)
    grad = cotangent_ref[...] * live_ref[pl.program_id(0)]
    grad_ref[:, :dim], grad_ref[:, dim:] = halves(grad)


def output_forward(live, tokens, cotangent, mixed, weights, bias, gain, shift):
    count, dim = tokens.shape
    parts = len(mixed)
    pair = jax.ShapeDtypeStruct((count, 2 * dim), jnp.bfloat16)
    return pl.pallas_call(
        functools.partial(output_kernel, parts),
        grid=(count // PATCHES,),
        in_specs=[scalars()]
        + [rows(PATCHES, dim)] * 2
        + [rows(PATCHES, m.shape[1]) for m in mixed]
        + [fixed(w.shape) for w in weights]
        + [fixed((1, dim))] * 3,
        out_specs=[
            rows(PATCHES, dim),
            rows(PATCHES, 2 * dim),
            rows(PATCHES, 2 * dim),
        ],
        out_shape=[
            jax.ShapeDtypeStruct((count, dim), jnp.float32),
            pair,
            pair,
        ],
        compiler_params=params(48),
        cost_estimate=cost(6 * count * dim * dim, 4 * (dim * dim + 5 * count * dim)),
    )(live, tokens, cotangent, *mixed, *weights, bias, gain, shift)


BLOCK = 256
PIECE = BLOCK // 16


def feed_kernel(split, core_ref, pair_ref, grad_ref, hidden_ref, bias_ref, return_ref, *refs):
    result_ref, second_ref, d_bias_ref = refs[:3]
    outs = refs[3:-5]
    hidden3_ref, return3_ref, active3_ref, slope3_ref, block_ref = refs[-5:]
    count = pair_ref.shape[0]
    dim = pair_ref.shape[1] // 2
    chunk = min(512, count)

    @pl.when(pl.program_id(0) == 0)
    def _():
        result_ref[...] = jnp.zeros_like(result_ref)
        second_ref[...] = jnp.zeros_like(second_ref)

    d_bias_ref[...] = jnp.zeros_like(d_bias_ref)
    high, low = halves(hidden_ref[...])
    hidden3_ref[:, :BLOCK] = high
    hidden3_ref[:, BLOCK : 2 * BLOCK] = high
    hidden3_ref[:, 2 * BLOCK :] = low
    high, low = halves(return_ref[...])
    return3_ref[:BLOCK] = high
    return3_ref[BLOCK : 2 * BLOCK] = high
    return3_ref[2 * BLOCK :] = low

    for begin in range(0, count, chunk):
        part = slice(begin, begin + chunk)
        hidden = (
            mul(pair_ref[part, :dim], hidden3_ref[:, :BLOCK], 1, 0)
            + mul(pair_ref[part, dim:], hidden3_ref[:, :BLOCK], 1, 0)
            + mul(pair_ref[part, :dim], hidden3_ref[:, 2 * BLOCK :], 1, 0)
            + bias_ref[...]
        )
        d_active = (
            mul(grad_ref[part, :dim], return3_ref[:BLOCK], 1, 1)
            + mul(grad_ref[part, dim:], return3_ref[:BLOCK], 1, 1)
            + mul(grad_ref[part, :dim], return3_ref[2 * BLOCK :], 1, 1)
        )
        cumul = 0.5 * (1.0 + lax.erf(hidden * 2.0 ** (-0.5)))
        high, low = halves(hidden * cumul)
        active3_ref[part, :BLOCK] = high
        active3_ref[part, BLOCK : 2 * BLOCK] = low
        active3_ref[part, 2 * BLOCK :] = high
        density = hidden * jnp.exp(-0.5 * hidden * hidden) * (1.0 / math.sqrt(2.0 * math.pi))
        d_hidden = d_active * (cumul + density)
        high, low = halves(d_hidden)
        slope3_ref[part, :BLOCK] = high
        slope3_ref[part, BLOCK : 2 * BLOCK] = low
        slope3_ref[part, 2 * BLOCK :] = high
        d_bias_ref[...] += jnp.sum(d_hidden, 0, keepdims=True)
        result_ref[part, :] += mul(active3_ref[part, :], return3_ref[...], 1, 0)
        second_ref[part, :] += mul(slope3_ref[part, :], hidden3_ref[...], 1, 1)

    def weight_grad(left_ref, right_ref):
        wide = mul(left_ref[:, :BLOCK], right_ref[...], 0, 0)
        return wide[:, :dim] + wide[:, dim:] + mul(left_ref[:, BLOCK : 2 * BLOCK], right_ref[:, :dim], 0, 0)

    if split:
        block_ref[0] = weight_grad(active3_ref, grad_ref)
        block_ref[1] = weight_grad(slope3_ref, pair_ref)

        def place(index, even_ref, odd_ref):
            for pair in range(8):
                even_ref[0, pair] = block_ref[index, 2 * pair * PIECE : (2 * pair + 1) * PIECE]
                odd_ref[0, pair] = block_ref[index, (2 * pair + 1) * PIECE : (2 * pair + 2) * PIECE]

        @pl.when(core_ref[0] == 0)
        def _():
            place(0, outs[2], outs[3])
            place(1, outs[0], outs[1])

        @pl.when(core_ref[0] == 1)
        def _():
            place(0, outs[3], outs[2])
            place(1, outs[1], outs[0])
    else:
        outs[1][...] = weight_grad(active3_ref, grad_ref)
        outs[0][...] = weight_grad(slope3_ref, pair_ref)


def feed(split, core, tokens_forms, hidden_weight, hidden_bias, return_weight, first, blocks):
    pair, grad = tokens_forms
    count = pair.shape[0]
    dim = pair.shape[1] // 2
    units = blocks * BLOCK
    whole = jax.ShapeDtypeStruct((count, dim), jnp.float32)
    if split:
        out_specs = [pl.BlockSpec((1, 8, PIECE, dim), lambda i: (i, 0, 0, 0))] * 4
        out_shape = [jax.ShapeDtypeStruct((blocks, 8, PIECE, dim), jnp.float32)] * 4
    else:
        out_specs = [rows(BLOCK, dim)] * 2
        out_shape = [jax.ShapeDtypeStruct((units, dim), jnp.float32)] * 2
    return pl.pallas_call(
        functools.partial(feed_kernel, split),
        grid=(blocks,),
        in_specs=[
            scalars(),
            fixed(pair.shape),
            fixed(grad.shape),
            pl.BlockSpec((dim, BLOCK), lambda i: (0, first + i)),
            pl.BlockSpec((1, BLOCK), lambda i: (0, first + i)),
            pl.BlockSpec((BLOCK, dim), lambda i: (first + i, 0)),
        ],
        out_specs=[fixed((count, dim)), fixed((count, dim)), pl.BlockSpec((1, BLOCK), lambda i: (0, i))] + out_specs,
        out_shape=[whole, whole, jax.ShapeDtypeStruct((1, units), jnp.float32)] + out_shape,
        scratch_shapes=[
            pltpu.VMEM((dim, 3 * BLOCK), jnp.bfloat16),
            pltpu.VMEM((3 * BLOCK, dim), jnp.bfloat16),
            pltpu.VMEM((count, 3 * BLOCK), jnp.bfloat16),
            pltpu.VMEM((count, 3 * BLOCK), jnp.bfloat16),
            pltpu.VMEM((2, BLOCK, dim), jnp.float32),
        ],
        compiler_params=params(60),
        cost_estimate=cost(36 * count * dim * units, 4 * (4 * dim * units + 5 * count * dim), 2 * count * units),
    )(core, pair, grad, hidden_weight, hidden_bias, return_weight)


def middle_kernel(parts, feeds, *refs):
    live_ref, middle_ref, cotangent_ref, gain_ref, bias_ref = refs[:5]
    result_parts = refs[5 : 5 + feeds]
    second_parts = refs[5 + feeds : 5 + 2 * feeds]
    weight_refs = refs[5 + 2 * feeds : 5 + 2 * feeds + parts]
    result_ref, d_middle_ref, sums_ref = refs[5 + 2 * feeds + parts : 8 + 2 * feeds + parts]
    mix_refs = refs[8 + 2 * feeds + parts :]
    middle = middle_ref[...]
    grad = cotangent_ref[...] * live_ref[pl.program_id(0)]
    result = middle + bias_ref[...]
    second = second_parts[0][...]
    for part in result_parts:
        result = result + part[...]
    for part in second_parts[1:]:
        second = second + part[...]
    result_ref[...] = result
    scaled, inverse = standardize(middle)
    d_middle = grad + norm_back(second * gain_ref[...], scaled, inverse)
    d_middle_ref[...] = d_middle

    @pl.when(pl.program_id(0) == 0)
    def _():
        sums_ref[...] = jnp.zeros_like(sums_ref)

    sums_ref[0:1, :] += jnp.sum(second * scaled, 0, keepdims=True)
    sums_ref[1:2, :] += jnp.sum(second, 0, keepdims=True)
    sums_ref[2:3, :] += jnp.sum(d_middle, 0, keepdims=True)
    sums_ref[3:4, :] += jnp.sum(grad, 0, keepdims=True)
    for weight_ref, mix_ref in zip(weight_refs, mix_refs):
        mix_ref[...] = dot_nt(d_middle, weight_ref[...])


def middle_backward(live, middle, cotangent, gain, bias, results, seconds, weights):
    count, dim = middle.shape
    parts = len(weights)
    block = jax.ShapeDtypeStruct((count, dim), jnp.float32)
    return pl.pallas_call(
        functools.partial(middle_kernel, parts, len(results)),
        grid=(count // PATCHES,),
        in_specs=[scalars()]
        + [rows(PATCHES, dim)] * 2
        + [fixed((1, dim))] * 2
        + [rows(PATCHES, dim)] * (2 * len(results))
        + [fixed(w.shape) for w in weights],
        out_specs=[rows(PATCHES, dim)] * 2 + [fixed((8, dim))] + [rows(PATCHES, w.shape[0]) for w in weights],
        out_shape=[block, block, jax.ShapeDtypeStruct((8, dim), jnp.float32)]
        + [jax.ShapeDtypeStruct((count, w.shape[0]), jnp.float32) for w in weights],
        compiler_params=params(60),
        cost_estimate=cost(6 * count * dim * dim, 4 * (dim * dim + 9 * count * dim)),
    )(live, middle, cotangent, gain, bias, *results, *seconds, *weights)


def attend_backward_kernel(
    heads, query_ref, keys_ref, values_ref, mixed_ref, grad_ref, lse_ref, strip_ref,
    d_proj_ref, flipped_ref, d_strip_ref, d_time_ref, bias_ref, total_ref, d_query_ref, d_keys_ref, d_values_ref,
):
    width = query_ref.shape[1]
    image = pl.program_id(0)

    @pl.when(image == 0)
    def _():
        build_bias(strip_ref, bias_ref, heads)
        total_ref[...] = jnp.zeros_like(total_ref)

    d_query_ref[...] = jnp.zeros_like(d_query_ref)
    d_keys_ref[...] = jnp.zeros_like(d_keys_ref)
    d_values_ref[...] = jnp.zeros_like(d_values_ref)
    for head in range(heads):
        start, stop, _ = head_window(head, width)
        mask = head_mask(head, width)
        query = jnp.where(mask, query_ref[:, start:stop], 0.0)
        keys = jnp.where(mask, keys_ref[:, start:stop], 0.0)
        grad = jnp.where(mask, grad_ref[:, start:stop], 0.0)
        scores = dot_nt(query, keys) + bias_ref[head]
        prob = jnp.exp(scores - lse_ref[:, head : head + 1])
        d_prob = dot_nt(grad, values_ref[:, start:stop])
        delta = jnp.sum(grad * mixed_ref[:, start:stop], -1, keepdims=True)
        d_scores = prob * (d_prob - delta)
        total_ref[head] += d_scores
        d_values_ref[:, start:stop] += dot_tn(prob, grad)
        d_query_ref[:, start:stop] += dot_nn(d_scores, keys)
        d_keys_ref[:, start:stop] += dot_tn(d_scores, query)
    d_proj_ref[:, :width] = d_query_ref[...] * SCALE
    d_proj_ref[:, width : 2 * width] = d_keys_ref[...]
    d_proj_ref[:, 2 * width :] = d_values_ref[...]
    d_time_ref[0] = jnp.sum(d_proj_ref[...], 0, keepdims=True)
    flipped_ref[:width] = (d_query_ref[...] * SCALE).T
    flipped_ref[width : 2 * width] = d_keys_ref[...].T
    flipped_ref[2 * width :] = d_values_ref[...].T

    @pl.when(image == pl.num_programs(0) - 1)
    def _():
        d_strip_ref[...] = jnp.zeros_like(d_strip_ref)

        def one(head, carry):
            for row in range(SIDE):
                shift = (SIDE - 1 - row) * SIDE
                d_strip_ref[head, :, shift : shift + PATCHES] += total_ref[head, row * SIDE : (row + 1) * SIDE, :]
            return carry

        lax.fori_loop(0, heads, one, 0)


def attend_backward(query, keys, values, mixed, grad, lse, strips):
    count, width = query.shape
    heads = strips.shape[0]
    images = count // PATCHES
    return pl.pallas_call(
        functools.partial(attend_backward_kernel, heads),
        grid=(images,),
        in_specs=[rows(PATCHES, width)] * 5 + [rows(PATCHES, heads), fixed(strips.shape)],
        out_specs=[
            rows(PATCHES, 3 * width),
            pl.BlockSpec((3 * width, PATCHES), lambda i: (0, i)),
            fixed(strips.shape),
            pl.BlockSpec((1, 1, 3 * width), lambda i: (i, 0, 0)),
        ],
        out_shape=[
            jax.ShapeDtypeStruct((count, 3 * width), jnp.float32),
            jax.ShapeDtypeStruct((3 * width, count), jnp.float32),
            jax.ShapeDtypeStruct(strips.shape, jnp.float32),
            jax.ShapeDtypeStruct((images, 1, 3 * width), jnp.float32),
        ],
        scratch_shapes=[pltpu.VMEM((heads, PATCHES, PATCHES), jnp.float32)] * 2
        + [pltpu.VMEM((PATCHES, width), jnp.float32)] * 3,
        compiler_params=params(56),
        cost_estimate=cost(30 * count * PATCHES * 256 * heads, 4 * 9 * count * width),
    )(query, keys, values, mixed, grad, lse, strips)


STEP = 576


def attend_weights_kernel(split, steps, core_ref, *refs):
    lefts, rights = refs[: len(steps)], refs[len(steps) : 2 * len(steps)]
    outs = refs[2 * len(steps) :]
    step = pl.program_id(0)
    piece = STEP // 8
    begin = 0
    for left_ref, right_ref, count in zip(lefts, rights, steps):

        @pl.when((step >= begin) & (step < begin + count))
        def _(left_ref=left_ref, right_ref=right_ref):
            value = dot_nn(left_ref[...], right_ref[...])
            if split:

                def store(even_ref, odd_ref):
                    for pair in range(4):
                        even_ref[pair] = value[2 * pair * piece : (2 * pair + 1) * piece]
                        odd_ref[pair] = value[(2 * pair + 1) * piece : (2 * pair + 2) * piece]

                pl.when(core_ref[0] == 0)(lambda: store(outs[0], outs[1]))
                pl.when(core_ref[0] == 1)(lambda: store(outs[1], outs[0]))
            else:
                outs[0][...] = value

        begin += count


def attend_weights(split, core, lefts, rights, firsts, steps):
    count, dim = rights[0].shape
    total = sum(steps)
    starts = [sum(steps[:i]) for i in range(len(steps))]

    def left_spec(start, first, size):
        return pl.BlockSpec((STEP, count), lambda i: (first + jnp.clip(i - start, 0, size - 1), 0))

    if split:
        out_specs = [pl.BlockSpec((4, STEP // 8, dim), lambda i: (i, 0, 0))] * 2
        out_shape = [jax.ShapeDtypeStruct((4 * total, STEP // 8, dim), jnp.float32)] * 2
    else:
        out_specs = [rows(STEP, dim)]
        out_shape = [jax.ShapeDtypeStruct((STEP * total, dim), jnp.float32)]
    return pl.pallas_call(
        functools.partial(attend_weights_kernel, split, steps),
        grid=(total,),
        in_specs=[scalars()]
        + [left_spec(a, b, c) for a, b, c in zip(starts, firsts, steps)]
        + [fixed((count, dim)) for _ in rights],
        out_specs=out_specs,
        out_shape=out_shape,
        compiler_params=params(60),
        cost_estimate=cost(6 * count * dim * STEP * total, 4 * (dim * STEP * total + count * 3 * dim)),
    )(core, *lefts, *rights)


def first_kernel(parts, *refs):
    tokens_ref, d_middle_ref, gain_ref = refs[:3]
    d_proj_refs = refs[3 : 3 + parts]
    weight_refs = refs[3 + parts : 3 + 2 * parts]
    out_ref, sums_ref = refs[3 + 2 * parts :]
    first = dot_nn(d_proj_refs[0][...], weight_refs[0][...])
    for d_proj_ref, weight_ref in zip(d_proj_refs[1:], weight_refs[1:]):
        first = first + dot_nn(d_proj_ref[...], weight_ref[...])
    scaled, inverse = standardize(tokens_ref[...])
    out_ref[...] = d_middle_ref[...] + norm_back(first * gain_ref[...], scaled, inverse)

    @pl.when(pl.program_id(0) == 0)
    def _():
        sums_ref[...] = jnp.zeros_like(sums_ref)

    sums_ref[0:1, :] += jnp.sum(first * scaled, 0, keepdims=True)
    sums_ref[1:2, :] += jnp.sum(first, 0, keepdims=True)


def first_backward(tokens, d_middle, gain, d_projs, weights, begin, images):
    dim = tokens.shape[1]
    count = images * PATCHES

    def some(width):
        return pl.BlockSpec((PATCHES, width), lambda i: (begin + i, 0))

    parts = len(d_projs)
    return pl.pallas_call(
        functools.partial(first_kernel, parts),
        grid=(count // PATCHES,),
        in_specs=[some(dim)] * 2
        + [fixed((1, dim))]
        + [some(d.shape[1]) for d in d_projs]
        + [fixed(w.shape) for w in weights],
        out_specs=[rows(PATCHES, dim), fixed((8, dim))],
        out_shape=[jax.ShapeDtypeStruct((count, dim), jnp.float32), jax.ShapeDtypeStruct((8, dim), jnp.float32)],
        compiler_params=params(60),
        cost_estimate=cost(18 * count * dim * dim, 4 * (3 * dim * dim + 6 * count * dim)),
    )(tokens, d_middle, gain, *d_projs, *weights)


def offset_matrix():
    place = jnp.arange(PATCHES)
    offset = place // SIDE - place % SIDE + SIDE - 1
    return (jnp.arange(STRIP)[:, None] == offset[None, :]).astype(jnp.float32)


def make_strips(table):
    heads = table.shape[0]
    grid = table.reshape(heads, STRIP, STRIP)[:, ::-1]
    wide = jnp.einsum("hmo,op->hmp", grid, offset_matrix(), precision=HIGHEST)
    wide = wide.reshape(heads, STRIP, SIDE, SIDE).transpose(0, 2, 1, 3).reshape(heads, SIDE, STRIP * SIDE)
    return jnp.pad(wide, ((0, 0), (0, 0), (0, 512 - STRIP * SIDE)))


def table_gradient(d_strips):
    heads = d_strips.shape[0]
    wide = d_strips[:, :, : STRIP * SIDE].reshape(heads, SIDE, STRIP, SIDE).transpose(0, 2, 1, 3)
    grid = jnp.einsum("hmp,op->hmo", wide.reshape(heads, STRIP, PATCHES), offset_matrix(), precision=HIGHEST)
    return grid[:, ::-1].reshape(heads, STRIP * STRIP)


def pick(array, index, axis):
    return lax.dynamic_index_in_dim(array, index, axis, keepdims=False)


def join(*values):
    return lax.optimization_barrier(values)


class Ring:
    def __init__(self):
        place = lax.axis_index("dp")
        self.place = place
        self.bits = [place & 1, (place >> 1) & 1, (place >> 2) & 1, (place >> 3) & 1]

    def across(self, value):
        return lax.ppermute(value, "mp", [(0, 1), (1, 0)])

    def along(self, value, bit):
        return lax.ppermute(value, "dp", [(i, i ^ (1 << bit)) for i in range(16)])

    def ordered(self, mine, theirs, bit, axis=0):
        flag = self.bits[bit] == 0
        return jnp.concatenate([jnp.where(flag, mine, theirs), jnp.where(flag, theirs, mine)], axis)

    def core_half(self, weight, base, count):
        half = count // 2
        return lax.dynamic_slice(weight, (base + self.bits[0] * half, 0), (half, weight.shape[1]))

    def share(self, weight, count, first, width):
        part = count // 16
        return lax.dynamic_slice(weight, (self.place * part, first), (part, width))

    def spread(self, part):
        return lax.all_gather(part, "dp", axis=0, tiled=True)

    def all_sum(self, value):
        value = value + self.along(value, 0)
        value = value + self.across(value)
        for bit in (1, 2, 3):
            value = value + self.along(value, bit)
        return value

    def rows_step(self, value, bit):
        return self.ordered(value, self.along(value, bit), bit)


class Reduction:
    def __init__(self, ring, axis):
        self.ring = ring
        self.axis = axis
        self.terms = {}
        self.level = {}

    def begin(self, side, keep, send):
        self.terms[side] = [keep, self.ring.along(send, 0)]
        self.level[side] = 1

    def value(self, side):
        out = self.terms[side][0]
        for term in self.terms[side][1:]:
            out = out + term
        return out

    def send(self, side):
        bit = self.ring.bits[self.level[side]]
        kept = []
        out = 0.0
        for term in self.terms[side]:
            shape = term.shape
            axis = self.axis
            cut = term.reshape(shape[:axis] + (shape[axis] // 2, 2) + shape[axis + 1 :])
            kept.append(pick(cut, bit, axis + 1))
            out = out + pick(cut, 1 - bit, axis + 1)
        self.terms[side] = kept
        return out

    def pass_on(self, side, value):
        self.terms[side].append(self.ring.along(value, self.level[side]))
        self.level[side] += 1

    def cross(self, value):
        self.terms["own"].append(self.ring.across(value))

    def gather(self, value):
        return lax.all_gather(value, "dp", axis=self.axis, tiled=True)

    def back(self, value, bit):
        axis = self.axis
        got = self.ring.along(value, bit)
        value, got = (v.reshape(v.shape[: axis + 1] + (1,) + v.shape[axis + 1 :]) for v in (value, got))
        out = self.ring.ordered(value, got, bit, axis + 1)
        return out.reshape(out.shape[:axis] + (-1,) + out.shape[axis + 2 :])


def body(split, *args):
    (
        tokens, cotangent, bucket, counts, first_gain, first_shift, attend_weight, time_weight, time_table,
        bias_table, output_weight, output_bias, second_gain, second_shift, hidden_weight, hidden_bias,
        return_weight, return_bias,
    ) = args
    own_images, patches, dim = tokens.shape
    images = bucket.shape[0]
    buckets = time_table.shape[0]
    heads_local = bias_table.shape[0]
    width = attend_weight.shape[2]
    units = hidden_bias.shape[0]
    group = lax.axis_index("dp")
    rank = lax.axis_index("mp")
    first_own = rank * own_images
    live = (first_own + jnp.arange(own_images) < counts[group]).astype(jnp.float32)
    inv_total = 1.0 / jnp.sum(counts).astype(jnp.float32)
    core = (group & 1).reshape(1)

    def row(vector):
        return vector.reshape(1, -1)

    def column(vector):
        return vector.reshape(-1, 1)

    tokens2 = tokens.reshape(own_images * patches, dim)
    cotangent2 = cotangent.reshape(own_images * patches, dim)
    onehot = (bucket[:, None] == jnp.arange(buckets)[None, :]).astype(jnp.float32)
    time_vec = jnp.dot(onehot, time_table, precision=HIGHEST)
    time_proj = jnp.einsum("sd,ced->sce", time_vec, time_weight.transpose(0, 2, 1), precision=HIGH)
    attend_own = attend_weight.transpose(0, 2, 1).reshape(3 * width, dim)
    norm_first = (row(first_gain), row(first_shift))
    norm_second = (row(second_gain), row(second_shift))

    def time_gradient(packed):
        d_time_all = packed[:, :-1].reshape(-1, 3, width)
        onehot_all = packed[:, -1:].astype(jnp.int32) == jnp.arange(buckets)[None, :]
        time_all = jnp.dot(onehot_all.astype(jnp.float32), time_table, precision=HIGHEST)
        grad = jnp.einsum("sce,sd->ced", d_time_all * inv_total, time_all, precision=HIGH)
        return grad.transpose(0, 2, 1)

    def absolute(own, other):
        flag = rank == 0
        return jnp.concatenate([jnp.where(flag, own, other), jnp.where(flag, other, own)], 0)

    def times_of(value):
        return value.reshape(own_images, 1, -1)

    if split:
        ring = Ring()
        less = units // BLOCK // 2
        cuts = [(0, less), (less, units // BLOCK - less)]
        table_other = ring.across(bias_table)
        bias_other = row(ring.across(hidden_bias))
        hidden_shares = [ring.share(hidden_weight, dim, first * BLOCK, blocks * BLOCK) for first, blocks in cuts]
        qk = ring.across(ring.share(attend_own, 2 * width, 0, dim))
        hidden_share, hidden_share_2 = [ring.across(share) for share in hidden_shares]
        values_half = ring.core_half(attend_own, 2 * width, width)
        output_half = ring.core_half(output_weight, 0, width)
        qk, table_other, bias_other, values_half, output_half, time_proj, strips_own = join(
            qk, table_other, bias_other, values_half, output_half, time_proj, make_strips(bias_table)
        )
        attend_qk = ring.spread(qk)
        values_mine = ring.across(values_half)
        output_mine = ring.across(output_half)
        time_mine = lax.dynamic_slice_in_dim(time_proj, first_own, own_images, 0)
        time_theirs = lax.dynamic_slice_in_dim(time_proj, (1 - rank) * own_images, own_images, 0)
        time_other = ring.across(time_theirs)
        own = attend_forward(tokens2, *norm_first, attend_own, times_of(time_mine), strips_own)
        return_halves = [ring.core_half(return_weight, first * BLOCK, blocks * BLOCK) for first, blocks in cuts]
        own, values_mine, output_mine, time_other, return_half, hidden_share, hidden_share_2 = join(
            own, values_mine, output_mine, time_other, return_halves[0], hidden_share, hidden_share_2
        )
        hidden_other = [ring.spread(hidden_share), ring.spread(hidden_share_2)]
        strips_other = make_strips(table_other)
        values_full = ring.ordered(values_mine, ring.along(values_mine, 0), 0)
        output_other = ring.ordered(output_mine, ring.along(output_mine, 0), 0)
        attend_other = jnp.concatenate([attend_qk, values_full], 0)
        return_mine = ring.across(return_half)
        other = attend_forward(tokens2, *norm_first, attend_other, times_of(time_other), strips_other)
        attend = [attend_own, attend_other]
        output = [output_weight, output_other]
        other, return_mine = join(other, return_mine)
        return_theirs = ring.along(return_mine, 0)
        middle, *forms = output_forward(
            live, tokens2, cotangent2, [own[3], other[3]], output, row(output_bias), *norm_second
        )
        forms, return_theirs, return_half = join(forms, return_theirs, return_halves[1])
        return_1 = ring.ordered(return_mine, return_theirs, 0)
        return_mine = ring.across(return_half)

        def feed_other(forms, index, hidden, back):
            first, blocks = cuts[index]
            bias = bias_other[:, first * BLOCK : (first + blocks) * BLOCK]
            return feed(True, core, forms, hidden, bias, back, 0, blocks)

        def feed_own(forms, index):
            return feed(True, core, forms, hidden_weight, row(hidden_bias), return_weight, *cuts[index])

        h1, h2, r1, r2, qa, qb = (Reduction(ring, axis) for axis in (1, 1, 1, 1, 0, 0))
        other_1 = feed_other(forms, 0, hidden_other[0], return_1)
        forms, other_1, return_mine = join(forms, other_1, return_mine)
        return_2 = ring.ordered(return_mine, ring.along(return_mine, 0), 0)
        forms, return_2, sent = join(forms, return_2, other_1[3:7])
        h1.begin("other", *sent[:2])
        r1.begin("other", *sent[2:])
        other_2 = feed_other(forms, 1, hidden_other[1], return_2)
        forms, other_2, a, b = join(forms, other_2, h1.value("other"), r1.send("other"))
        h1_cross, r1_y = a, b
        h2.begin("other", *other_2[3:5])
        r2.begin("other", *other_2[5:7])
        h1_crossed = ring.across(h1_cross)
        r1.pass_on("other", r1_y)
        own_1 = feed_own(forms, 0)
        forms, own_1, a, b, h1_crossed, r1.terms["other"] = join(
            forms, own_1, h2.value("other"), r2.send("other"), h1_crossed, r1.terms["other"]
        )
        h1.begin("own", *own_1[3:5])
        r1.begin("own", *own_1[5:7])
        h1.terms["own"].append(h1_crossed)
        h2_crossed = ring.across(a)
        r2.pass_on("other", b)
        own_2 = feed_own(forms, 1)
        middle, own_2, a, b, h2_crossed = join(middle, own_2, r1.send("own"), r1.value("other"), h2_crossed)
        h2.begin("own", *own_2[3:5])
        r2.begin("own", *own_2[5:7])
        h2.terms["own"].append(h2_crossed)
        r1.pass_on("own", a)
        r1.cross(b)
        fed = [other_1, own_1, other_2, own_2]
        result, d_middle, second_sums, d_mixed_own, d_mixed_other = middle_backward(
            live, middle, cotangent2, row(second_gain), row(return_bias), [f[0] for f in fed], [f[1] for f in fed], output
        )
        d_mixed_other, a, b, c = join(d_mixed_other, h1.send("own"), r2.value("other"), r1.send("own"))
        h1.pass_on("own", a)
        r2_crossed = ring.across(b)
        r1.pass_on("own", c)
        attended_other = attend_backward(*other[:4], d_mixed_other, other[5], strips_other)
        attended_other, a, b, c, r2_crossed = join(
            attended_other, h1.send("own"), r1.send("own"), h2.send("own"), r2_crossed
        )
        h1.pass_on("own", a)
        r1.pass_on("own", b)
        h2.pass_on("own", c)

        def pair_up(first, second):
            return jnp.stack([first, second]).reshape(1, -1, dim)

        def weights_a(attended, normed):
            return attend_weights(True, core, [attended[1]], [normed], [0], [2])

        def weights_b(attended, normed, flipped_mixed):
            return attend_weights(True, core, [attended[1], flipped_mixed], [normed, d_middle], [2, 0], [1, 1])

        normed_first = own[6]
        part = weights_a(attended_other, normed_first)
        part, normed_first = join(part, normed_first)
        qa.begin("other", *part)
        part = weights_b(attended_other, normed_first, other[4])
        part, d_mixed_own, a, b, c, d, e = join(
            part, d_mixed_own, qa.value("other"), h1.send("own"), r2.send("own"), h2.send("own"), r1.value("own")
        )
        qb.begin("other", *part)
        qa_first = ring.across(a[:4])
        h1.pass_on("own", b)
        r2.pass_on("own", c)
        r2.terms["own"].append(r2_crossed)
        h2.pass_on("own", d)
        return_1 = e
        attended_own = attend_backward(*own[:4], d_mixed_own, own[5], strips_own)
        attended_own, a, b, c, d, e, qa_first = join(
            attended_own, qb.send("other"), pair_up(h1.value("own"), return_1), r2.send("own"), h2.send("own"), a[4:],
            qa_first,
        )
        qb.pass_on("other", a)
        units_1 = ring.spread(b)
        r2.pass_on("own", c)
        h2.pass_on("own", d)
        qa_second = ring.across(e)
        d_time_got = ring.across(attended_other[3].reshape(own_images, 3, width))
        part = weights_b(attended_own, normed_first, own[4])
        part, normed_first, d_time_got = join(part, normed_first, d_time_got)
        d_time = absolute(attended_own[3].reshape(own_images, 3, width), d_time_got)
        packed = jnp.concatenate([d_time.reshape(images, -1), bucket.astype(jnp.float32)[:, None]], 1)
        packed = ring.rows_step(packed, 0)
        qb.begin("own", *part)
        part = weights_a(attended_own, normed_first)
        part, d_projs, a, b, c, qa_second, packed = join(
            part, [attended_own[0], attended_other[0]], qb.send("own"), qb.value("other"), r2.send("own"),
            qa_second, packed,
        )
        qa.begin("own", *part)
        qa.terms["own"].append(jnp.concatenate([qa_first, qa_second], 0))
        qb.pass_on("own", a)
        qb.cross(b)
        r2.pass_on("own", c)
        packed = ring.rows_step(packed, 1)
        half = own_images // 2
        tokens_a, sums_a = first_backward(tokens2, d_middle, row(first_gain), d_projs, attend, 0, half)
        tokens_a, d_projs, a, b, c, packed = join(
            tokens_a, d_projs, qa.send("own"), qb.send("own"), pair_up(h2.value("own"), r2.value("own")), packed
        )
        qa.pass_on("own", a)
        qb.pass_on("own", b)
        units_2 = ring.spread(c)
        packed = ring.rows_step(packed, 2)
        tokens_b, sums_b = first_backward(
            tokens2, d_middle, row(first_gain), d_projs, attend, half, own_images - half
        )
        tokens_b, sums_b, a, b, packed = join(tokens_b, sums_b, qa.send("own"), qb.send("own"), packed)
        qa.pass_on("own", a)
        qb.pass_on("own", b)
        packed = ring.rows_step(packed, 3)
        a, packed, strips_a, strips_b, d_time, tokens_a, units_1 = join(
            qa.send("own"), packed, attended_own[2], attended_other[2], d_time, tokens_a, units_1
        )
        qa.pass_on("own", a)
        d_time_vec = jnp.einsum("sce,ced->sd", d_time, time_weight.transpose(0, 2, 1), precision=HIGH)
        time_table_part = jnp.dot(onehot.T, d_time_vec, precision=HIGHEST)
        table_full = absolute(table_gradient(strips_a), table_gradient(strips_b))
        bias_own = jnp.concatenate([own_1[2][0], own_2[2][0]])
        hidden_bias_full = absolute(bias_own, jnp.concatenate([other_1[2][0], other_2[2][0]]))
        first_sums = sums_a + sums_b
        small = [
            first_sums[0], first_sums[1], time_table_part, second_sums[2], second_sums[0], second_sums[1],
            second_sums[3], table_full, hidden_bias_full,
        ]
        flat = jnp.concatenate([v.reshape(-1) for v in small]) * inv_total
        flat = jnp.pad(flat, (0, -flat.shape[0] % 1024)).reshape(-1, 128)
        last = jnp.stack([qa.value("own"), qb.value("own")]).reshape(1, -1, dim)
        last, flat, packed, units_1, units_2, tokens_a = join(last, flat, packed, units_1, units_2, tokens_a)
        attend_all = ring.spread(last).reshape(16, 2, -1, dim)
        flat = ring.all_sum(flat)
        time_weight_grad = time_gradient(packed)
        tokens_grad = jnp.concatenate([tokens_a, tokens_b], 0)

        def units_of(index):
            found = [
                g.reshape(16, 2, -1, PIECE, dim)[:, index].transpose(1, 0, 2, 3).reshape(-1, dim)
                for g in (units_1, units_2)
            ]
            return jnp.concatenate(found, 0) * inv_total

        hidden_grad = units_of(0).T
        return_grad = units_of(1)
        attend_all = attend_all.transpose(1, 0, 2, 3).reshape(4, width, dim) * inv_total
        attend_weight_grad = attend_all[:3].transpose(0, 2, 1)
        output_weight_grad = attend_all[3]
    else:
        attend = [lax.all_gather(attend_weight, "mp", axis=2, tiled=True).transpose(0, 2, 1).reshape(-1, dim)]
        output = [lax.all_gather(output_weight, "mp", axis=0, tiled=True)]
        hidden_full = lax.all_gather(hidden_weight, "mp", axis=1, tiled=True)
        return_full = lax.all_gather(return_weight, "mp", axis=0, tiled=True)
        bias_full = lax.all_gather(hidden_bias, "mp", axis=0, tiled=True)
        strips = make_strips(lax.all_gather(bias_table, "mp", axis=0, tiled=True))
        full = lax.all_gather(time_proj, "mp", axis=2, tiled=True)
        times = times_of(lax.dynamic_slice_in_dim(full, first_own, own_images, 0))
        all_of = attend_forward(tokens2, *norm_first, attend[0], times, strips)
        middle, *forms = output_forward(
            live, tokens2, cotangent2, [all_of[3]], output, row(output_bias), *norm_second
        )
        fed = feed(False, core, forms, hidden_full, row(bias_full), return_full, 0, hidden_full.shape[1] // BLOCK)
        result, d_middle, second_sums, d_mixed = middle_backward(
            live, middle, cotangent2, row(second_gain), row(return_bias), [fed[0]], [fed[1]], output
        )
        attended = attend_backward(*all_of[:4], d_mixed, all_of[5], strips)
        (attend_full,) = attend_weights(
            False, core, [attended[1]], [all_of[6]], [0], [attended[1].shape[0] // STEP]
        )
        (output_full,) = attend_weights(False, core, [all_of[4]], [d_middle], [0], [dim // STEP])
        tokens_grad, first_sums = first_backward(
            tokens2, d_middle, row(first_gain), [attended[0]], attend, 0, own_images
        )

        def settle(value, axis):
            return lax.psum(lax.psum_scatter(value * inv_total, "mp", scatter_dimension=axis, tiled=True), "dp")

        hidden_grad = settle(fed[3], 0).T
        return_grad = settle(fed[4], 0)
        attend_weight_grad = settle(attend_full.reshape(3, -1, dim), 1).transpose(0, 2, 1)
        output_weight_grad = settle(output_full, 0)
        table_full = table_gradient(attended[2])
        hidden_bias_full = fed[2][0]
        d_time = lax.all_gather(attended[3].reshape(own_images, 3, -1), "mp", axis=0, tiled=True)
        d_time = lax.dynamic_slice_in_dim(d_time, rank * width, width, 2)

        packed = jnp.concatenate([d_time.reshape(images, -1), bucket.astype(jnp.float32)[:, None]], 1)
        time_weight_grad = time_gradient(lax.all_gather(packed, "dp", axis=0, tiled=True))
        d_time_vec = jnp.einsum("sce,ced->sd", d_time, time_weight.transpose(0, 2, 1), precision=HIGH)
        time_table_part = jnp.dot(onehot.T, d_time_vec, precision=HIGHEST)
        small = [
            first_sums[0], first_sums[1], time_table_part, second_sums[2], second_sums[0], second_sums[1],
            second_sums[3], table_full, hidden_bias_full,
        ]
        flat = lax.psum(jnp.concatenate([v.reshape(-1) for v in small]) * inv_total, ("dp", "mp"))

    flat = flat.reshape(-1)
    sums = []
    start = 0
    for s in small:
        sums.append(flat[start : start + s.size].reshape(s.shape))
        start += s.size
    bias_table_grad = lax.dynamic_slice_in_dim(sums[7], rank * heads_local, heads_local, 0)
    hidden_bias_grad = lax.dynamic_slice_in_dim(sums[8], rank * units, units, 0)
    return (
        result.reshape(tokens.shape),
        tokens_grad.reshape(tokens.shape),
        sums[0],
        sums[1],
        attend_weight_grad,
        time_weight_grad,
        sums[2],
        bias_table_grad,
        output_weight_grad,
        sums[3],
        sums[4],
        sums[5],
        hidden_grad,
        hidden_bias_grad,
        return_grad,
        sums[6],
    )


def solution(mesh):
    in_specs = (
        P(("dp", "mp"), None, None),
        P(("dp", "mp"), None, None),
        P("dp"),
        P(),
        P(),
        P(),
        P(None, None, "mp"),
        P(None, None, "mp"),
        P(),
        P("mp", None),
        P("mp", None),
        P(),
        P(),
        P(),
        P(None, "mp"),
        P("mp"),
        P("mp", None),
        P(),
    )
    out_specs = (
        P(("dp", "mp"), None, None),
        P(("dp", "mp"), None, None),
        P(),
        P(),
        P(None, None, "mp"),
        P(None, None, "mp"),
        P(),
        P("mp", None),
        P("mp", None),
        P(),
        P(),
        P(),
        P(None, "mp"),
        P("mp"),
        P("mp", None),
        P(),
    )
    split = mesh.shape["dp"] == 16 and mesh.shape["mp"] == 2
    return jax.shard_map(
        functools.partial(body, split), mesh=mesh, in_specs=in_specs, out_specs=out_specs, check_vma=False
    )
```

```python
import functools
import math

import jax
import jax.numpy as jnp
from jax import lax
from jax.experimental import pallas as pl
from jax.experimental.pallas import tpu as pltpu
from jax.sharding import PartitionSpec as P

HEAD_DIM = 72
SIDE = 16
PATCHES = SIDE * SIDE
STRIP = 2 * SIDE - 1
EPS = 1e-05
SCALE = HEAD_DIM ** (-0.5)
MIB = 1024 * 1024
HIGHEST = lax.Precision.HIGHEST
HIGH = lax.Precision.HIGH


def dot_nn(a, b):
    return lax.dot_general(a, b, (((1,), (0,)), ((), ())), precision=HIGH, preferred_element_type=jnp.float32)


def dot_nt(a, b):
    return lax.dot_general(a, b, (((1,), (1,)), ((), ())), precision=HIGH, preferred_element_type=jnp.float32)


def dot_tn(a, b):
    return lax.dot_general(a, b, (((0,), (0,)), ((), ())), precision=HIGH, preferred_element_type=jnp.float32)


def standardize(values):
    centre = values - jnp.mean(values, -1, keepdims=True)
    inverse = lax.rsqrt(jnp.mean(centre * centre, -1, keepdims=True) + EPS)
    return centre * inverse, inverse


def norm_back(grad_hat, scaled, inverse):
    return inverse * (
        grad_hat
        - jnp.mean(grad_hat, -1, keepdims=True)
        - scaled * jnp.mean(grad_hat * scaled, -1, keepdims=True)
    )


def head_window(head, width):
    first = head * HEAD_DIM
    start = first // 128 * 128
    stop = min(-(-(first + HEAD_DIM) // 128) * 128, width)
    return start, stop, first - start


def head_mask(head, width):
    start, stop, offset = head_window(head, width)
    lane = lax.broadcasted_iota(jnp.int32, (1, stop - start), 1)
    return (lane >= offset) & (lane < offset + HEAD_DIM)


def fixed(shape, **kw):
    return pl.BlockSpec(shape, lambda i: (0,) * len(shape), pipeline_mode=pl.Buffered(1), **kw)


def rows(count, width):
    return pl.BlockSpec((count, width), lambda i: (i, 0))


def params(limit):
    return pltpu.CompilerParams(dimension_semantics=("arbitrary",), vmem_limit_bytes=limit * MIB)


def cost(flops, nbytes, trans=0):
    return pl.CostEstimate(flops=int(flops) // 1000, bytes_accessed=int(nbytes) // 1000, transcendentals=0)


def halves(value):
    high = value.astype(jnp.bfloat16)
    return high, (value - high.astype(jnp.float32)).astype(jnp.bfloat16)


def mul(a, b, left, right):
    return lax.dot_general(a, b, (((left,), (right,)), ((), ())), preferred_element_type=jnp.float32)


def scalars():
    return pl.BlockSpec(memory_space=pltpu.SMEM)


def build_bias(strip_ref, bias_ref, heads):
    def one(head, carry):
        strip = strip_ref[head]
        for row in range(SIDE):
            shift = (SIDE - 1 - row) * SIDE
            bias_ref[head, row * SIDE : (row + 1) * SIDE, :] = strip[:, shift : shift + PATCHES]
        return carry

    lax.fori_loop(0, heads, one, 0)


def attend_forward_kernel(
    heads, tokens_ref, gain_ref, shift_ref, weight_ref, time_ref, strip_ref,
    query_ref, keys_ref, values_ref, mixed_ref, flipped_ref, lse_ref, normed_ref, bias_ref,
):
    width = query_ref.shape[1]

    @pl.when(pl.program_id(0) == 0)
    def _():
        build_bias(strip_ref, bias_ref, heads)

    scaled, _ = standardize(tokens_ref[...])
    normed = scaled * gain_ref[...] + shift_ref[...]
    normed_ref[...] = normed
    proj = dot_nt(normed, weight_ref[...]) + time_ref[0]
    query_ref[...] = proj[:, :width] * SCALE
    keys_ref[...] = proj[:, width : 2 * width]
    values_ref[...] = proj[:, 2 * width :]
    mixed_ref[...] = jnp.zeros_like(mixed_ref)
    columns = lax.broadcasted_iota(jnp.int32, (1, heads), 1)
    stats = jnp.zeros((PATCHES, heads), jnp.float32)
    for head in range(heads):
        start, stop, _ = head_window(head, width)
        mask = head_mask(head, width)
        query = jnp.where(mask, query_ref[:, start:stop], 0.0)
        scores = dot_nt(query, keys_ref[:, start:stop]) + bias_ref[head]
        peak = jnp.max(scores, -1, keepdims=True)
        weights = jnp.exp(scores - peak)
        total = jnp.sum(weights, -1, keepdims=True)
        values = jnp.where(mask, values_ref[:, start:stop], 0.0)
        mixed_ref[:, start:stop] += dot_nn(weights, values) * (1.0 / total)
        stats = jnp.where(columns == head, peak + jnp.log(total), stats)
    lse_ref[...] = stats
    flipped_ref[...] = mixed_ref[...].T


def attend_forward(tokens, gain, shift, weight, time_proj, strips):
    count, dim = tokens.shape
    heads = strips.shape[0]
    width = weight.shape[0] // 3
    images = count // PATCHES
    piece = jax.ShapeDtypeStruct((count, width), jnp.float32)
    return pl.pallas_call(
        functools.partial(attend_forward_kernel, heads),
        grid=(images,),
        in_specs=[
            rows(PATCHES, dim),
            fixed((1, dim)),
            fixed((1, dim)),
            fixed((3 * width, dim)),
            pl.BlockSpec((1, 1, 3 * width), lambda i: (i, 0, 0)),
            fixed(strips.shape),
        ],
        out_specs=[rows(PATCHES, width)] * 4
        + [pl.BlockSpec((width, PATCHES), lambda i: (0, i)), rows(PATCHES, heads), rows(PATCHES, dim)],
        out_shape=[piece] * 4
        + [
            jax.ShapeDtypeStruct((width, count), jnp.float32),
            jax.ShapeDtypeStruct((count, heads), jnp.float32),
            jax.ShapeDtypeStruct((count, dim), jnp.float32),
        ],
        scratch_shapes=[pltpu.VMEM((heads, PATCHES, PATCHES), jnp.float32)],
        compiler_params=params(56),
        cost_estimate=cost(6 * count * dim * width * 3 + 24 * count * PATCHES * 256 * heads // 2, 4 * (weight.size + 6 * count * width)),
    )(tokens, gain, shift, weight, time_proj, strips)


def output_kernel(parts, *refs):
    live_ref, tokens_ref, cotangent_ref = refs[:3]
    mixed_refs = refs[3 : 3 + parts]
    weight_refs = refs[3 + parts : 3 + 2 * parts]
    bias_ref, gain_ref, shift_ref, middle_ref, pair_ref, grad_ref = refs[3 + 2 * parts :]
    dim = tokens_ref.shape[1]
    middle = tokens_ref[...] + bias_ref[...]
    for mixed_ref, weight_ref in zip(mixed_refs, weight_refs):
        middle = middle + dot_nn(mixed_ref[...], weight_ref[...])
    middle_ref[...] = middle
    scaled, _ = standardize(middle)
    normed = scaled * gain_ref[...] + shift_ref[...]
    pair_ref[:, :dim], pair_ref[:, dim:] = halves(normed)
    grad = cotangent_ref[...] * live_ref[pl.program_id(0)]
    grad_ref[:, :dim], grad_ref[:, dim:] = halves(grad)


def output_forward(live, tokens, cotangent, mixed, weights, bias, gain, shift):
    count, dim = tokens.shape
    parts = len(mixed)
    pair = jax.ShapeDtypeStruct((count, 2 * dim), jnp.bfloat16)
    return pl.pallas_call(
        functools.partial(output_kernel, parts),
        grid=(count // PATCHES,),
        in_specs=[scalars()]
        + [rows(PATCHES, dim)] * 2
        + [rows(PATCHES, m.shape[1]) for m in mixed]
        + [fixed(w.shape) for w in weights]
        + [fixed((1, dim))] * 3,
        out_specs=[
            rows(PATCHES, dim),
            rows(PATCHES, 2 * dim),
            rows(PATCHES, 2 * dim),
        ],
        out_shape=[
            jax.ShapeDtypeStruct((count, dim), jnp.float32),
            pair,
            pair,
        ],
        compiler_params=params(48),
        cost_estimate=cost(6 * count * dim * dim, 4 * (dim * dim + 5 * count * dim)),
    )(live, tokens, cotangent, *mixed, *weights, bias, gain, shift)


BLOCK = 256
PIECE = BLOCK // 16


def feed_kernel(split, core_ref, pair_ref, grad_ref, hidden_ref, bias_ref, return_ref, *refs):
    result_ref, second_ref, d_bias_ref = refs[:3]
    outs = refs[3:-5]
    hidden3_ref, return3_ref, active3_ref, slope3_ref, block_ref = refs[-5:]
    count = pair_ref.shape[0]
    dim = pair_ref.shape[1] // 2
    chunk = min(512, count)

    @pl.when(pl.program_id(0) == 0)
    def _():
        result_ref[...] = jnp.zeros_like(result_ref)
        second_ref[...] = jnp.zeros_like(second_ref)

    d_bias_ref[...] = jnp.zeros_like(d_bias_ref)
    high, low = halves(hidden_ref[...])
    hidden3_ref[:, :BLOCK] = high
    hidden3_ref[:, BLOCK : 2 * BLOCK] = high
    hidden3_ref[:, 2 * BLOCK :] = low
    high, low = halves(return_ref[...])
    return3_ref[:BLOCK] = high
    return3_ref[BLOCK : 2 * BLOCK] = high
    return3_ref[2 * BLOCK :] = low

    for begin in range(0, count, chunk):
        part = slice(begin, begin + chunk)
        hidden = (
            mul(pair_ref[part, :dim], hidden3_ref[:, :BLOCK], 1, 0)
            + mul(pair_ref[part, dim:], hidden3_ref[:, :BLOCK], 1, 0)
            + mul(pair_ref[part, :dim], hidden3_ref[:, 2 * BLOCK :], 1, 0)
            + bias_ref[...]
        )
        d_active = (
            mul(grad_ref[part, :dim], return3_ref[:BLOCK], 1, 1)
            + mul(grad_ref[part, dim:], return3_ref[:BLOCK], 1, 1)
            + mul(grad_ref[part, :dim], return3_ref[2 * BLOCK :], 1, 1)
        )
        cumul = 0.5 * (1.0 + lax.erf(hidden * 2.0 ** (-0.5)))
        high, low = halves(hidden * cumul)
        active3_ref[part, :BLOCK] = high
        active3_ref[part, BLOCK : 2 * BLOCK] = low
        active3_ref[part, 2 * BLOCK :] = high
        density = hidden * jnp.exp(-0.5 * hidden * hidden) * (1.0 / math.sqrt(2.0 * math.pi))
        d_hidden = d_active * (cumul + density)
        high, low = halves(d_hidden)
        slope3_ref[part, :BLOCK] = high
        slope3_ref[part, BLOCK : 2 * BLOCK] = low
        slope3_ref[part, 2 * BLOCK :] = high
        d_bias_ref[...] += jnp.sum(d_hidden, 0, keepdims=True)
        result_ref[part, :] += mul(active3_ref[part, :], return3_ref[...], 1, 0)
        second_ref[part, :] += mul(slope3_ref[part, :], hidden3_ref[...], 1, 1)

    def weight_grad(left_ref, right_ref):
        wide = mul(left_ref[:, :BLOCK], right_ref[...], 0, 0)
        return wide[:, :dim] + wide[:, dim:] + mul(left_ref[:, BLOCK : 2 * BLOCK], right_ref[:, :dim], 0, 0)

    if split:
        block_ref[0] = weight_grad(active3_ref, grad_ref)
        block_ref[1] = weight_grad(slope3_ref, pair_ref)

        def place(index, even_ref, odd_ref):
            for pair in range(8):
                even_ref[0, pair] = block_ref[index, 2 * pair * PIECE : (2 * pair + 1) * PIECE]
                odd_ref[0, pair] = block_ref[index, (2 * pair + 1) * PIECE : (2 * pair + 2) * PIECE]

        @pl.when(core_ref[0] == 0)
        def _():
            place(0, outs[2], outs[3])
            place(1, outs[0], outs[1])

        @pl.when(core_ref[0] == 1)
        def _():
            place(0, outs[3], outs[2])
            place(1, outs[1], outs[0])
    else:
        outs[1][...] = weight_grad(active3_ref, grad_ref)
        outs[0][...] = weight_grad(slope3_ref, pair_ref)


def feed(split, core, tokens_forms, hidden_weight, hidden_bias, return_weight, first, blocks):
    pair, grad = tokens_forms
    count = pair.shape[0]
    dim = pair.shape[1] // 2
    units = blocks * BLOCK
    whole = jax.ShapeDtypeStruct((count, dim), jnp.float32)
    if split:
        out_specs = [pl.BlockSpec((1, 8, PIECE, dim), lambda i: (i, 0, 0, 0))] * 4
        out_shape = [jax.ShapeDtypeStruct((blocks, 8, PIECE, dim), jnp.float32)] * 4
    else:
        out_specs = [rows(BLOCK, dim)] * 2
        out_shape = [jax.ShapeDtypeStruct((units, dim), jnp.float32)] * 2
    return pl.pallas_call(
        functools.partial(feed_kernel, split),
        grid=(blocks,),
        in_specs=[
            scalars(),
            fixed(pair.shape),
            fixed(grad.shape),
            pl.BlockSpec((dim, BLOCK), lambda i: (0, first + i)),
            pl.BlockSpec((1, BLOCK), lambda i: (0, first + i)),
            pl.BlockSpec((BLOCK, dim), lambda i: (first + i, 0)),
        ],
        out_specs=[fixed((count, dim)), fixed((count, dim)), pl.BlockSpec((1, BLOCK), lambda i: (0, i))] + out_specs,
        out_shape=[whole, whole, jax.ShapeDtypeStruct((1, units), jnp.float32)] + out_shape,
        scratch_shapes=[
            pltpu.VMEM((dim, 3 * BLOCK), jnp.bfloat16),
            pltpu.VMEM((3 * BLOCK, dim), jnp.bfloat16),
            pltpu.VMEM((count, 3 * BLOCK), jnp.bfloat16),
            pltpu.VMEM((count, 3 * BLOCK), jnp.bfloat16),
            pltpu.VMEM((2, BLOCK, dim), jnp.float32),
        ],
        compiler_params=params(60),
        cost_estimate=cost(36 * count * dim * units, 4 * (4 * dim * units + 5 * count * dim), 2 * count * units),
    )(core, pair, grad, hidden_weight, hidden_bias, return_weight)


def middle_kernel(parts, feeds, *refs):
    live_ref, middle_ref, cotangent_ref, gain_ref, bias_ref = refs[:5]
    result_parts = refs[5 : 5 + feeds]
    second_parts = refs[5 + feeds : 5 + 2 * feeds]
    weight_refs = refs[5 + 2 * feeds : 5 + 2 * feeds + parts]
    result_ref, d_middle_ref, sums_ref = refs[5 + 2 * feeds + parts : 8 + 2 * feeds + parts]
    mix_refs = refs[8 + 2 * feeds + parts :]
    middle = middle_ref[...]
    grad = cotangent_ref[...] * live_ref[pl.program_id(0)]
    result = middle + bias_ref[...]
    second = second_parts[0][...]
    for part in result_parts:
        result = result + part[...]
    for part in second_parts[1:]:
        second = second + part[...]
    result_ref[...] = result
    scaled, inverse = standardize(middle)
    d_middle = grad + norm_back(second * gain_ref[...], scaled, inverse)
    d_middle_ref[...] = d_middle

    @pl.when(pl.program_id(0) == 0)
    def _():
        sums_ref[...] = jnp.zeros_like(sums_ref)

    sums_ref[0:1, :] += jnp.sum(second * scaled, 0, keepdims=True)
    sums_ref[1:2, :] += jnp.sum(second, 0, keepdims=True)
    sums_ref[2:3, :] += jnp.sum(d_middle, 0, keepdims=True)
    sums_ref[3:4, :] += jnp.sum(grad, 0, keepdims=True)
    for weight_ref, mix_ref in zip(weight_refs, mix_refs):
        mix_ref[...] = dot_nt(d_middle, weight_ref[...])


def middle_backward(live, middle, cotangent, gain, bias, results, seconds, weights):
    count, dim = middle.shape
    parts = len(weights)
    block = jax.ShapeDtypeStruct((count, dim), jnp.float32)
    return pl.pallas_call(
        functools.partial(middle_kernel, parts, len(results)),
        grid=(count // PATCHES,),
        in_specs=[scalars()]
        + [rows(PATCHES, dim)] * 2
        + [fixed((1, dim))] * 2
        + [rows(PATCHES, dim)] * (2 * len(results))
        + [fixed(w.shape) for w in weights],
        out_specs=[rows(PATCHES, dim)] * 2 + [fixed((8, dim))] + [rows(PATCHES, w.shape[0]) for w in weights],
        out_shape=[block, block, jax.ShapeDtypeStruct((8, dim), jnp.float32)]
        + [jax.ShapeDtypeStruct((count, w.shape[0]), jnp.float32) for w in weights],
        compiler_params=params(60),
        cost_estimate=cost(6 * count * dim * dim, 4 * (dim * dim + 9 * count * dim)),
    )(live, middle, cotangent, gain, bias, *results, *seconds, *weights)


def attend_backward_kernel(
    heads, query_ref, keys_ref, values_ref, mixed_ref, grad_ref, lse_ref, strip_ref,
    d_proj_ref, flipped_ref, d_strip_ref, d_time_ref, bias_ref, total_ref, d_query_ref, d_keys_ref, d_values_ref,
):
    width = query_ref.shape[1]
    image = pl.program_id(0)

    @pl.when(image == 0)
    def _():
        build_bias(strip_ref, bias_ref, heads)
        total_ref[...] = jnp.zeros_like(total_ref)

    d_query_ref[...] = jnp.zeros_like(d_query_ref)
    d_keys_ref[...] = jnp.zeros_like(d_keys_ref)
    d_values_ref[...] = jnp.zeros_like(d_values_ref)
    for head in range(heads):
        start, stop, _ = head_window(head, width)
        mask = head_mask(head, width)
        query = jnp.where(mask, query_ref[:, start:stop], 0.0)
        keys = jnp.where(mask, keys_ref[:, start:stop], 0.0)
        grad = jnp.where(mask, grad_ref[:, start:stop], 0.0)
        scores = dot_nt(query, keys) + bias_ref[head]
        prob = jnp.exp(scores - lse_ref[:, head : head + 1])
        d_prob = dot_nt(grad, values_ref[:, start:stop])
        delta = jnp.sum(grad * mixed_ref[:, start:stop], -1, keepdims=True)
        d_scores = prob * (d_prob - delta)
        total_ref[head] += d_scores
        d_values_ref[:, start:stop] += dot_tn(prob, grad)
        d_query_ref[:, start:stop] += dot_nn(d_scores, keys)
        d_keys_ref[:, start:stop] += dot_tn(d_scores, query)
    d_proj_ref[:, :width] = d_query_ref[...] * SCALE
    d_proj_ref[:, width : 2 * width] = d_keys_ref[...]
    d_proj_ref[:, 2 * width :] = d_values_ref[...]
    d_time_ref[0] = jnp.sum(d_proj_ref[...], 0, keepdims=True)
    flipped_ref[:width] = (d_query_ref[...] * SCALE).T
    flipped_ref[width : 2 * width] = d_keys_ref[...].T
    flipped_ref[2 * width :] = d_values_ref[...].T

    @pl.when(image == pl.num_programs(0) - 1)
    def _():
        d_strip_ref[...] = jnp.zeros_like(d_strip_ref)

        def one(head, carry):
            for row in range(SIDE):
                shift = (SIDE - 1 - row) * SIDE
                d_strip_ref[head, :, shift : shift + PATCHES] += total_ref[head, row * SIDE : (row + 1) * SIDE, :]
            return carry

        lax.fori_loop(0, heads, one, 0)


def attend_backward(query, keys, values, mixed, grad, lse, strips):
    count, width = query.shape
    heads = strips.shape[0]
    images = count // PATCHES
    return pl.pallas_call(
        functools.partial(attend_backward_kernel, heads),
        grid=(images,),
        in_specs=[rows(PATCHES, width)] * 5 + [rows(PATCHES, heads), fixed(strips.shape)],
        out_specs=[
            rows(PATCHES, 3 * width),
            pl.BlockSpec((3 * width, PATCHES), lambda i: (0, i)),
            fixed(strips.shape),
            pl.BlockSpec((1, 1, 3 * width), lambda i: (i, 0, 0)),
        ],
        out_shape=[
            jax.ShapeDtypeStruct((count, 3 * width), jnp.float32),
            jax.ShapeDtypeStruct((3 * width, count), jnp.float32),
            jax.ShapeDtypeStruct(strips.shape, jnp.float32),
            jax.ShapeDtypeStruct((images, 1, 3 * width), jnp.float32),
        ],
        scratch_shapes=[pltpu.VMEM((heads, PATCHES, PATCHES), jnp.float32)] * 2
        + [pltpu.VMEM((PATCHES, width), jnp.float32)] * 3,
        compiler_params=params(56),
        cost_estimate=cost(30 * count * PATCHES * 256 * heads, 4 * 9 * count * width),
    )(query, keys, values, mixed, grad, lse, strips)


STEP = 576


def attend_weights_kernel(split, steps, core_ref, *refs):
    lefts, rights = refs[: len(steps)], refs[len(steps) : 2 * len(steps)]
    outs = refs[2 * len(steps) :]
    step = pl.program_id(0)
    piece = STEP // 8
    begin = 0
    for left_ref, right_ref, count in zip(lefts, rights, steps):

        @pl.when((step >= begin) & (step < begin + count))
        def _(left_ref=left_ref, right_ref=right_ref):
            value = dot_nn(left_ref[...], right_ref[...])
            if split:

                def store(even_ref, odd_ref):
                    for pair in range(4):
                        even_ref[pair] = value[2 * pair * piece : (2 * pair + 1) * piece]
                        odd_ref[pair] = value[(2 * pair + 1) * piece : (2 * pair + 2) * piece]

                pl.when(core_ref[0] == 0)(lambda: store(outs[0], outs[1]))
                pl.when(core_ref[0] == 1)(lambda: store(outs[1], outs[0]))
            else:
                outs[0][...] = value

        begin += count


def attend_weights(split, core, lefts, rights, firsts, steps):
    count, dim = rights[0].shape
    total = sum(steps)
    starts = [sum(steps[:i]) for i in range(len(steps))]

    def left_spec(start, first, size):
        return pl.BlockSpec((STEP, count), lambda i: (first + jnp.clip(i - start, 0, size - 1), 0))

    if split:
        out_specs = [pl.BlockSpec((4, STEP // 8, dim), lambda i: (i, 0, 0))] * 2
        out_shape = [jax.ShapeDtypeStruct((4 * total, STEP // 8, dim), jnp.float32)] * 2
    else:
        out_specs = [rows(STEP, dim)]
        out_shape = [jax.ShapeDtypeStruct((STEP * total, dim), jnp.float32)]
    return pl.pallas_call(
        functools.partial(attend_weights_kernel, split, steps),
        grid=(total,),
        in_specs=[scalars()]
        + [left_spec(a, b, c) for a, b, c in zip(starts, firsts, steps)]
        + [fixed((count, dim)) for _ in rights],
        out_specs=out_specs,
        out_shape=out_shape,
        compiler_params=params(60),
        cost_estimate=cost(6 * count * dim * STEP * total, 4 * (dim * STEP * total + count * 3 * dim)),
    )(core, *lefts, *rights)


def first_kernel(parts, aliased, *refs):
    refs = refs[1:] if aliased else refs
    tokens_ref, d_middle_ref, gain_ref = refs[:3]
    d_proj_refs = refs[3 : 3 + parts]
    weight_refs = refs[3 + parts : 3 + 2 * parts]
    out_ref, sums_ref = refs[3 + 2 * parts :]
    first = dot_nn(d_proj_refs[0][...], weight_refs[0][...])
    for d_proj_ref, weight_ref in zip(d_proj_refs[1:], weight_refs[1:]):
        first = first + dot_nn(d_proj_ref[...], weight_ref[...])
    scaled, inverse = standardize(tokens_ref[...])
    out_ref[...] = d_middle_ref[...] + norm_back(first * gain_ref[...], scaled, inverse)

    @pl.when(pl.program_id(0) == 0)
    def _():
        sums_ref[...] = jnp.zeros_like(sums_ref)

    sums_ref[0:1, :] += jnp.sum(first * scaled, 0, keepdims=True)
    sums_ref[1:2, :] += jnp.sum(first, 0, keepdims=True)


def first_backward(tokens, d_middle, gain, d_projs, weights, begin, images, previous=()):
    dim = tokens.shape[1]
    count = images * PATCHES

    def some(width):
        return pl.BlockSpec((PATCHES, width), lambda i: (begin + i, 0))

    parts = len(d_projs)
    return pl.pallas_call(
        functools.partial(first_kernel, parts, len(previous) > 0),
        grid=(images,),
        in_specs=[pl.BlockSpec(memory_space=pl.ANY) for _ in previous]
        + [some(dim)] * 2
        + [fixed((1, dim))]
        + [some(d.shape[1]) for d in d_projs]
        + [fixed(w.shape) for w in weights],
        out_specs=[some(dim), fixed((8, dim))],
        out_shape=[jax.ShapeDtypeStruct(tokens.shape, jnp.float32), jax.ShapeDtypeStruct((8, dim), jnp.float32)],
        input_output_aliases={0: 0} if previous else {},
        compiler_params=params(60),
        cost_estimate=cost(18 * count * dim * dim, 4 * (3 * dim * dim + 6 * count * dim)),
    )(*previous, tokens, d_middle, gain, *d_projs, *weights)


def settle_units_kernel(first, scale_ref, one_ref, two_ref, hidden_ref, return_ref):
    step = pl.program_id(0)

    def put(ref):
        hidden_ref[...] = (ref[:, 0, 0].reshape(BLOCK, -1) * scale_ref[0]).T
        return_ref[...] = ref[:, 1, 0].reshape(BLOCK, -1) * scale_ref[0]

    pl.when(step < first)(lambda: put(one_ref))
    pl.when(step >= first)(lambda: put(two_ref))


def settle_units(scale, one, two):
    first, second, dim = one.shape[2], two.shape[2], one.shape[4]
    units = (first + second) * BLOCK
    block = (16, 2, 1, PIECE, dim)
    return pl.pallas_call(
        functools.partial(settle_units_kernel, first),
        grid=(first + second,),
        in_specs=[
            scalars(),
            pl.BlockSpec(block, lambda i: (0, 0, jnp.minimum(i, first - 1), 0, 0)),
            pl.BlockSpec(block, lambda i: (0, 0, jnp.maximum(i - first, 0), 0, 0)),
        ],
        out_specs=[pl.BlockSpec((dim, BLOCK), lambda i: (0, i)), rows(BLOCK, dim)],
        out_shape=[
            jax.ShapeDtypeStruct((dim, units), jnp.float32),
            jax.ShapeDtypeStruct((units, dim), jnp.float32),
        ],
        compiler_params=params(40),
        cost_estimate=cost(0, 16 * units * dim),
    )(scale, one, two)


def settle_attend_kernel(scale_ref, value_ref, attend_ref, output_ref):
    step = pl.program_id(0)
    size, dim = attend_ref.shape

    @pl.when(step < 3)
    def _():
        attend_ref[...] = value_ref[:, 0].reshape(size, dim) * scale_ref[0]

    @pl.when(step == 3)
    def _():
        output_ref[...] = value_ref[:, 0].reshape(size, dim) * scale_ref[0]


def settle_attend(scale, value):
    piece, dim = value.shape[2:]
    size = 8 * piece
    return pl.pallas_call(
        settle_attend_kernel,
        grid=(4,),
        in_specs=[scalars(), pl.BlockSpec((8, 1, piece, dim), lambda i: (i % 2, i // 2, 0, 0))],
        out_specs=[
            pl.BlockSpec((size, dim), lambda i: (jnp.minimum(i, 2), 0)),
            pl.BlockSpec((size, dim), lambda i: (0, 0)),
        ],
        out_shape=[
            jax.ShapeDtypeStruct((3 * size, dim), jnp.float32),
            jax.ShapeDtypeStruct((size, dim), jnp.float32),
        ],
        compiler_params=params(40),
        cost_estimate=cost(0, 16 * size * dim),
    )(scale, value)


def offset_matrix():
    place = jnp.arange(PATCHES)
    offset = place // SIDE - place % SIDE + SIDE - 1
    return (jnp.arange(STRIP)[:, None] == offset[None, :]).astype(jnp.float32)


def make_strips(table):
    heads = table.shape[0]
    grid = table.reshape(heads, STRIP, STRIP)[:, ::-1]
    wide = jnp.einsum("hmo,op->hmp", grid, offset_matrix(), precision=HIGHEST)
    wide = wide.reshape(heads, STRIP, SIDE, SIDE).transpose(0, 2, 1, 3).reshape(heads, SIDE, STRIP * SIDE)
    return jnp.pad(wide, ((0, 0), (0, 0), (0, 512 - STRIP * SIDE)))


def table_gradient(d_strips):
    heads = d_strips.shape[0]
    wide = d_strips[:, :, : STRIP * SIDE].reshape(heads, SIDE, STRIP, SIDE).transpose(0, 2, 1, 3)
    grid = jnp.einsum("hmp,op->hmo", wide.reshape(heads, STRIP, PATCHES), offset_matrix(), precision=HIGHEST)
    return grid[:, ::-1].reshape(heads, STRIP * STRIP)


def pick(array, index, axis):
    return lax.dynamic_index_in_dim(array, index, axis, keepdims=False)


def join(*values):
    return lax.optimization_barrier(values)


class Ring:
    def __init__(self):
        place = lax.axis_index("dp")
        self.place = place
        self.bits = [place & 1, (place >> 1) & 1, (place >> 2) & 1, (place >> 3) & 1]

    def across(self, value):
        return lax.ppermute(value, "mp", [(0, 1), (1, 0)])

    def along(self, value, bit):
        return lax.ppermute(value, "dp", [(i, i ^ (1 << bit)) for i in range(16)])

    def ordered(self, mine, theirs, bit, axis=0):
        flag = self.bits[bit] == 0
        return jnp.concatenate([jnp.where(flag, mine, theirs), jnp.where(flag, theirs, mine)], axis)

    def core_half(self, weight, base, count):
        half = count // 2
        return lax.dynamic_slice(weight, (base + self.bits[0] * half, 0), (half, weight.shape[1]))

    def share(self, weight, count, first, width):
        part = count // 16
        return lax.dynamic_slice(weight, (self.place * part, first), (part, width))

    def spread(self, part):
        return lax.all_gather(part, "dp", axis=0, tiled=True)

    def rows_step(self, value, bit):
        return self.ordered(value, self.along(value, bit), bit)


class Reduction:
    def __init__(self, ring, axis):
        self.ring = ring
        self.axis = axis
        self.terms = {}
        self.level = {}

    def begin(self, side, keep, send):
        self.terms[side] = [keep, self.ring.along(send, 0)]
        self.level[side] = 1

    def value(self, side):
        out = self.terms[side][0]
        for term in self.terms[side][1:]:
            out = out + term
        return out

    def send(self, side):
        bit = self.ring.bits[self.level[side]]
        kept = []
        out = 0.0
        for term in self.terms[side]:
            shape = term.shape
            axis = self.axis
            cut = term.reshape(shape[:axis] + (shape[axis] // 2, 2) + shape[axis + 1 :])
            kept.append(pick(cut, bit, axis + 1))
            out = out + pick(cut, 1 - bit, axis + 1)
        self.terms[side] = kept
        return out

    def pass_on(self, side, value):
        self.terms[side].append(self.ring.along(value, self.level[side]))
        self.level[side] += 1

    def cross(self, value):
        self.terms["own"].append(self.ring.across(value))

    def gather(self, value):
        return lax.all_gather(value, "dp", axis=self.axis, tiled=True)

    def back(self, value, bit):
        axis = self.axis
        got = self.ring.along(value, bit)
        value, got = (v.reshape(v.shape[: axis + 1] + (1,) + v.shape[axis + 1 :]) for v in (value, got))
        out = self.ring.ordered(value, got, bit, axis + 1)
        return out.reshape(out.shape[:axis] + (-1,) + out.shape[axis + 2 :])


def body(split, *args):
    (
        tokens, cotangent, bucket, counts, first_gain, first_shift, attend_weight, time_weight, time_table,
        bias_table, output_weight, output_bias, second_gain, second_shift, hidden_weight, hidden_bias,
        return_weight, return_bias,
    ) = args
    own_images, patches, dim = tokens.shape
    images = bucket.shape[0]
    buckets = time_table.shape[0]
    heads_local = bias_table.shape[0]
    width = attend_weight.shape[2]
    units = hidden_bias.shape[0]
    group = lax.axis_index("dp")
    rank = lax.axis_index("mp")
    first_own = rank * own_images
    live = (first_own + jnp.arange(own_images) < counts[group]).astype(jnp.float32)
    inv_total = 1.0 / jnp.sum(counts).astype(jnp.float32)
    core = (group & 1).reshape(1)

    def row(vector):
        return vector.reshape(1, -1)

    def column(vector):
        return vector.reshape(-1, 1)

    tokens2 = tokens.reshape(own_images * patches, dim)
    cotangent2 = cotangent.reshape(own_images * patches, dim)
    onehot = (bucket[:, None] == jnp.arange(buckets)[None, :]).astype(jnp.float32)
    time_vec = jnp.dot(onehot, time_table, precision=HIGHEST)
    time_proj = jnp.einsum("sd,ced->sce", time_vec, time_weight.transpose(0, 2, 1), precision=HIGH)
    attend_own = attend_weight.transpose(0, 2, 1).reshape(3 * width, dim)
    norm_first = (row(first_gain), row(first_shift))
    norm_second = (row(second_gain), row(second_shift))

    def time_gradient(packed):
        d_time_all = packed[:, :-1].reshape(-1, 3, width)
        onehot_all = packed[:, -1:].astype(jnp.int32) == jnp.arange(buckets)[None, :]
        time_all = jnp.dot(onehot_all.astype(jnp.float32), time_table, precision=HIGHEST)
        grad = jnp.einsum("sce,sd->ced", d_time_all * inv_total, time_all, precision=HIGH)
        return grad.transpose(0, 2, 1)

    def absolute(own, other):
        flag = rank == 0
        return jnp.concatenate([jnp.where(flag, own, other), jnp.where(flag, other, own)], 0)

    def times_of(value):
        return value.reshape(own_images, 1, -1)

    if split:
        ring = Ring()
        less = units // BLOCK // 2
        cuts = [(0, less), (less, units // BLOCK - less)]
        table_other = ring.across(bias_table)
        bias_other = row(ring.across(hidden_bias))
        hidden_shares = [ring.share(hidden_weight, dim, first * BLOCK, blocks * BLOCK) for first, blocks in cuts]
        qk = ring.across(ring.share(attend_own, 2 * width, 0, dim))
        values_half = ring.core_half(attend_own, 2 * width, width)
        qk, table_other, bias_other, values_half, time_proj, strips_own = join(
            qk, table_other, bias_other, values_half, time_proj, make_strips(bias_table)
        )
        attend_qk = ring.spread(qk)
        values_mine = ring.across(values_half)
        hidden_share = ring.across(hidden_shares[0])
        time_mine = lax.dynamic_slice_in_dim(time_proj, first_own, own_images, 0)
        time_theirs = lax.dynamic_slice_in_dim(time_proj, (1 - rank) * own_images, own_images, 0)
        time_other = ring.across(time_theirs)
        own = attend_forward(tokens2, *norm_first, attend_own, times_of(time_mine), strips_own)
        return_halves = [ring.core_half(return_weight, first * BLOCK, blocks * BLOCK) for first, blocks in cuts]
        own, values_mine, time_other, return_half, output_half, hidden_share, share_2 = join(
            own, values_mine, time_other, return_halves[0], ring.core_half(output_weight, 0, width), hidden_share,
            hidden_shares[1],
        )
        output_mine = ring.across(output_half)
        hidden_other = [ring.spread(hidden_share), ring.spread(ring.across(share_2))]
        strips_other = make_strips(table_other)
        values_full = ring.ordered(values_mine, ring.along(values_mine, 0), 0)
        attend_other = jnp.concatenate([attend_qk, values_full], 0)
        return_mine = ring.across(return_half)
        other = attend_forward(tokens2, *norm_first, attend_other, times_of(time_other), strips_other)
        attend = [attend_own, attend_other]
        other, return_mine, output_mine = join(other, return_mine, output_mine)
        output_other = ring.ordered(output_mine, ring.along(output_mine, 0), 0)
        return_theirs = ring.along(return_mine, 0)
        output = [output_weight, output_other]
        middle, *forms = output_forward(
            live, tokens2, cotangent2, [own[3], other[3]], output, row(output_bias), *norm_second
        )
        forms, return_theirs, return_half = join(forms, return_theirs, return_halves[1])
        return_1 = ring.ordered(return_mine, return_theirs, 0)
        return_mine = ring.across(return_half)

        def feed_other(forms, index, hidden, back):
            first, blocks = cuts[index]
            bias = bias_other[:, first * BLOCK : (first + blocks) * BLOCK]
            return feed(True, core, forms, hidden, bias, back, 0, blocks)

        def feed_own(forms, index):
            return feed(True, core, forms, hidden_weight, row(hidden_bias), return_weight, *cuts[index])

        h1, h2, r1, r2, qa, qb = (Reduction(ring, axis) for axis in (1, 1, 1, 1, 0, 0))
        other_1 = feed_other(forms, 0, hidden_other[0], return_1)
        forms, other_1, return_mine = join(forms, other_1, return_mine)
        return_2 = ring.ordered(return_mine, ring.along(return_mine, 0), 0)
        forms, return_2, sent = join(forms, return_2, other_1[3:7])
        h1.begin("other", *sent[:2])
        r1.begin("other", *sent[2:])
        other_2 = feed_other(forms, 1, hidden_other[1], return_2)
        forms, other_2, a, b = join(forms, other_2, h1.value("other"), r1.send("other"))
        h1_cross, r1_y = a, b
        h2.begin("other", *other_2[3:5])
        r2.begin("other", *other_2[5:7])
        h1_crossed = ring.across(h1_cross)
        r1.pass_on("other", r1_y)
        own_1 = feed_own(forms, 0)
        forms, own_1, a, b, h1_crossed, r1.terms["other"] = join(
            forms, own_1, h2.value("other"), r2.send("other"), h1_crossed, r1.terms["other"]
        )
        h1.begin("own", *own_1[3:5])
        r1.begin("own", *own_1[5:7])
        h1.terms["own"].append(h1_crossed)
        h2_crossed = ring.across(a)
        r2.pass_on("other", b)
        own_2 = feed_own(forms, 1)
        middle, own_2, a, b, h2_crossed = join(middle, own_2, r1.send("own"), r1.value("other"), h2_crossed)
        h2.begin("own", *own_2[3:5])
        r2.begin("own", *own_2[5:7])
        h2.terms["own"].append(h2_crossed)
        r1.pass_on("own", a)
        r1.cross(b)
        fed = [other_1, own_1, other_2, own_2]
        result, d_middle, second_sums, d_mixed_own, d_mixed_other = middle_backward(
            live, middle, cotangent2, row(second_gain), row(return_bias), [f[0] for f in fed], [f[1] for f in fed], output
        )
        d_mixed_other, a, b, c = join(d_mixed_other, h1.send("own"), r2.value("other"), r1.send("own"))
        h1.pass_on("own", a)
        r2_crossed = ring.across(b)
        r1.pass_on("own", c)
        attended_other = attend_backward(*other[:4], d_mixed_other, other[5], strips_other)
        attended_other, a, b, c, r2_crossed = join(
            attended_other, h1.send("own"), r1.send("own"), h2.send("own"), r2_crossed
        )
        h1.pass_on("own", a)
        r1.pass_on("own", b)
        h2.pass_on("own", c)

        def pair_up(first, second):
            return jnp.stack([first, second]).reshape(1, -1, dim)

        def weights_a(attended, normed):
            return attend_weights(True, core, [attended[1]], [normed], [0], [2])

        def weights_b(attended, normed, flipped_mixed):
            return attend_weights(True, core, [attended[1], flipped_mixed], [normed, d_middle], [2, 0], [1, 1])

        normed_first = own[6]
        part = weights_a(attended_other, normed_first)
        part, normed_first = join(part, normed_first)
        qa.begin("other", *part)
        part = weights_b(attended_other, normed_first, other[4])
        part, d_mixed_own, a, b, c, d, e = join(
            part, d_mixed_own, qa.value("other"), h1.send("own"), r2.send("own"), h2.send("own"), r1.value("own")
        )
        qb.begin("other", *part)
        qa_first = ring.across(a[:4])
        h1.pass_on("own", b)
        r2.pass_on("own", c)
        r2.terms["own"].append(r2_crossed)
        h2.pass_on("own", d)
        return_1 = e
        attended_own = attend_backward(*own[:4], d_mixed_own, own[5], strips_own)
        attended_own, a, b, c, d, e, qa_first = join(
            attended_own, qb.send("other"), pair_up(h1.value("own"), return_1), r2.send("own"), h2.send("own"), a[4:],
            qa_first,
        )
        qb.pass_on("other", a)
        units_1 = ring.spread(b)
        r2.pass_on("own", c)
        h2.pass_on("own", d)
        qa_second = ring.across(e)
        d_time_got = ring.across(attended_other[3].reshape(own_images, 3, width))
        part = weights_b(attended_own, normed_first, own[4])
        part, normed_first, d_time_got = join(part, normed_first, d_time_got)
        d_time = absolute(attended_own[3].reshape(own_images, 3, width), d_time_got)
        packed = jnp.concatenate([d_time.reshape(images, -1), bucket.astype(jnp.float32)[:, None]], 1)
        packed = ring.rows_step(packed, 0)
        qb.begin("own", *part)
        part = weights_a(attended_own, normed_first)
        part, d_projs, a, b, c, qa_second, packed = join(
            part, [attended_own[0], attended_other[0]], qb.send("own"), qb.value("other"), r2.send("own"),
            qa_second, packed,
        )
        qa.begin("own", *part)
        qa.terms["own"].append(jnp.concatenate([qa_first, qa_second], 0))
        qb.pass_on("own", a)
        qb.cross(b)
        r2.pass_on("own", c)
        packed = ring.rows_step(packed, 1)
        half = own_images // 2
        tokens_a, sums_a = first_backward(tokens2, d_middle, row(first_gain), d_projs, attend, 0, half)
        tokens_a, d_projs, a, b, c, packed = join(
            tokens_a, d_projs, qa.send("own"), qb.send("own"), pair_up(h2.value("own"), r2.value("own")), packed
        )
        qa.pass_on("own", a)
        qb.pass_on("own", b)
        units_2 = ring.spread(c)
        packed = ring.rows_step(packed, 2)
        tokens_grad, sums_b = first_backward(
            tokens2, d_middle, row(first_gain), d_projs, attend, half, own_images - half, (tokens_a,)
        )
        tokens_grad, sums_b, a, b, packed, strips_a, strips_b, d_time = join(
            tokens_grad, sums_b, qa.send("own"), qb.send("own"), packed, attended_own[2], attended_other[2], d_time
        )
        qa.pass_on("own", a)
        qb.pass_on("own", b)
        packed = ring.rows_step(packed, 3)
        d_time_vec = jnp.einsum("sce,ced->sd", d_time, time_weight.transpose(0, 2, 1), precision=HIGH)
        time_table_part = jnp.dot(onehot.T, d_time_vec, precision=HIGHEST)
        table_full = absolute(table_gradient(strips_a), table_gradient(strips_b))
        bias_own = jnp.concatenate([own_1[2][0], own_2[2][0]])
        hidden_bias_full = absolute(bias_own, jnp.concatenate([other_1[2][0], other_2[2][0]]))
        first_sums = sums_a + sums_b
        small = [
            first_sums[0], first_sums[1], time_table_part, second_sums[2], second_sums[0], second_sums[1],
            second_sums[3], table_full, hidden_bias_full,
        ]
        flat = jnp.concatenate([v.reshape(-1) for v in small]) * inv_total
        flat = jnp.pad(flat, (0, -flat.shape[0] % 1024)).reshape(-1, 128)
        a, packed, flat = join(qa.send("own"), packed, flat)
        qa.pass_on("own", a)
        flat = flat + ring.along(flat, 0)
        time_weight_grad = time_gradient(packed)
        last = jnp.stack([qa.value("own"), qb.value("own")]).reshape(1, -1, dim)
        last, flat, time_weight_grad, units_1, units_2 = join(last, flat, time_weight_grad, units_1, units_2)
        attend_all = ring.spread(last).reshape(16, 2, -1, dim)
        flat = flat + ring.across(flat)
        scale = inv_total.reshape(1)
        hidden_grad, return_grad = settle_units(
            scale, *(g.reshape(16, 2, -1, PIECE, dim) for g in (units_1, units_2))
        )
        flat, hidden_grad, return_grad = join(flat, hidden_grad, return_grad)
        for bit in (1, 2, 3):
            flat = flat + ring.along(flat, bit)
        attend_weight_grad, output_weight_grad = settle_attend(scale, attend_all)
        attend_weight_grad = attend_weight_grad.reshape(3, width, dim).transpose(0, 2, 1)
    else:
        attend = [lax.all_gather(attend_weight, "mp", axis=2, tiled=True).transpose(0, 2, 1).reshape(-1, dim)]
        output = [lax.all_gather(output_weight, "mp", axis=0, tiled=True)]
        hidden_full = lax.all_gather(hidden_weight, "mp", axis=1, tiled=True)
        return_full = lax.all_gather(return_weight, "mp", axis=0, tiled=True)
        bias_full = lax.all_gather(hidden_bias, "mp", axis=0, tiled=True)
        strips = make_strips(lax.all_gather(bias_table, "mp", axis=0, tiled=True))
        full = lax.all_gather(time_proj, "mp", axis=2, tiled=True)
        times = times_of(lax.dynamic_slice_in_dim(full, first_own, own_images, 0))
        all_of = attend_forward(tokens2, *norm_first, attend[0], times, strips)
        middle, *forms = output_forward(
            live, tokens2, cotangent2, [all_of[3]], output, row(output_bias), *norm_second
        )
        fed = feed(False, core, forms, hidden_full, row(bias_full), return_full, 0, hidden_full.shape[1] // BLOCK)
        result, d_middle, second_sums, d_mixed = middle_backward(
            live, middle, cotangent2, row(second_gain), row(return_bias), [fed[0]], [fed[1]], output
        )
        attended = attend_backward(*all_of[:4], d_mixed, all_of[5], strips)
        (attend_full,) = attend_weights(
            False, core, [attended[1]], [all_of[6]], [0], [attended[1].shape[0] // STEP]
        )
        (output_full,) = attend_weights(False, core, [all_of[4]], [d_middle], [0], [dim // STEP])
        tokens_grad, first_sums = first_backward(
            tokens2, d_middle, row(first_gain), [attended[0]], attend, 0, own_images
        )

        def settle(value, axis):
            return lax.psum(lax.psum_scatter(value * inv_total, "mp", scatter_dimension=axis, tiled=True), "dp")

        hidden_grad = settle(fed[3], 0).T
        return_grad = settle(fed[4], 0)
        attend_weight_grad = settle(attend_full.reshape(3, -1, dim), 1).transpose(0, 2, 1)
        output_weight_grad = settle(output_full, 0)
        table_full = table_gradient(attended[2])
        hidden_bias_full = fed[2][0]
        d_time = lax.all_gather(attended[3].reshape(own_images, 3, -1), "mp", axis=0, tiled=True)
        d_time = lax.dynamic_slice_in_dim(d_time, rank * width, width, 2)

        packed = jnp.concatenate([d_time.reshape(images, -1), bucket.astype(jnp.float32)[:, None]], 1)
        time_weight_grad = time_gradient(lax.all_gather(packed, "dp", axis=0, tiled=True))
        d_time_vec = jnp.einsum("sce,ced->sd", d_time, time_weight.transpose(0, 2, 1), precision=HIGH)
        time_table_part = jnp.dot(onehot.T, d_time_vec, precision=HIGHEST)
        small = [
            first_sums[0], first_sums[1], time_table_part, second_sums[2], second_sums[0], second_sums[1],
            second_sums[3], table_full, hidden_bias_full,
        ]
        flat = lax.psum(jnp.concatenate([v.reshape(-1) for v in small]) * inv_total, ("dp", "mp"))

    flat = flat.reshape(-1)
    sums = []
    start = 0
    for s in small:
        sums.append(flat[start : start + s.size].reshape(s.shape))
        start += s.size
    bias_table_grad = lax.dynamic_slice_in_dim(sums[7], rank * heads_local, heads_local, 0)
    hidden_bias_grad = lax.dynamic_slice_in_dim(sums[8], rank * units, units, 0)
    return (
        result.reshape(tokens.shape),
        tokens_grad.reshape(tokens.shape),
        sums[0],
        sums[1],
        attend_weight_grad,
        time_weight_grad,
        sums[2],
        bias_table_grad,
        output_weight_grad,
        sums[3],
        sums[4],
        sums[5],
        hidden_grad,
        hidden_bias_grad,
        return_grad,
        sums[6],
    )


def solution(mesh):
    in_specs = (
        P(("dp", "mp"), None, None),
        P(("dp", "mp"), None, None),
        P("dp"),
        P(),
        P(),
        P(),
        P(None, None, "mp"),
        P(None, None, "mp"),
        P(),
        P("mp", None),
        P("mp", None),
        P(),
        P(),
        P(),
        P(None, "mp"),
        P("mp"),
        P("mp", None),
        P(),
    )
    out_specs = (
        P(("dp", "mp"), None, None),
        P(("dp", "mp"), None, None),
        P(),
        P(),
        P(None, None, "mp"),
        P(None, None, "mp"),
        P(),
        P("mp", None),
        P("mp", None),
        P(),
        P(),
        P(),
        P(None, "mp"),
        P("mp"),
        P("mp", None),
        P(),
    )
    split = mesh.shape["dp"] == 16 and mesh.shape["mp"] == 2
    return jax.shard_map(
        functools.partial(body, split), mesh=mesh, in_specs=in_specs, out_specs=out_specs, check_vma=False
    )
```

```python
import functools
import math

import jax
import jax.numpy as jnp
from jax import lax
from jax.experimental import pallas as pl
from jax.experimental.pallas import tpu as pltpu
from jax.sharding import PartitionSpec as P

HEAD_DIM = 72
SIDE = 16
PATCHES = SIDE * SIDE
STRIP = 2 * SIDE - 1
EPS = 1e-05
SCALE = HEAD_DIM ** (-0.5)
MIB = 1024 * 1024
HIGHEST = lax.Precision.HIGHEST
HIGH = lax.Precision.HIGH


def dot_nn(a, b):
    return lax.dot_general(a, b, (((1,), (0,)), ((), ())), precision=HIGH, preferred_element_type=jnp.float32)


def dot_nt(a, b):
    return lax.dot_general(a, b, (((1,), (1,)), ((), ())), precision=HIGH, preferred_element_type=jnp.float32)


def dot_tn(a, b):
    return lax.dot_general(a, b, (((0,), (0,)), ((), ())), precision=HIGH, preferred_element_type=jnp.float32)


def standardize(values):
    centre = values - jnp.mean(values, -1, keepdims=True)
    inverse = lax.rsqrt(jnp.mean(centre * centre, -1, keepdims=True) + EPS)
    return centre * inverse, inverse


def norm_back(grad_hat, scaled, inverse):
    return inverse * (
        grad_hat
        - jnp.mean(grad_hat, -1, keepdims=True)
        - scaled * jnp.mean(grad_hat * scaled, -1, keepdims=True)
    )


def head_window(head, width):
    first = head * HEAD_DIM
    start = first // 128 * 128
    stop = min(-(-(first + HEAD_DIM) // 128) * 128, width)
    return start, stop, first - start


def head_mask(head, width):
    start, stop, offset = head_window(head, width)
    lane = lax.broadcasted_iota(jnp.int32, (1, stop - start), 1)
    return (lane >= offset) & (lane < offset + HEAD_DIM)


def fixed(shape, **kw):
    return pl.BlockSpec(shape, lambda i: (0,) * len(shape), pipeline_mode=pl.Buffered(1), **kw)


def rows(count, width):
    return pl.BlockSpec((count, width), lambda i: (i, 0))


def params(limit):
    return pltpu.CompilerParams(dimension_semantics=("arbitrary",), vmem_limit_bytes=limit * MIB)


def cost(flops, nbytes, trans=0):
    return pl.CostEstimate(flops=int(flops) // 1000, bytes_accessed=int(nbytes) // 1000, transcendentals=0)


def halves(value):
    high = value.astype(jnp.bfloat16)
    return high, (value - high.astype(jnp.float32)).astype(jnp.bfloat16)


def mul(a, b, left, right):
    return lax.dot_general(a, b, (((left,), (right,)), ((), ())), preferred_element_type=jnp.float32)


def scalars():
    return pl.BlockSpec(memory_space=pltpu.SMEM)


def build_bias(strip_ref, bias_ref, heads):
    def one(head, carry):
        strip = strip_ref[head]
        for row in range(SIDE):
            shift = (SIDE - 1 - row) * SIDE
            bias_ref[head, row * SIDE : (row + 1) * SIDE, :] = strip[:, shift : shift + PATCHES]
        return carry

    lax.fori_loop(0, heads, one, 0)


def attend_forward_kernel(
    heads, tokens_ref, gain_ref, shift_ref, weight_ref, time_ref, strip_ref,
    query_ref, keys_ref, values_ref, mixed_ref, flipped_ref, lse_ref, normed_ref, bias_ref,
):
    width = query_ref.shape[1]

    @pl.when(pl.program_id(0) == 0)
    def _():
        build_bias(strip_ref, bias_ref, heads)

    scaled, _ = standardize(tokens_ref[...])
    normed = scaled * gain_ref[...] + shift_ref[...]
    normed_ref[...] = normed
    proj = dot_nt(normed, weight_ref[...]) + time_ref[0]
    query_ref[...] = proj[:, :width] * SCALE
    keys_ref[...] = proj[:, width : 2 * width]
    values_ref[...] = proj[:, 2 * width :]
    mixed_ref[...] = jnp.zeros_like(mixed_ref)
    columns = lax.broadcasted_iota(jnp.int32, (1, heads), 1)
    stats = jnp.zeros((PATCHES, heads), jnp.float32)
    for head in range(heads):
        start, stop, _ = head_window(head, width)
        mask = head_mask(head, width)
        query = jnp.where(mask, query_ref[:, start:stop], 0.0)
        scores = dot_nt(query, keys_ref[:, start:stop]) + bias_ref[head]
        peak = jnp.max(scores, -1, keepdims=True)
        weights = jnp.exp(scores - peak)
        total = jnp.sum(weights, -1, keepdims=True)
        values = jnp.where(mask, values_ref[:, start:stop], 0.0)
        mixed_ref[:, start:stop] += dot_nn(weights, values) * (1.0 / total)
        stats = jnp.where(columns == head, peak + jnp.log(total), stats)
    lse_ref[...] = stats
    flipped_ref[...] = mixed_ref[...].T


def attend_forward(tokens, gain, shift, weight, time_proj, strips):
    count, dim = tokens.shape
    heads = strips.shape[0]
    width = weight.shape[0] // 3
    images = count // PATCHES
    piece = jax.ShapeDtypeStruct((count, width), jnp.float32)
    return pl.pallas_call(
        functools.partial(attend_forward_kernel, heads),
        grid=(images,),
        in_specs=[
            rows(PATCHES, dim),
            fixed((1, dim)),
            fixed((1, dim)),
            fixed((3 * width, dim)),
            pl.BlockSpec((1, 1, 3 * width), lambda i: (i, 0, 0)),
            fixed(strips.shape),
        ],
        out_specs=[rows(PATCHES, width)] * 4
        + [pl.BlockSpec((width, PATCHES), lambda i: (0, i)), rows(PATCHES, heads), rows(PATCHES, dim)],
        out_shape=[piece] * 4
        + [
            jax.ShapeDtypeStruct((width, count), jnp.float32),
            jax.ShapeDtypeStruct((count, heads), jnp.float32),
            jax.ShapeDtypeStruct((count, dim), jnp.float32),
        ],
        scratch_shapes=[pltpu.VMEM((heads, PATCHES, PATCHES), jnp.float32)],
        compiler_params=params(56),
        cost_estimate=cost(6 * count * dim * width * 3 + 24 * count * PATCHES * 256 * heads // 2, 4 * (weight.size + 6 * count * width)),
    )(tokens, gain, shift, weight, time_proj, strips)


def output_kernel(parts, *refs):
    live_ref, tokens_ref, cotangent_ref = refs[:3]
    mixed_refs = refs[3 : 3 + parts]
    weight_refs = refs[3 + parts : 3 + 2 * parts]
    bias_ref, gain_ref, shift_ref, middle_ref, pair_ref, grad_ref = refs[3 + 2 * parts :]
    dim = tokens_ref.shape[1]
    middle = tokens_ref[...] + bias_ref[...]
    for mixed_ref, weight_ref in zip(mixed_refs, weight_refs):
        middle = middle + dot_nn(mixed_ref[...], weight_ref[...])
    middle_ref[...] = middle
    scaled, _ = standardize(middle)
    normed = scaled * gain_ref[...] + shift_ref[...]
    pair_ref[:, :dim], pair_ref[:, dim:] = halves(normed)
    grad = cotangent_ref[...] * live_ref[pl.program_id(0)]
    grad_ref[:, :dim], grad_ref[:, dim:] = halves(grad)


def output_forward(live, tokens, cotangent, mixed, weights, bias, gain, shift):
    count, dim = tokens.shape
    parts = len(mixed)
    pair = jax.ShapeDtypeStruct((count, 2 * dim), jnp.bfloat16)
    return pl.pallas_call(
        functools.partial(output_kernel, parts),
        grid=(count // PATCHES,),
        in_specs=[scalars()]
        + [rows(PATCHES, dim)] * 2
        + [rows(PATCHES, m.shape[1]) for m in mixed]
        + [fixed(w.shape) for w in weights]
        + [fixed((1, dim))] * 3,
        out_specs=[
            rows(PATCHES, dim),
            rows(PATCHES, 2 * dim),
            rows(PATCHES, 2 * dim),
        ],
        out_shape=[
            jax.ShapeDtypeStruct((count, dim), jnp.float32),
            pair,
            pair,
        ],
        compiler_params=params(48),
        cost_estimate=cost(6 * count * dim * dim, 4 * (dim * dim + 5 * count * dim)),
    )(live, tokens, cotangent, *mixed, *weights, bias, gain, shift)


BLOCK = 256
PIECE = BLOCK // 16


def feed_kernel(split, core_ref, pair_ref, grad_ref, hidden_ref, bias_ref, return_ref, *refs):
    result_ref, second_ref, d_bias_ref = refs[:3]
    outs = refs[3:-5]
    hidden3_ref, return3_ref, active3_ref, slope3_ref, block_ref = refs[-5:]
    count = pair_ref.shape[0]
    dim = pair_ref.shape[1] // 2
    chunk = min(512, count)

    @pl.when(pl.program_id(0) == 0)
    def _():
        result_ref[...] = jnp.zeros_like(result_ref)
        second_ref[...] = jnp.zeros_like(second_ref)

    d_bias_ref[...] = jnp.zeros_like(d_bias_ref)
    high, low = halves(hidden_ref[...])
    hidden3_ref[:, :BLOCK] = high
    hidden3_ref[:, BLOCK : 2 * BLOCK] = high
    hidden3_ref[:, 2 * BLOCK :] = low
    high, low = halves(return_ref[...])
    return3_ref[:BLOCK] = high
    return3_ref[BLOCK : 2 * BLOCK] = high
    return3_ref[2 * BLOCK :] = low

    for begin in range(0, count, chunk):
        part = slice(begin, begin + chunk)
        hidden = (
            mul(pair_ref[part, :dim], hidden3_ref[:, :BLOCK], 1, 0)
            + mul(pair_ref[part, dim:], hidden3_ref[:, :BLOCK], 1, 0)
            + mul(pair_ref[part, :dim], hidden3_ref[:, 2 * BLOCK :], 1, 0)
            + bias_ref[...]
        )
        d_active = (
            mul(grad_ref[part, :dim], return3_ref[:BLOCK], 1, 1)
            + mul(grad_ref[part, dim:], return3_ref[:BLOCK], 1, 1)
            + mul(grad_ref[part, :dim], return3_ref[2 * BLOCK :], 1, 1)
        )
        cumul = 0.5 * (1.0 + lax.erf(hidden * 2.0 ** (-0.5)))
        high, low = halves(hidden * cumul)
        active3_ref[part, :BLOCK] = high
        active3_ref[part, BLOCK : 2 * BLOCK] = low
        active3_ref[part, 2 * BLOCK :] = high
        density = hidden * jnp.exp(-0.5 * hidden * hidden) * (1.0 / math.sqrt(2.0 * math.pi))
        d_hidden = d_active * (cumul + density)
        high, low = halves(d_hidden)
        slope3_ref[part, :BLOCK] = high
        slope3_ref[part, BLOCK : 2 * BLOCK] = low
        slope3_ref[part, 2 * BLOCK :] = high
        d_bias_ref[...] += jnp.sum(d_hidden, 0, keepdims=True)
        result_ref[part, :] += mul(active3_ref[part, :], return3_ref[...], 1, 0)
        second_ref[part, :] += mul(slope3_ref[part, :], hidden3_ref[...], 1, 1)

    def weight_grad(left_ref, right_ref):
        wide = mul(left_ref[:, :BLOCK], right_ref[...], 0, 0)
        return wide[:, :dim] + wide[:, dim:] + mul(left_ref[:, BLOCK : 2 * BLOCK], right_ref[:, :dim], 0, 0)

    if split:
        block_ref[0] = weight_grad(active3_ref, grad_ref)
        block_ref[1] = weight_grad(slope3_ref, pair_ref)

        def place(index, even_ref, odd_ref):
            for pair in range(8):
                even_ref[0, pair] = block_ref[index, 2 * pair * PIECE : (2 * pair + 1) * PIECE]
                odd_ref[0, pair] = block_ref[index, (2 * pair + 1) * PIECE : (2 * pair + 2) * PIECE]

        @pl.when(core_ref[0] == 0)
        def _():
            place(0, outs[2], outs[3])
            place(1, outs[0], outs[1])

        @pl.when(core_ref[0] == 1)
        def _():
            place(0, outs[3], outs[2])
            place(1, outs[1], outs[0])
    else:
        outs[1][...] = weight_grad(active3_ref, grad_ref)
        outs[0][...] = weight_grad(slope3_ref, pair_ref)


def feed(split, core, tokens_forms, hidden_weight, hidden_bias, return_weight, first, blocks):
    pair, grad = tokens_forms
    count = pair.shape[0]
    dim = pair.shape[1] // 2
    units = blocks * BLOCK
    whole = jax.ShapeDtypeStruct((count, dim), jnp.float32)
    if split:
        out_specs = [pl.BlockSpec((1, 8, PIECE, dim), lambda i: (i, 0, 0, 0))] * 4
        out_shape = [jax.ShapeDtypeStruct((blocks, 8, PIECE, dim), jnp.float32)] * 4
    else:
        out_specs = [rows(BLOCK, dim)] * 2
        out_shape = [jax.ShapeDtypeStruct((units, dim), jnp.float32)] * 2
    return pl.pallas_call(
        functools.partial(feed_kernel, split),
        grid=(blocks,),
        in_specs=[
            scalars(),
            fixed(pair.shape),
            fixed(grad.shape),
            pl.BlockSpec((dim, BLOCK), lambda i: (0, first + i)),
            pl.BlockSpec((1, BLOCK), lambda i: (0, first + i)),
            pl.BlockSpec((BLOCK, dim), lambda i: (first + i, 0)),
        ],
        out_specs=[fixed((count, dim)), fixed((count, dim)), pl.BlockSpec((1, BLOCK), lambda i: (0, i))] + out_specs,
        out_shape=[whole, whole, jax.ShapeDtypeStruct((1, units), jnp.float32)] + out_shape,
        scratch_shapes=[
            pltpu.VMEM((dim, 3 * BLOCK), jnp.bfloat16),
            pltpu.VMEM((3 * BLOCK, dim), jnp.bfloat16),
            pltpu.VMEM((count, 3 * BLOCK), jnp.bfloat16),
            pltpu.VMEM((count, 3 * BLOCK), jnp.bfloat16),
            pltpu.VMEM((2, BLOCK, dim), jnp.float32),
        ],
        compiler_params=params(60),
        cost_estimate=cost(36 * count * dim * units, 4 * (4 * dim * units + 5 * count * dim), 2 * count * units),
    )(core, pair, grad, hidden_weight, hidden_bias, return_weight)


def middle_kernel(parts, feeds, *refs):
    live_ref, middle_ref, cotangent_ref, gain_ref, bias_ref = refs[:5]
    result_parts = refs[5 : 5 + feeds]
    second_parts = refs[5 + feeds : 5 + 2 * feeds]
    weight_refs = refs[5 + 2 * feeds : 5 + 2 * feeds + parts]
    result_ref, d_middle_ref, sums_ref = refs[5 + 2 * feeds + parts : 8 + 2 * feeds + parts]
    mix_refs = refs[8 + 2 * feeds + parts :]
    middle = middle_ref[...]
    grad = cotangent_ref[...] * live_ref[pl.program_id(0)]
    result = middle + bias_ref[...]
    second = second_parts[0][...]
    for part in result_parts:
        result = result + part[...]
    for part in second_parts[1:]:
        second = second + part[...]
    result_ref[...] = result
    scaled, inverse = standardize(middle)
    d_middle = grad + norm_back(second * gain_ref[...], scaled, inverse)
    d_middle_ref[...] = d_middle

    @pl.when(pl.program_id(0) == 0)
    def _():
        sums_ref[...] = jnp.zeros_like(sums_ref)

    sums_ref[0:1, :] += jnp.sum(second * scaled, 0, keepdims=True)
    sums_ref[1:2, :] += jnp.sum(second, 0, keepdims=True)
    sums_ref[2:3, :] += jnp.sum(d_middle, 0, keepdims=True)
    sums_ref[3:4, :] += jnp.sum(grad, 0, keepdims=True)
    for weight_ref, mix_ref in zip(weight_refs, mix_refs):
        mix_ref[...] = dot_nt(d_middle, weight_ref[...])


def middle_backward(live, middle, cotangent, gain, bias, results, seconds, weights):
    count, dim = middle.shape
    parts = len(weights)
    block = jax.ShapeDtypeStruct((count, dim), jnp.float32)
    return pl.pallas_call(
        functools.partial(middle_kernel, parts, len(results)),
        grid=(count // PATCHES,),
        in_specs=[scalars()]
        + [rows(PATCHES, dim)] * 2
        + [fixed((1, dim))] * 2
        + [rows(PATCHES, dim)] * (2 * len(results))
        + [fixed(w.shape) for w in weights],
        out_specs=[rows(PATCHES, dim)] * 2 + [fixed((8, dim))] + [rows(PATCHES, w.shape[0]) for w in weights],
        out_shape=[block, block, jax.ShapeDtypeStruct((8, dim), jnp.float32)]
        + [jax.ShapeDtypeStruct((count, w.shape[0]), jnp.float32) for w in weights],
        compiler_params=params(60),
        cost_estimate=cost(6 * count * dim * dim, 4 * (dim * dim + 9 * count * dim)),
    )(live, middle, cotangent, gain, bias, *results, *seconds, *weights)


def attend_backward_kernel(
    heads, query_ref, keys_ref, values_ref, mixed_ref, grad_ref, lse_ref, strip_ref,
    d_proj_ref, flipped_ref, d_strip_ref, d_time_ref, bias_ref, total_ref, d_query_ref, d_keys_ref, d_values_ref,
):
    width = query_ref.shape[1]
    image = pl.program_id(0)

    @pl.when(image == 0)
    def _():
        build_bias(strip_ref, bias_ref, heads)
        total_ref[...] = jnp.zeros_like(total_ref)

    d_query_ref[...] = jnp.zeros_like(d_query_ref)
    d_keys_ref[...] = jnp.zeros_like(d_keys_ref)
    d_values_ref[...] = jnp.zeros_like(d_values_ref)
    for head in range(heads):
        start, stop, _ = head_window(head, width)
        mask = head_mask(head, width)
        query = jnp.where(mask, query_ref[:, start:stop], 0.0)
        keys = jnp.where(mask, keys_ref[:, start:stop], 0.0)
        grad = jnp.where(mask, grad_ref[:, start:stop], 0.0)
        scores = dot_nt(query, keys) + bias_ref[head]
        prob = jnp.exp(scores - lse_ref[:, head : head + 1])
        d_prob = dot_nt(grad, values_ref[:, start:stop])
        delta = jnp.sum(grad * mixed_ref[:, start:stop], -1, keepdims=True)
        d_scores = prob * (d_prob - delta)
        total_ref[head] += d_scores
        d_values_ref[:, start:stop] += dot_tn(prob, grad)
        d_query_ref[:, start:stop] += dot_nn(d_scores, keys)
        d_keys_ref[:, start:stop] += dot_tn(d_scores, query)
    d_proj_ref[:, :width] = d_query_ref[...] * SCALE
    d_proj_ref[:, width : 2 * width] = d_keys_ref[...]
    d_proj_ref[:, 2 * width :] = d_values_ref[...]
    d_time_ref[0] = jnp.sum(d_proj_ref[...], 0, keepdims=True)
    flipped_ref[:width] = (d_query_ref[...] * SCALE).T
    flipped_ref[width : 2 * width] = d_keys_ref[...].T
    flipped_ref[2 * width :] = d_values_ref[...].T

    @pl.when(image == pl.num_programs(0) - 1)
    def _():
        d_strip_ref[...] = jnp.zeros_like(d_strip_ref)

        def one(head, carry):
            for row in range(SIDE):
                shift = (SIDE - 1 - row) * SIDE
                d_strip_ref[head, :, shift : shift + PATCHES] += total_ref[head, row * SIDE : (row + 1) * SIDE, :]
            return carry

        lax.fori_loop(0, heads, one, 0)


def attend_backward(query, keys, values, mixed, grad, lse, strips):
    count, width = query.shape
    heads = strips.shape[0]
    images = count // PATCHES
    return pl.pallas_call(
        functools.partial(attend_backward_kernel, heads),
        grid=(images,),
        in_specs=[rows(PATCHES, width)] * 5 + [rows(PATCHES, heads), fixed(strips.shape)],
        out_specs=[
            rows(PATCHES, 3 * width),
            pl.BlockSpec((3 * width, PATCHES), lambda i: (0, i)),
            fixed(strips.shape),
            pl.BlockSpec((1, 1, 3 * width), lambda i: (i, 0, 0)),
        ],
        out_shape=[
            jax.ShapeDtypeStruct((count, 3 * width), jnp.float32),
            jax.ShapeDtypeStruct((3 * width, count), jnp.float32),
            jax.ShapeDtypeStruct(strips.shape, jnp.float32),
            jax.ShapeDtypeStruct((images, 1, 3 * width), jnp.float32),
        ],
        scratch_shapes=[pltpu.VMEM((heads, PATCHES, PATCHES), jnp.float32)] * 2
        + [pltpu.VMEM((PATCHES, width), jnp.float32)] * 3,
        compiler_params=params(56),
        cost_estimate=cost(30 * count * PATCHES * 256 * heads, 4 * 9 * count * width),
    )(query, keys, values, mixed, grad, lse, strips)


STEP = 576


def attend_weights_kernel(split, steps, core_ref, *refs):
    lefts, rights = refs[: len(steps)], refs[len(steps) : 2 * len(steps)]
    outs = refs[2 * len(steps) :]
    step = pl.program_id(0)
    piece = STEP // 8
    begin = 0
    for left_ref, right_ref, count in zip(lefts, rights, steps):

        @pl.when((step >= begin) & (step < begin + count))
        def _(left_ref=left_ref, right_ref=right_ref):
            value = dot_nn(left_ref[...], right_ref[...])
            if split:

                def store(even_ref, odd_ref):
                    for pair in range(4):
                        even_ref[pair] = value[2 * pair * piece : (2 * pair + 1) * piece]
                        odd_ref[pair] = value[(2 * pair + 1) * piece : (2 * pair + 2) * piece]

                pl.when(core_ref[0] == 0)(lambda: store(outs[0], outs[1]))
                pl.when(core_ref[0] == 1)(lambda: store(outs[1], outs[0]))
            else:
                outs[0][...] = value

        begin += count


def attend_weights(split, core, lefts, rights, firsts, steps):
    count, dim = rights[0].shape
    total = sum(steps)
    starts = [sum(steps[:i]) for i in range(len(steps))]

    def left_spec(start, first, size):
        return pl.BlockSpec((STEP, count), lambda i: (first + jnp.clip(i - start, 0, size - 1), 0))

    if split:
        out_specs = [pl.BlockSpec((4, STEP // 8, dim), lambda i: (i, 0, 0))] * 2
        out_shape = [jax.ShapeDtypeStruct((4 * total, STEP // 8, dim), jnp.float32)] * 2
    else:
        out_specs = [rows(STEP, dim)]
        out_shape = [jax.ShapeDtypeStruct((STEP * total, dim), jnp.float32)]
    return pl.pallas_call(
        functools.partial(attend_weights_kernel, split, steps),
        grid=(total,),
        in_specs=[scalars()]
        + [left_spec(a, b, c) for a, b, c in zip(starts, firsts, steps)]
        + [fixed((count, dim)) for _ in rights],
        out_specs=out_specs,
        out_shape=out_shape,
        compiler_params=params(60),
        cost_estimate=cost(6 * count * dim * STEP * total, 4 * (dim * STEP * total + count * 3 * dim)),
    )(core, *lefts, *rights)


def first_kernel(parts, aliased, *refs):
    refs = refs[1:] if aliased else refs
    tokens_ref, d_middle_ref, gain_ref = refs[:3]
    d_proj_refs = refs[3 : 3 + parts]
    weight_refs = refs[3 + parts : 3 + 2 * parts]
    out_ref, sums_ref = refs[3 + 2 * parts :]
    first = dot_nn(d_proj_refs[0][...], weight_refs[0][...])
    for d_proj_ref, weight_ref in zip(d_proj_refs[1:], weight_refs[1:]):
        first = first + dot_nn(d_proj_ref[...], weight_ref[...])
    scaled, inverse = standardize(tokens_ref[...])
    out_ref[...] = d_middle_ref[...] + norm_back(first * gain_ref[...], scaled, inverse)

    @pl.when(pl.program_id(0) == 0)
    def _():
        sums_ref[...] = jnp.zeros_like(sums_ref)

    sums_ref[0:1, :] += jnp.sum(first * scaled, 0, keepdims=True)
    sums_ref[1:2, :] += jnp.sum(first, 0, keepdims=True)


def first_backward(tokens, d_middle, gain, d_projs, weights, begin, images, previous=()):
    dim = tokens.shape[1]
    count = images * PATCHES

    def some(width):
        return pl.BlockSpec((PATCHES, width), lambda i: (begin + i, 0))

    parts = len(d_projs)
    return pl.pallas_call(
        functools.partial(first_kernel, parts, len(previous) > 0),
        grid=(images,),
        in_specs=[pl.BlockSpec(memory_space=pl.ANY) for _ in previous]
        + [some(dim)] * 2
        + [fixed((1, dim))]
        + [some(d.shape[1]) for d in d_projs]
        + [fixed(w.shape) for w in weights],
        out_specs=[some(dim), fixed((8, dim))],
        out_shape=[jax.ShapeDtypeStruct(tokens.shape, jnp.float32), jax.ShapeDtypeStruct((8, dim), jnp.float32)],
        input_output_aliases={0: 0} if previous else {},
        compiler_params=params(60),
        cost_estimate=cost(18 * count * dim * dim, 4 * (3 * dim * dim + 6 * count * dim)),
    )(*previous, tokens, d_middle, gain, *d_projs, *weights)


def settle_units_kernel(first, scale_ref, one_ref, two_ref, hidden_ref, return_ref):
    step = pl.program_id(0)

    def put(ref):
        hidden_ref[...] = (ref[:, 0, 0].reshape(BLOCK, -1) * scale_ref[0]).T
        return_ref[...] = ref[:, 1, 0].reshape(BLOCK, -1) * scale_ref[0]

    pl.when(step < first)(lambda: put(one_ref))
    pl.when(step >= first)(lambda: put(two_ref))


def settle_units(scale, one, two):
    first, second, dim = one.shape[2], two.shape[2], one.shape[4]
    units = (first + second) * BLOCK
    block = (16, 2, 1, PIECE, dim)
    return pl.pallas_call(
        functools.partial(settle_units_kernel, first),
        grid=(first + second,),
        in_specs=[
            scalars(),
            pl.BlockSpec(block, lambda i: (0, 0, jnp.minimum(i, first - 1), 0, 0)),
            pl.BlockSpec(block, lambda i: (0, 0, jnp.maximum(i - first, 0), 0, 0)),
        ],
        out_specs=[pl.BlockSpec((dim, BLOCK), lambda i: (0, i)), rows(BLOCK, dim)],
        out_shape=[
            jax.ShapeDtypeStruct((dim, units), jnp.float32),
            jax.ShapeDtypeStruct((units, dim), jnp.float32),
        ],
        compiler_params=params(40),
        cost_estimate=cost(0, 16 * units * dim),
    )(scale, one, two)


def settle_attend_kernel(scale_ref, value_ref, attend_ref, output_ref):
    step = pl.program_id(0)
    size, dim = attend_ref.shape

    @pl.when(step < 3)
    def _():
        attend_ref[...] = value_ref[:, 0].reshape(size, dim) * scale_ref[0]

    @pl.when(step == 3)
    def _():
        output_ref[...] = value_ref[:, 0].reshape(size, dim) * scale_ref[0]


def settle_attend(scale, value):
    piece, dim = value.shape[2:]
    size = 8 * piece
    return pl.pallas_call(
        settle_attend_kernel,
        grid=(4,),
        in_specs=[scalars(), pl.BlockSpec((8, 1, piece, dim), lambda i: (i % 2, i // 2, 0, 0))],
        out_specs=[
            pl.BlockSpec((size, dim), lambda i: (jnp.minimum(i, 2), 0)),
            pl.BlockSpec((size, dim), lambda i: (0, 0)),
        ],
        out_shape=[
            jax.ShapeDtypeStruct((3 * size, dim), jnp.float32),
            jax.ShapeDtypeStruct((size, dim), jnp.float32),
        ],
        compiler_params=params(40),
        cost_estimate=cost(0, 16 * size * dim),
    )(scale, value)


def offset_matrix():
    place = jnp.arange(PATCHES)
    offset = place // SIDE - place % SIDE + SIDE - 1
    return (jnp.arange(STRIP)[:, None] == offset[None, :]).astype(jnp.float32)


def make_strips(table):
    heads = table.shape[0]
    grid = table.reshape(heads, STRIP, STRIP)[:, ::-1]
    wide = jnp.einsum("hmo,op->hmp", grid, offset_matrix(), precision=HIGHEST)
    wide = wide.reshape(heads, STRIP, SIDE, SIDE).transpose(0, 2, 1, 3).reshape(heads, SIDE, STRIP * SIDE)
    return jnp.pad(wide, ((0, 0), (0, 0), (0, 512 - STRIP * SIDE)))


def table_gradient(d_strips):
    heads = d_strips.shape[0]
    wide = d_strips[:, :, : STRIP * SIDE].reshape(heads, SIDE, STRIP, SIDE).transpose(0, 2, 1, 3)
    grid = jnp.einsum("hmp,op->hmo", wide.reshape(heads, STRIP, PATCHES), offset_matrix(), precision=HIGHEST)
    return grid[:, ::-1].reshape(heads, STRIP * STRIP)


def pick(array, index, axis):
    return lax.dynamic_index_in_dim(array, index, axis, keepdims=False)


def join(*values):
    return lax.optimization_barrier(values)


class Ring:
    def __init__(self):
        place = lax.axis_index("dp")
        self.place = place
        self.bits = [place & 1, (place >> 1) & 1, (place >> 2) & 1, (place >> 3) & 1]

    def across(self, value):
        return lax.ppermute(value, "mp", [(0, 1), (1, 0)])

    def along(self, value, bit):
        return lax.ppermute(value, "dp", [(i, i ^ (1 << bit)) for i in range(16)])

    def ordered(self, mine, theirs, bit, axis=0):
        flag = self.bits[bit] == 0
        return jnp.concatenate([jnp.where(flag, mine, theirs), jnp.where(flag, theirs, mine)], axis)

    def core_half(self, weight, base, count):
        half = count // 2
        return lax.dynamic_slice(weight, (base + self.bits[0] * half, 0), (half, weight.shape[1]))

    def share(self, weight, count, first, width):
        part = count // 16
        return lax.dynamic_slice(weight, (self.place * part, first), (part, width))

    def spread(self, part):
        return lax.all_gather(part, "dp", axis=0, tiled=True)

    def rows_step(self, value, bit):
        return self.ordered(value, self.along(value, bit), bit)


class Reduction:
    def __init__(self, ring, axis):
        self.ring = ring
        self.axis = axis
        self.terms = {}
        self.level = {}

    def begin(self, side, keep, send):
        self.terms[side] = [keep, self.ring.along(send, 0)]
        self.level[side] = 1

    def value(self, side):
        out = self.terms[side][0]
        for term in self.terms[side][1:]:
            out = out + term
        return out

    def send(self, side):
        bit = self.ring.bits[self.level[side]]
        kept = []
        out = 0.0
        for term in self.terms[side]:
            shape = term.shape
            axis = self.axis
            cut = term.reshape(shape[:axis] + (shape[axis] // 2, 2) + shape[axis + 1 :])
            kept.append(pick(cut, bit, axis + 1))
            out = out + pick(cut, 1 - bit, axis + 1)
        self.terms[side] = kept
        return out

    def pass_on(self, side, value):
        self.terms[side].append(self.ring.along(value, self.level[side]))
        self.level[side] += 1

    def cross(self, value):
        self.terms["own"].append(self.ring.across(value))

    def gather(self, value):
        return lax.all_gather(value, "dp", axis=self.axis, tiled=True)

    def back(self, value, bit):
        axis = self.axis
        got = self.ring.along(value, bit)
        value, got = (v.reshape(v.shape[: axis + 1] + (1,) + v.shape[axis + 1 :]) for v in (value, got))
        out = self.ring.ordered(value, got, bit, axis + 1)
        return out.reshape(out.shape[:axis] + (-1,) + out.shape[axis + 2 :])


def body(split, *args):
    (
        tokens, cotangent, bucket, counts, first_gain, first_shift, attend_weight, time_weight, time_table,
        bias_table, output_weight, output_bias, second_gain, second_shift, hidden_weight, hidden_bias,
        return_weight, return_bias,
    ) = args
    own_images, patches, dim = tokens.shape
    images = bucket.shape[0]
    buckets = time_table.shape[0]
    heads_local = bias_table.shape[0]
    width = attend_weight.shape[2]
    units = hidden_bias.shape[0]
    group = lax.axis_index("dp")
    rank = lax.axis_index("mp")
    first_own = rank * own_images
    live = (first_own + jnp.arange(own_images) < counts[group]).astype(jnp.float32)
    inv_total = 1.0 / jnp.sum(counts).astype(jnp.float32)
    core = (group & 1).reshape(1)

    def row(vector):
        return vector.reshape(1, -1)

    def column(vector):
        return vector.reshape(-1, 1)

    tokens2 = tokens.reshape(own_images * patches, dim)
    cotangent2 = cotangent.reshape(own_images * patches, dim)
    onehot = (bucket[:, None] == jnp.arange(buckets)[None, :]).astype(jnp.float32)
    time_vec = jnp.dot(onehot, time_table, precision=HIGHEST)
    time_proj = jnp.einsum("sd,ced->sce", time_vec, time_weight.transpose(0, 2, 1), precision=HIGH)
    attend_own = attend_weight.transpose(0, 2, 1).reshape(3 * width, dim)
    norm_first = (row(first_gain), row(first_shift))
    norm_second = (row(second_gain), row(second_shift))

    def time_gradient(packed):
        d_time_all = packed[:, :-1].reshape(-1, 3, width)
        onehot_all = packed[:, -1:].astype(jnp.int32) == jnp.arange(buckets)[None, :]
        time_all = jnp.dot(onehot_all.astype(jnp.float32), time_table, precision=HIGHEST)
        grad = jnp.einsum("sce,sd->ced", d_time_all * inv_total, time_all, precision=HIGH)
        return grad.transpose(0, 2, 1)

    def absolute(own, other):
        flag = rank == 0
        return jnp.concatenate([jnp.where(flag, own, other), jnp.where(flag, other, own)], 0)

    def times_of(value):
        return value.reshape(own_images, 1, -1)

    if split:
        ring = Ring()
        less = units // BLOCK // 2
        cuts = [(0, less), (less, units // BLOCK - less)]
        table_other = ring.across(bias_table)
        bias_other = row(ring.across(hidden_bias))
        hidden_shares = [ring.share(hidden_weight, dim, first * BLOCK, blocks * BLOCK) for first, blocks in cuts]
        qk = ring.across(ring.share(attend_own, 2 * width, 0, dim))
        values_half = ring.core_half(attend_own, 2 * width, width)
        output_half = ring.core_half(output_weight, 0, width)
        qk, table_other, bias_other, values_half, output_half, time_proj, strips_own = join(
            qk, table_other, bias_other, values_half, output_half, time_proj, make_strips(bias_table)
        )
        attend_qk = ring.spread(qk)
        values_mine = ring.across(values_half)
        output_mine = ring.across(output_half)
        time_mine = lax.dynamic_slice_in_dim(time_proj, first_own, own_images, 0)
        time_theirs = lax.dynamic_slice_in_dim(time_proj, (1 - rank) * own_images, own_images, 0)
        time_other = ring.across(time_theirs)
        own = attend_forward(tokens2, *norm_first, attend_own, times_of(time_mine), strips_own)
        return_halves = [ring.core_half(return_weight, first * BLOCK, blocks * BLOCK) for first, blocks in cuts]
        own, values_mine, output_mine, time_other, return_half, share_1, share_2 = join(
            own, values_mine, output_mine, time_other, return_halves[0], *hidden_shares
        )
        hidden_other = [ring.spread(ring.across(share_1)), ring.spread(ring.across(share_2))]
        output_theirs = ring.along(output_mine, 0)
        strips_other = make_strips(table_other)
        values_full = ring.ordered(values_mine, ring.along(values_mine, 0), 0)
        attend_other = jnp.concatenate([attend_qk, values_full], 0)
        return_mine = ring.across(return_half)
        other = attend_forward(tokens2, *norm_first, attend_other, times_of(time_other), strips_other)
        attend = [attend_own, attend_other]
        other, return_mine, output_mine, output_theirs = join(other, return_mine, output_mine, output_theirs)
        output_other = ring.ordered(output_mine, output_theirs, 0)
        return_theirs = ring.along(return_mine, 0)
        output = [output_weight, output_other]
        middle, *forms = output_forward(
            live, tokens2, cotangent2, [own[3], other[3]], output, row(output_bias), *norm_second
        )
        forms, return_theirs, return_half = join(forms, return_theirs, return_halves[1])
        return_1 = ring.ordered(return_mine, return_theirs, 0)
        return_mine = ring.across(return_half)

        def feed_other(forms, index, hidden, back):
            first, blocks = cuts[index]
            bias = bias_other[:, first * BLOCK : (first + blocks) * BLOCK]
            return feed(True, core, forms, hidden, bias, back, 0, blocks)

        def feed_own(forms, index):
            return feed(True, core, forms, hidden_weight, row(hidden_bias), return_weight, *cuts[index])

        h1, h2, r1, r2, qa, qb = (Reduction(ring, axis) for axis in (1, 1, 1, 1, 0, 0))
        other_1 = feed_other(forms, 0, hidden_other[0], return_1)
        forms, other_1, return_mine = join(forms, other_1, return_mine)
        return_2 = ring.ordered(return_mine, ring.along(return_mine, 0), 0)
        forms, return_2, sent = join(forms, return_2, other_1[3:7])
        h1.begin("other", *sent[:2])
        r1.begin("other", *sent[2:])
        other_2 = feed_other(forms, 1, hidden_other[1], return_2)
        forms, other_2, a, b = join(forms, other_2, h1.value("other"), r1.send("other"))
        h1_cross, r1_y = a, b
        h2.begin("other", *other_2[3:5])
        r2.begin("other", *other_2[5:7])
        h1_crossed = ring.across(h1_cross)
        r1.pass_on("other", r1_y)
        own_1 = feed_own(forms, 0)
        forms, own_1, a, b, h1_crossed, r1.terms["other"] = join(
            forms, own_1, h2.value("other"), r2.send("other"), h1_crossed, r1.terms["other"]
        )
        h1.begin("own", *own_1[3:5])
        r1.begin("own", *own_1[5:7])
        h1.terms["own"].append(h1_crossed)
        h2_crossed = ring.across(a)
        r2.pass_on("other", b)
        own_2 = feed_own(forms, 1)
        middle, own_2, a, b, h2_crossed = join(middle, own_2, r1.send("own"), r1.value("other"), h2_crossed)
        h2.begin("own", *own_2[3:5])
        r2.begin("own", *own_2[5:7])
        h2.terms["own"].append(h2_crossed)
        r1.pass_on("own", a)
        r1.cross(b)
        fed = [other_1, own_1, other_2, own_2]
        result, d_middle, second_sums, d_mixed_own, d_mixed_other = middle_backward(
            live, middle, cotangent2, row(second_gain), row(return_bias), [f[0] for f in fed], [f[1] for f in fed], output
        )
        d_mixed_other, a, b, c = join(d_mixed_other, h1.send("own"), r2.value("other"), r1.send("own"))
        h1.pass_on("own", a)
        r2_crossed = ring.across(b)
        r1.pass_on("own", c)
        attended_other = attend_backward(*other[:4], d_mixed_other, other[5], strips_other)
        attended_other, a, b, c, r2_crossed = join(
            attended_other, h1.send("own"), r1.send("own"), h2.send("own"), r2_crossed
        )
        h1.pass_on("own", a)
        r1.pass_on("own", b)
        h2.pass_on("own", c)

        def pair_up(first, second):
            return jnp.stack([first, second]).reshape(1, -1, dim)

        def weights_a(attended, normed):
            return attend_weights(True, core, [attended[1]], [normed], [0], [2])

        def weights_b(attended, normed, flipped_mixed):
            return attend_weights(True, core, [attended[1], flipped_mixed], [normed, d_middle], [2, 0], [1, 1])

        normed_first = own[6]
        part = attend_weights(
            True, core, [attended_other[1], other[4]], [normed_first, d_middle], [0, 0], [3, 1]
        )
        part, normed_first, d_mixed_own, b, c, d, return_1 = join(
            part, normed_first, d_mixed_own, h1.send("own"), r2.send("own"), h2.send("own"), r1.value("own")
        )
        got = ring.along(part[1], 0)
        for reduction, begin in ((qa, 0), (qb, 8)):
            reduction.terms["other"] = [part[0][begin : begin + 8], got[begin : begin + 8]]
            reduction.level["other"] = 1
        h1.pass_on("own", b)
        r2.pass_on("own", c)
        r2.terms["own"].append(r2_crossed)
        h2.pass_on("own", d)
        attended_own = attend_backward(*own[:4], d_mixed_own, own[5], strips_own)
        attended_own, a, b, c, d, e = join(
            attended_own, qb.send("other"), pair_up(h1.value("own"), return_1), r2.send("own"), h2.send("own"),
            qa.value("other"),
        )
        qb.pass_on("other", a)
        units_1 = ring.spread(b)
        r2.pass_on("own", c)
        h2.pass_on("own", d)
        qa_first = ring.across(e[:4])
        d_time_got = ring.across(attended_other[3].reshape(own_images, 3, width))
        part = weights_b(attended_own, normed_first, own[4])
        part, normed_first, d_time_got = join(part, normed_first, d_time_got)
        d_time = absolute(attended_own[3].reshape(own_images, 3, width), d_time_got)
        packed = jnp.concatenate([d_time.reshape(images, -1), bucket.astype(jnp.float32)[:, None]], 1)
        packed = ring.rows_step(packed, 0)
        qb.begin("own", *part)
        part = weights_a(attended_own, normed_first)
        part, d_projs, a, b, c, qa_first, packed, e = join(
            part, [attended_own[0], attended_other[0]], qb.send("own"), qb.value("other"), r2.send("own"),
            qa_first, packed, e[4:],
        )
        qa.begin("own", *part)
        qa_second = ring.across(e)
        qb.pass_on("own", a)
        qb.cross(b)
        r2.pass_on("own", c)
        packed = ring.rows_step(packed, 1)
        half = own_images // 2
        tokens_a, sums_a = first_backward(tokens2, d_middle, row(first_gain), d_projs, attend, 0, half)
        tokens_a, d_projs, qa_second, qa.terms["own"], b, c, packed = join(
            tokens_a, d_projs, qa_second, qa.terms["own"], qb.send("own"),
            pair_up(h2.value("own"), r2.value("own")), packed,
        )
        qa.terms["own"].append(jnp.concatenate([qa_first, qa_second], 0))
        d_projs, a = join(d_projs, qa.send("own"))
        qa.pass_on("own", a)
        qb.pass_on("own", b)
        units_2 = ring.spread(c)
        packed = ring.rows_step(packed, 2)
        tokens_grad, sums_b = first_backward(
            tokens2, d_middle, row(first_gain), d_projs, attend, half, own_images - half, (tokens_a,)
        )
        tokens_grad, sums_b, a, b, packed, strips_a, strips_b, d_time = join(
            tokens_grad, sums_b, qa.send("own"), qb.send("own"), packed, attended_own[2], attended_other[2], d_time
        )
        qa.pass_on("own", a)
        qb.pass_on("own", b)
        packed = ring.rows_step(packed, 3)
        d_time_vec = jnp.einsum("sce,ced->sd", d_time, time_weight.transpose(0, 2, 1), precision=HIGH)
        time_table_part = jnp.dot(onehot.T, d_time_vec, precision=HIGHEST)
        table_full = absolute(table_gradient(strips_a), table_gradient(strips_b))
        bias_own = jnp.concatenate([own_1[2][0], own_2[2][0]])
        hidden_bias_full = absolute(bias_own, jnp.concatenate([other_1[2][0], other_2[2][0]]))
        first_sums = sums_a + sums_b
        small = [
            first_sums[0], first_sums[1], time_table_part, second_sums[2], second_sums[0], second_sums[1],
            second_sums[3], table_full, hidden_bias_full,
        ]
        flat = jnp.concatenate([v.reshape(-1) for v in small]) * inv_total
        flat = jnp.pad(flat, (0, -flat.shape[0] % 1024)).reshape(-1, 128)
        a, packed, flat = join(qa.send("own"), packed, flat)
        qa.pass_on("own", a)
        flat = flat + ring.along(flat, 0)
        time_weight_grad = time_gradient(packed)
        last = jnp.stack([qa.value("own"), qb.value("own")]).reshape(1, -1, dim)
        last, flat, time_weight_grad, units_1, units_2 = join(last, flat, time_weight_grad, units_1, units_2)
        attend_all = ring.spread(last).reshape(16, 2, -1, dim)
        flat = flat + ring.across(flat)
        scale = inv_total.reshape(1)
        hidden_grad, return_grad = settle_units(
            scale, *(g.reshape(16, 2, -1, PIECE, dim) for g in (units_1, units_2))
        )
        flat, hidden_grad, return_grad = join(flat, hidden_grad, return_grad)
        for bit in (1, 2, 3):
            flat = flat + ring.along(flat, bit)
        attend_weight_grad, output_weight_grad = settle_attend(scale, attend_all)
        attend_weight_grad = attend_weight_grad.reshape(3, width, dim).transpose(0, 2, 1)
    else:
        attend = [lax.all_gather(attend_weight, "mp", axis=2, tiled=True).transpose(0, 2, 1).reshape(-1, dim)]
        output = [lax.all_gather(output_weight, "mp", axis=0, tiled=True)]
        hidden_full = lax.all_gather(hidden_weight, "mp", axis=1, tiled=True)
        return_full = lax.all_gather(return_weight, "mp", axis=0, tiled=True)
        bias_full = lax.all_gather(hidden_bias, "mp", axis=0, tiled=True)
        strips = make_strips(lax.all_gather(bias_table, "mp", axis=0, tiled=True))
        full = lax.all_gather(time_proj, "mp", axis=2, tiled=True)
        times = times_of(lax.dynamic_slice_in_dim(full, first_own, own_images, 0))
        all_of = attend_forward(tokens2, *norm_first, attend[0], times, strips)
        middle, *forms = output_forward(
            live, tokens2, cotangent2, [all_of[3]], output, row(output_bias), *norm_second
        )
        fed = feed(False, core, forms, hidden_full, row(bias_full), return_full, 0, hidden_full.shape[1] // BLOCK)
        result, d_middle, second_sums, d_mixed = middle_backward(
            live, middle, cotangent2, row(second_gain), row(return_bias), [fed[0]], [fed[1]], output
        )
        attended = attend_backward(*all_of[:4], d_mixed, all_of[5], strips)
        (attend_full,) = attend_weights(
            False, core, [attended[1]], [all_of[6]], [0], [attended[1].shape[0] // STEP]
        )
        (output_full,) = attend_weights(False, core, [all_of[4]], [d_middle], [0], [dim // STEP])
        tokens_grad, first_sums = first_backward(
            tokens2, d_middle, row(first_gain), [attended[0]], attend, 0, own_images
        )

        def settle(value, axis):
            return lax.psum(lax.psum_scatter(value * inv_total, "mp", scatter_dimension=axis, tiled=True), "dp")

        hidden_grad = settle(fed[3], 0).T
        return_grad = settle(fed[4], 0)
        attend_weight_grad = settle(attend_full.reshape(3, -1, dim), 1).transpose(0, 2, 1)
        output_weight_grad = settle(output_full, 0)
        table_full = table_gradient(attended[2])
        hidden_bias_full = fed[2][0]
        d_time = lax.all_gather(attended[3].reshape(own_images, 3, -1), "mp", axis=0, tiled=True)
        d_time = lax.dynamic_slice_in_dim(d_time, rank * width, width, 2)

        packed = jnp.concatenate([d_time.reshape(images, -1), bucket.astype(jnp.float32)[:, None]], 1)
        time_weight_grad = time_gradient(lax.all_gather(packed, "dp", axis=0, tiled=True))
        d_time_vec = jnp.einsum("sce,ced->sd", d_time, time_weight.transpose(0, 2, 1), precision=HIGH)
        time_table_part = jnp.dot(onehot.T, d_time_vec, precision=HIGHEST)
        small = [
            first_sums[0], first_sums[1], time_table_part, second_sums[2], second_sums[0], second_sums[1],
            second_sums[3], table_full, hidden_bias_full,
        ]
        flat = lax.psum(jnp.concatenate([v.reshape(-1) for v in small]) * inv_total, ("dp", "mp"))

    flat = flat.reshape(-1)
    sums = []
    start = 0
    for s in small:
        sums.append(flat[start : start + s.size].reshape(s.shape))
        start += s.size
    bias_table_grad = lax.dynamic_slice_in_dim(sums[7], rank * heads_local, heads_local, 0)
    hidden_bias_grad = lax.dynamic_slice_in_dim(sums[8], rank * units, units, 0)
    return (
        result.reshape(tokens.shape),
        tokens_grad.reshape(tokens.shape),
        sums[0],
        sums[1],
        attend_weight_grad,
        time_weight_grad,
        sums[2],
        bias_table_grad,
        output_weight_grad,
        sums[3],
        sums[4],
        sums[5],
        hidden_grad,
        hidden_bias_grad,
        return_grad,
        sums[6],
    )


def solution(mesh):
    in_specs = (
        P(("dp", "mp"), None, None),
        P(("dp", "mp"), None, None),
        P("dp"),
        P(),
        P(),
        P(),
        P(None, None, "mp"),
        P(None, None, "mp"),
        P(),
        P("mp", None),
        P("mp", None),
        P(),
        P(),
        P(),
        P(None, "mp"),
        P("mp"),
        P("mp", None),
        P(),
    )
    out_specs = (
        P(("dp", "mp"), None, None),
        P(("dp", "mp"), None, None),
        P(),
        P(),
        P(None, None, "mp"),
        P(None, None, "mp"),
        P(),
        P("mp", None),
        P("mp", None),
        P(),
        P(),
        P(),
        P(None, "mp"),
        P("mp"),
        P("mp", None),
        P(),
    )
    split = mesh.shape["dp"] == 16 and mesh.shape["mp"] == 2
    return jax.shard_map(
        functools.partial(body, split), mesh=mesh, in_specs=in_specs, out_specs=out_specs, check_vma=False
    )
```

```python
import functools
import math

import jax
import jax.numpy as jnp
from jax import lax
from jax.experimental import pallas as pl
from jax.experimental.pallas import tpu as pltpu
from jax.sharding import PartitionSpec as P

HEAD_DIM = 72
SIDE = 16
PATCHES = SIDE * SIDE
STRIP = 2 * SIDE - 1
EPS = 1e-05
SCALE = HEAD_DIM ** (-0.5)
MIB = 1024 * 1024
HIGHEST = lax.Precision.HIGHEST
HIGH = lax.Precision.HIGH


def dot_nn(a, b):
    return lax.dot_general(a, b, (((1,), (0,)), ((), ())), precision=HIGH, preferred_element_type=jnp.float32)


def dot_nt(a, b):
    return lax.dot_general(a, b, (((1,), (1,)), ((), ())), precision=HIGH, preferred_element_type=jnp.float32)


def dot_tn(a, b):
    return lax.dot_general(a, b, (((0,), (0,)), ((), ())), precision=HIGH, preferred_element_type=jnp.float32)


def standardize(values):
    centre = values - jnp.mean(values, -1, keepdims=True)
    inverse = lax.rsqrt(jnp.mean(centre * centre, -1, keepdims=True) + EPS)
    return centre * inverse, inverse


def norm_back(grad_hat, scaled, inverse):
    return inverse * (
        grad_hat
        - jnp.mean(grad_hat, -1, keepdims=True)
        - scaled * jnp.mean(grad_hat * scaled, -1, keepdims=True)
    )


def head_window(head, width):
    first = head * HEAD_DIM
    start = first // 128 * 128
    stop = min(-(-(first + HEAD_DIM) // 128) * 128, width)
    return start, stop, first - start


def head_mask(head, width):
    start, stop, offset = head_window(head, width)
    lane = lax.broadcasted_iota(jnp.int32, (1, stop - start), 1)
    return (lane >= offset) & (lane < offset + HEAD_DIM)


def fixed(shape, **kw):
    return pl.BlockSpec(shape, lambda i: (0,) * len(shape), pipeline_mode=pl.Buffered(1), **kw)


def rows(count, width):
    return pl.BlockSpec((count, width), lambda i: (i, 0))


def params(limit):
    return pltpu.CompilerParams(dimension_semantics=("arbitrary",), vmem_limit_bytes=limit * MIB)


def cost(flops, nbytes, trans=0):
    return pl.CostEstimate(flops=int(flops) // 1000, bytes_accessed=int(nbytes) // 1000, transcendentals=0)


def halves(value):
    high = value.astype(jnp.bfloat16)
    return high, (value - high.astype(jnp.float32)).astype(jnp.bfloat16)


def mul(a, b, left, right):
    return lax.dot_general(a, b, (((left,), (right,)), ((), ())), preferred_element_type=jnp.float32)


def scalars():
    return pl.BlockSpec(memory_space=pltpu.SMEM)


def build_bias(strip_ref, bias_ref, heads):
    def one(head, carry):
        strip = strip_ref[head]
        for row in range(SIDE):
            shift = (SIDE - 1 - row) * SIDE
            bias_ref[head, row * SIDE : (row + 1) * SIDE, :] = strip[:, shift : shift + PATCHES]
        return carry

    lax.fori_loop(0, heads, one, 0)


def attend_forward_kernel(
    heads, tokens_ref, gain_ref, shift_ref, weight_ref, time_ref, strip_ref,
    query_ref, keys_ref, values_ref, mixed_ref, flipped_ref, lse_ref, normed_ref, bias_ref,
):
    width = query_ref.shape[1]

    @pl.when(pl.program_id(0) == 0)
    def _():
        build_bias(strip_ref, bias_ref, heads)

    scaled, _ = standardize(tokens_ref[...])
    normed = scaled * gain_ref[...] + shift_ref[...]
    normed_ref[...] = normed
    proj = dot_nt(normed, weight_ref[...]) + time_ref[0]
    query_ref[...] = proj[:, :width] * SCALE
    keys_ref[...] = proj[:, width : 2 * width]
    values_ref[...] = proj[:, 2 * width :]
    mixed_ref[...] = jnp.zeros_like(mixed_ref)
    columns = lax.broadcasted_iota(jnp.int32, (1, heads), 1)
    stats = jnp.zeros((PATCHES, heads), jnp.float32)
    for head in range(heads):
        start, stop, _ = head_window(head, width)
        mask = head_mask(head, width)
        query = jnp.where(mask, query_ref[:, start:stop], 0.0)
        scores = dot_nt(query, keys_ref[:, start:stop]) + bias_ref[head]
        peak = jnp.max(scores, -1, keepdims=True)
        weights = jnp.exp(scores - peak)
        total = jnp.sum(weights, -1, keepdims=True)
        values = jnp.where(mask, values_ref[:, start:stop], 0.0)
        mixed_ref[:, start:stop] += dot_nn(weights, values) * (1.0 / total)
        stats = jnp.where(columns == head, peak + jnp.log(total), stats)
    lse_ref[...] = stats
    flipped_ref[...] = mixed_ref[...].T


def attend_forward(tokens, gain, shift, weight, time_proj, strips):
    count, dim = tokens.shape
    heads = strips.shape[0]
    width = weight.shape[0] // 3
    images = count // PATCHES
    piece = jax.ShapeDtypeStruct((count, width), jnp.float32)
    return pl.pallas_call(
        functools.partial(attend_forward_kernel, heads),
        grid=(images,),
        in_specs=[
            rows(PATCHES, dim),
            fixed((1, dim)),
            fixed((1, dim)),
            fixed((3 * width, dim)),
            pl.BlockSpec((1, 1, 3 * width), lambda i: (i, 0, 0)),
            fixed(strips.shape),
        ],
        out_specs=[rows(PATCHES, width)] * 4
        + [pl.BlockSpec((width, PATCHES), lambda i: (0, i)), rows(PATCHES, heads), rows(PATCHES, dim)],
        out_shape=[piece] * 4
        + [
            jax.ShapeDtypeStruct((width, count), jnp.float32),
            jax.ShapeDtypeStruct((count, heads), jnp.float32),
            jax.ShapeDtypeStruct((count, dim), jnp.float32),
        ],
        scratch_shapes=[pltpu.VMEM((heads, PATCHES, PATCHES), jnp.float32)],
        compiler_params=params(56),
        cost_estimate=cost(6 * count * dim * width * 3 + 24 * count * PATCHES * 256 * heads // 2, 4 * (weight.size + 6 * count * width)),
    )(tokens, gain, shift, weight, time_proj, strips)


def output_kernel(parts, *refs):
    live_ref, tokens_ref, cotangent_ref = refs[:3]
    mixed_refs = refs[3 : 3 + parts]
    weight_refs = refs[3 + parts : 3 + 2 * parts]
    bias_ref, gain_ref, shift_ref, middle_ref, pair_ref, grad_ref = refs[3 + 2 * parts :]
    dim = tokens_ref.shape[1]
    middle = tokens_ref[...] + bias_ref[...]
    for mixed_ref, weight_ref in zip(mixed_refs, weight_refs):
        middle = middle + dot_nn(mixed_ref[...], weight_ref[...])
    middle_ref[...] = middle
    scaled, _ = standardize(middle)
    normed = scaled * gain_ref[...] + shift_ref[...]
    pair_ref[:, :dim], pair_ref[:, dim:] = halves(normed)
    grad = cotangent_ref[...] * live_ref[pl.program_id(0)]
    grad_ref[:, :dim], grad_ref[:, dim:] = halves(grad)


def output_forward(live, tokens, cotangent, mixed, weights, bias, gain, shift):
    count, dim = tokens.shape
    parts = len(mixed)
    pair = jax.ShapeDtypeStruct((count, 2 * dim), jnp.bfloat16)
    return pl.pallas_call(
        functools.partial(output_kernel, parts),
        grid=(count // PATCHES,),
        in_specs=[scalars()]
        + [rows(PATCHES, dim)] * 2
        + [rows(PATCHES, m.shape[1]) for m in mixed]
        + [fixed(w.shape) for w in weights]
        + [fixed((1, dim))] * 3,
        out_specs=[
            rows(PATCHES, dim),
            rows(PATCHES, 2 * dim),
            rows(PATCHES, 2 * dim),
        ],
        out_shape=[
            jax.ShapeDtypeStruct((count, dim), jnp.float32),
            pair,
            pair,
        ],
        compiler_params=params(48),
        cost_estimate=cost(6 * count * dim * dim, 4 * (dim * dim + 5 * count * dim)),
    )(live, tokens, cotangent, *mixed, *weights, bias, gain, shift)


BLOCK = 256
PIECE = BLOCK // 16


def feed_kernel(split, core_ref, pair_ref, grad_ref, hidden_ref, bias_ref, return_ref, *refs):
    result_ref, second_ref, d_bias_ref = refs[:3]
    outs = refs[3:-5]
    hidden3_ref, return3_ref, active3_ref, slope3_ref, block_ref = refs[-5:]
    count = pair_ref.shape[0]
    dim = pair_ref.shape[1] // 2
    chunk = min(512, count)

    @pl.when(pl.program_id(0) == 0)
    def _():
        result_ref[...] = jnp.zeros_like(result_ref)
        second_ref[...] = jnp.zeros_like(second_ref)

    d_bias_ref[...] = jnp.zeros_like(d_bias_ref)
    high, low = halves(hidden_ref[...])
    hidden3_ref[:, :BLOCK] = high
    hidden3_ref[:, BLOCK : 2 * BLOCK] = high
    hidden3_ref[:, 2 * BLOCK :] = low
    high, low = halves(return_ref[...])
    return3_ref[:BLOCK] = high
    return3_ref[BLOCK : 2 * BLOCK] = high
    return3_ref[2 * BLOCK :] = low

    for begin in range(0, count, chunk):
        part = slice(begin, begin + chunk)
        hidden = (
            mul(pair_ref[part, :dim], hidden3_ref[:, :BLOCK], 1, 0)
            + mul(pair_ref[part, dim:], hidden3_ref[:, :BLOCK], 1, 0)
            + mul(pair_ref[part, :dim], hidden3_ref[:, 2 * BLOCK :], 1, 0)
            + bias_ref[...]
        )
        d_active = (
            mul(grad_ref[part, :dim], return3_ref[:BLOCK], 1, 1)
            + mul(grad_ref[part, dim:], return3_ref[:BLOCK], 1, 1)
            + mul(grad_ref[part, :dim], return3_ref[2 * BLOCK :], 1, 1)
        )
        cumul = 0.5 * (1.0 + lax.erf(hidden * 2.0 ** (-0.5)))
        high, low = halves(hidden * cumul)
        active3_ref[part, :BLOCK] = high
        active3_ref[part, BLOCK : 2 * BLOCK] = low
        active3_ref[part, 2 * BLOCK :] = high
        density = hidden * jnp.exp(-0.5 * hidden * hidden) * (1.0 / math.sqrt(2.0 * math.pi))
        d_hidden = d_active * (cumul + density)
        high, low = halves(d_hidden)
        slope3_ref[part, :BLOCK] = high
        slope3_ref[part, BLOCK : 2 * BLOCK] = low
        slope3_ref[part, 2 * BLOCK :] = high
        d_bias_ref[...] += jnp.sum(d_hidden, 0, keepdims=True)
        result_ref[part, :] += mul(active3_ref[part, :], return3_ref[...], 1, 0)
        second_ref[part, :] += mul(slope3_ref[part, :], hidden3_ref[...], 1, 1)

    def weight_grad(left_ref, right_ref):
        wide = mul(left_ref[:, :BLOCK], right_ref[...], 0, 0)
        return wide[:, :dim] + wide[:, dim:] + mul(left_ref[:, BLOCK : 2 * BLOCK], right_ref[:, :dim], 0, 0)

    if split:
        block_ref[0] = weight_grad(active3_ref, grad_ref)
        block_ref[1] = weight_grad(slope3_ref, pair_ref)

        def place(index, even_ref, odd_ref):
            for pair in range(8):
                even_ref[0, pair] = block_ref[index, 2 * pair * PIECE : (2 * pair + 1) * PIECE]
                odd_ref[0, pair] = block_ref[index, (2 * pair + 1) * PIECE : (2 * pair + 2) * PIECE]

        @pl.when(core_ref[0] == 0)
        def _():
            place(0, outs[2], outs[3])
            place(1, outs[0], outs[1])

        @pl.when(core_ref[0] == 1)
        def _():
            place(0, outs[3], outs[2])
            place(1, outs[1], outs[0])
    else:
        outs[1][...] = weight_grad(active3_ref, grad_ref)
        outs[0][...] = weight_grad(slope3_ref, pair_ref)


def feed(split, core, tokens_forms, hidden_weight, hidden_bias, return_weight, first, blocks):
    pair, grad = tokens_forms
    count = pair.shape[0]
    dim = pair.shape[1] // 2
    units = blocks * BLOCK
    whole = jax.ShapeDtypeStruct((count, dim), jnp.float32)
    if split:
        out_specs = [pl.BlockSpec((1, 8, PIECE, dim), lambda i: (i, 0, 0, 0))] * 4
        out_shape = [jax.ShapeDtypeStruct((blocks, 8, PIECE, dim), jnp.float32)] * 4
    else:
        out_specs = [rows(BLOCK, dim)] * 2
        out_shape = [jax.ShapeDtypeStruct((units, dim), jnp.float32)] * 2
    return pl.pallas_call(
        functools.partial(feed_kernel, split),
        grid=(blocks,),
        in_specs=[
            scalars(),
            fixed(pair.shape),
            fixed(grad.shape),
            pl.BlockSpec((dim, BLOCK), lambda i: (0, first + i)),
            pl.BlockSpec((1, BLOCK), lambda i: (0, first + i)),
            pl.BlockSpec((BLOCK, dim), lambda i: (first + i, 0)),
        ],
        out_specs=[fixed((count, dim)), fixed((count, dim)), pl.BlockSpec((1, BLOCK), lambda i: (0, i))] + out_specs,
        out_shape=[whole, whole, jax.ShapeDtypeStruct((1, units), jnp.float32)] + out_shape,
        scratch_shapes=[
            pltpu.VMEM((dim, 3 * BLOCK), jnp.bfloat16),
            pltpu.VMEM((3 * BLOCK, dim), jnp.bfloat16),
            pltpu.VMEM((count, 3 * BLOCK), jnp.bfloat16),
            pltpu.VMEM((count, 3 * BLOCK), jnp.bfloat16),
            pltpu.VMEM((2, BLOCK, dim), jnp.float32),
        ],
        compiler_params=params(60),
        cost_estimate=cost(36 * count * dim * units, 4 * (4 * dim * units + 5 * count * dim), 2 * count * units),
    )(core, pair, grad, hidden_weight, hidden_bias, return_weight)


def middle_kernel(parts, feeds, *refs):
    live_ref, middle_ref, cotangent_ref, gain_ref, bias_ref = refs[:5]
    result_parts = refs[5 : 5 + feeds]
    second_parts = refs[5 + feeds : 5 + 2 * feeds]
    weight_refs = refs[5 + 2 * feeds : 5 + 2 * feeds + parts]
    result_ref, d_middle_ref, sums_ref = refs[5 + 2 * feeds + parts : 8 + 2 * feeds + parts]
    mix_refs = refs[8 + 2 * feeds + parts :]
    middle = middle_ref[...]
    grad = cotangent_ref[...] * live_ref[pl.program_id(0)]
    result = middle + bias_ref[...]
    second = second_parts[0][...]
    for part in result_parts:
        result = result + part[...]
    for part in second_parts[1:]:
        second = second + part[...]
    result_ref[...] = result
    scaled, inverse = standardize(middle)
    d_middle = grad + norm_back(second * gain_ref[...], scaled, inverse)
    d_middle_ref[...] = d_middle

    @pl.when(pl.program_id(0) == 0)
    def _():
        sums_ref[...] = jnp.zeros_like(sums_ref)

    sums_ref[0:1, :] += jnp.sum(second * scaled, 0, keepdims=True)
    sums_ref[1:2, :] += jnp.sum(second, 0, keepdims=True)
    sums_ref[2:3, :] += jnp.sum(d_middle, 0, keepdims=True)
    sums_ref[3:4, :] += jnp.sum(grad, 0, keepdims=True)
    for weight_ref, mix_ref in zip(weight_refs, mix_refs):
        mix_ref[...] = dot_nt(d_middle, weight_ref[...])


def middle_backward(live, middle, cotangent, gain, bias, results, seconds, weights):
    count, dim = middle.shape
    parts = len(weights)
    block = jax.ShapeDtypeStruct((count, dim), jnp.float32)
    return pl.pallas_call(
        functools.partial(middle_kernel, parts, len(results)),
        grid=(count // PATCHES,),
        in_specs=[scalars()]
        + [rows(PATCHES, dim)] * 2
        + [fixed((1, dim))] * 2
        + [rows(PATCHES, dim)] * (2 * len(results))
        + [fixed(w.shape) for w in weights],
        out_specs=[rows(PATCHES, dim)] * 2 + [fixed((8, dim))] + [rows(PATCHES, w.shape[0]) for w in weights],
        out_shape=[block, block, jax.ShapeDtypeStruct((8, dim), jnp.float32)]
        + [jax.ShapeDtypeStruct((count, w.shape[0]), jnp.float32) for w in weights],
        compiler_params=params(60),
        cost_estimate=cost(6 * count * dim * dim, 4 * (dim * dim + 9 * count * dim)),
    )(live, middle, cotangent, gain, bias, *results, *seconds, *weights)


def attend_backward_kernel(
    heads, query_ref, keys_ref, values_ref, mixed_ref, grad_ref, lse_ref, strip_ref,
    d_proj_ref, flipped_ref, d_strip_ref, d_time_ref, bias_ref, total_ref, d_query_ref, d_keys_ref, d_values_ref,
):
    width = query_ref.shape[1]
    image = pl.program_id(0)

    @pl.when(image == 0)
    def _():
        build_bias(strip_ref, bias_ref, heads)
        total_ref[...] = jnp.zeros_like(total_ref)

    d_query_ref[...] = jnp.zeros_like(d_query_ref)
    d_keys_ref[...] = jnp.zeros_like(d_keys_ref)
    d_values_ref[...] = jnp.zeros_like(d_values_ref)
    for head in range(heads):
        start, stop, _ = head_window(head, width)
        mask = head_mask(head, width)
        query = jnp.where(mask, query_ref[:, start:stop], 0.0)
        keys = jnp.where(mask, keys_ref[:, start:stop], 0.0)
        grad = jnp.where(mask, grad_ref[:, start:stop], 0.0)
        scores = dot_nt(query, keys) + bias_ref[head]
        prob = jnp.exp(scores - lse_ref[:, head : head + 1])
        d_prob = dot_nt(grad, values_ref[:, start:stop])
        delta = jnp.sum(grad * mixed_ref[:, start:stop], -1, keepdims=True)
        d_scores = prob * (d_prob - delta)
        total_ref[head] += d_scores
        d_values_ref[:, start:stop] += dot_tn(prob, grad)
        d_query_ref[:, start:stop] += dot_nn(d_scores, keys)
        d_keys_ref[:, start:stop] += dot_tn(d_scores, query)
    d_proj_ref[:, :width] = d_query_ref[...] * SCALE
    d_proj_ref[:, width : 2 * width] = d_keys_ref[...]
    d_proj_ref[:, 2 * width :] = d_values_ref[...]
    d_time_ref[0] = jnp.sum(d_proj_ref[...], 0, keepdims=True)
    flipped_ref[:width] = (d_query_ref[...] * SCALE).T
    flipped_ref[width : 2 * width] = d_keys_ref[...].T
    flipped_ref[2 * width :] = d_values_ref[...].T

    @pl.when(image == pl.num_programs(0) - 1)
    def _():
        d_strip_ref[...] = jnp.zeros_like(d_strip_ref)

        def one(head, carry):
            for row in range(SIDE):
                shift = (SIDE - 1 - row) * SIDE
                d_strip_ref[head, :, shift : shift + PATCHES] += total_ref[head, row * SIDE : (row + 1) * SIDE, :]
            return carry

        lax.fori_loop(0, heads, one, 0)


def attend_backward(query, keys, values, mixed, grad, lse, strips):
    count, width = query.shape
    heads = strips.shape[0]
    images = count // PATCHES
    return pl.pallas_call(
        functools.partial(attend_backward_kernel, heads),
        grid=(images,),
        in_specs=[rows(PATCHES, width)] * 5 + [rows(PATCHES, heads), fixed(strips.shape)],
        out_specs=[
            rows(PATCHES, 3 * width),
            pl.BlockSpec((3 * width, PATCHES), lambda i: (0, i)),
            fixed(strips.shape),
            pl.BlockSpec((1, 1, 3 * width), lambda i: (i, 0, 0)),
        ],
        out_shape=[
            jax.ShapeDtypeStruct((count, 3 * width), jnp.float32),
            jax.ShapeDtypeStruct((3 * width, count), jnp.float32),
            jax.ShapeDtypeStruct(strips.shape, jnp.float32),
            jax.ShapeDtypeStruct((images, 1, 3 * width), jnp.float32),
        ],
        scratch_shapes=[pltpu.VMEM((heads, PATCHES, PATCHES), jnp.float32)] * 2
        + [pltpu.VMEM((PATCHES, width), jnp.float32)] * 3,
        compiler_params=params(56),
        cost_estimate=cost(30 * count * PATCHES * 256 * heads, 4 * 9 * count * width),
    )(query, keys, values, mixed, grad, lse, strips)


STEP = 576


def attend_weights_kernel(split, steps, core_ref, *refs):
    lefts, rights = refs[: len(steps)], refs[len(steps) : 2 * len(steps)]
    outs = refs[2 * len(steps) :]
    step = pl.program_id(0)
    piece = STEP // 8
    begin = 0
    for left_ref, right_ref, count in zip(lefts, rights, steps):

        @pl.when((step >= begin) & (step < begin + count))
        def _(left_ref=left_ref, right_ref=right_ref):
            value = dot_nn(left_ref[...], right_ref[...])
            if split:

                def store(even_ref, odd_ref):
                    for pair in range(4):
                        even_ref[pair] = value[2 * pair * piece : (2 * pair + 1) * piece]
                        odd_ref[pair] = value[(2 * pair + 1) * piece : (2 * pair + 2) * piece]

                pl.when(core_ref[0] == 0)(lambda: store(outs[0], outs[1]))
                pl.when(core_ref[0] == 1)(lambda: store(outs[1], outs[0]))
            else:
                outs[0][...] = value

        begin += count


def attend_weights(split, core, lefts, rights, firsts, steps):
    count, dim = rights[0].shape
    total = sum(steps)
    starts = [sum(steps[:i]) for i in range(len(steps))]

    def left_spec(start, first, size):
        return pl.BlockSpec((STEP, count), lambda i: (first + jnp.clip(i - start, 0, size - 1), 0))

    if split:
        out_specs = [pl.BlockSpec((4, STEP // 8, dim), lambda i: (i, 0, 0))] * 2
        out_shape = [jax.ShapeDtypeStruct((4 * total, STEP // 8, dim), jnp.float32)] * 2
    else:
        out_specs = [rows(STEP, dim)]
        out_shape = [jax.ShapeDtypeStruct((STEP * total, dim), jnp.float32)]
    return pl.pallas_call(
        functools.partial(attend_weights_kernel, split, steps),
        grid=(total,),
        in_specs=[scalars()]
        + [left_spec(a, b, c) for a, b, c in zip(starts, firsts, steps)]
        + [fixed((count, dim)) for _ in rights],
        out_specs=out_specs,
        out_shape=out_shape,
        compiler_params=params(60),
        cost_estimate=cost(6 * count * dim * STEP * total, 4 * (dim * STEP * total + count * 3 * dim)),
    )(core, *lefts, *rights)


def first_kernel(parts, aliased, *refs):
    refs = refs[1:] if aliased else refs
    tokens_ref, d_middle_ref, gain_ref = refs[:3]
    d_proj_refs = refs[3 : 3 + parts]
    weight_refs = refs[3 + parts : 3 + 2 * parts]
    out_ref, sums_ref = refs[3 + 2 * parts :]
    first = dot_nn(d_proj_refs[0][...], weight_refs[0][...])
    for d_proj_ref, weight_ref in zip(d_proj_refs[1:], weight_refs[1:]):
        first = first + dot_nn(d_proj_ref[...], weight_ref[...])
    scaled, inverse = standardize(tokens_ref[...])
    out_ref[...] = d_middle_ref[...] + norm_back(first * gain_ref[...], scaled, inverse)

    @pl.when(pl.program_id(0) == 0)
    def _():
        sums_ref[...] = jnp.zeros_like(sums_ref)

    sums_ref[0:1, :] += jnp.sum(first * scaled, 0, keepdims=True)
    sums_ref[1:2, :] += jnp.sum(first, 0, keepdims=True)


def first_backward(tokens, d_middle, gain, d_projs, weights, begin, images, previous=()):
    dim = tokens.shape[1]
    count = images * PATCHES

    def some(width):
        return pl.BlockSpec((PATCHES, width), lambda i: (begin + i, 0))

    parts = len(d_projs)
    return pl.pallas_call(
        functools.partial(first_kernel, parts, len(previous) > 0),
        grid=(images,),
        in_specs=[pl.BlockSpec(memory_space=pl.ANY) for _ in previous]
        + [some(dim)] * 2
        + [fixed((1, dim))]
        + [some(d.shape[1]) for d in d_projs]
        + [fixed(w.shape) for w in weights],
        out_specs=[some(dim), fixed((8, dim))],
        out_shape=[jax.ShapeDtypeStruct(tokens.shape, jnp.float32), jax.ShapeDtypeStruct((8, dim), jnp.float32)],
        input_output_aliases={0: 0} if previous else {},
        compiler_params=params(60),
        cost_estimate=cost(18 * count * dim * dim, 4 * (3 * dim * dim + 6 * count * dim)),
    )(*previous, tokens, d_middle, gain, *d_projs, *weights)


def settle_units_kernel(first, scale_ref, one_ref, two_ref, hidden_ref, return_ref):
    step = pl.program_id(0)

    def put(ref):
        hidden_ref[...] = (ref[:, 0, 0].reshape(BLOCK, -1) * scale_ref[0]).T
        return_ref[...] = ref[:, 1, 0].reshape(BLOCK, -1) * scale_ref[0]

    pl.when(step < first)(lambda: put(one_ref))
    pl.when(step >= first)(lambda: put(two_ref))


def settle_units(scale, one, two):
    first, second, dim = one.shape[2], two.shape[2], one.shape[4]
    units = (first + second) * BLOCK
    block = (16, 2, 1, PIECE, dim)
    return pl.pallas_call(
        functools.partial(settle_units_kernel, first),
        grid=(first + second,),
        in_specs=[
            scalars(),
            pl.BlockSpec(block, lambda i: (0, 0, jnp.minimum(i, first - 1), 0, 0)),
            pl.BlockSpec(block, lambda i: (0, 0, jnp.maximum(i - first, 0), 0, 0)),
        ],
        out_specs=[pl.BlockSpec((dim, BLOCK), lambda i: (0, i)), rows(BLOCK, dim)],
        out_shape=[
            jax.ShapeDtypeStruct((dim, units), jnp.float32),
            jax.ShapeDtypeStruct((units, dim), jnp.float32),
        ],
        compiler_params=params(40),
        cost_estimate=cost(0, 16 * units * dim),
    )(scale, one, two)


def settle_attend_kernel(scale_ref, value_ref, attend_ref, output_ref):
    step = pl.program_id(0)
    size, dim = attend_ref.shape

    @pl.when(step < 3)
    def _():
        attend_ref[...] = value_ref[:, 0].reshape(size, dim) * scale_ref[0]

    @pl.when(step == 3)
    def _():
        output_ref[...] = value_ref[:, 0].reshape(size, dim) * scale_ref[0]


def settle_attend(scale, value):
    piece, dim = value.shape[2:]
    size = 8 * piece
    return pl.pallas_call(
        settle_attend_kernel,
        grid=(4,),
        in_specs=[scalars(), pl.BlockSpec((8, 1, piece, dim), lambda i: (i % 2, i // 2, 0, 0))],
        out_specs=[
            pl.BlockSpec((size, dim), lambda i: (jnp.minimum(i, 2), 0)),
            pl.BlockSpec((size, dim), lambda i: (0, 0)),
        ],
        out_shape=[
            jax.ShapeDtypeStruct((3 * size, dim), jnp.float32),
            jax.ShapeDtypeStruct((size, dim), jnp.float32),
        ],
        compiler_params=params(40),
        cost_estimate=cost(0, 16 * size * dim),
    )(scale, value)


def offset_matrix():
    place = jnp.arange(PATCHES)
    offset = place // SIDE - place % SIDE + SIDE - 1
    return (jnp.arange(STRIP)[:, None] == offset[None, :]).astype(jnp.float32)


def make_strips(table):
    heads = table.shape[0]
    grid = table.reshape(heads, STRIP, STRIP)[:, ::-1]
    wide = jnp.einsum("hmo,op->hmp", grid, offset_matrix(), precision=HIGHEST)
    wide = wide.reshape(heads, STRIP, SIDE, SIDE).transpose(0, 2, 1, 3).reshape(heads, SIDE, STRIP * SIDE)
    return jnp.pad(wide, ((0, 0), (0, 0), (0, 512 - STRIP * SIDE)))


def table_gradient(d_strips):
    heads = d_strips.shape[0]
    wide = d_strips[:, :, : STRIP * SIDE].reshape(heads, SIDE, STRIP, SIDE).transpose(0, 2, 1, 3)
    grid = jnp.einsum("hmp,op->hmo", wide.reshape(heads, STRIP, PATCHES), offset_matrix(), precision=HIGHEST)
    return grid[:, ::-1].reshape(heads, STRIP * STRIP)


def pick(array, index, axis):
    return lax.dynamic_index_in_dim(array, index, axis, keepdims=False)


def join(*values):
    return lax.optimization_barrier(values)


class Ring:
    def __init__(self):
        place = lax.axis_index("dp")
        self.place = place
        self.bits = [place & 1, (place >> 1) & 1, (place >> 2) & 1, (place >> 3) & 1]

    def across(self, value):
        return lax.ppermute(value, "mp", [(0, 1), (1, 0)])

    def along(self, value, bit):
        return lax.ppermute(value, "dp", [(i, i ^ (1 << bit)) for i in range(16)])

    def ordered(self, mine, theirs, bit, axis=0):
        flag = self.bits[bit] == 0
        return jnp.concatenate([jnp.where(flag, mine, theirs), jnp.where(flag, theirs, mine)], axis)

    def core_half(self, weight, base, count):
        half = count // 2
        return lax.dynamic_slice(weight, (base + self.bits[0] * half, 0), (half, weight.shape[1]))

    def share(self, weight, count, first, width):
        part = count // 16
        return lax.dynamic_slice(weight, (self.place * part, first), (part, width))

    def spread(self, part):
        return lax.all_gather(part, "dp", axis=0, tiled=True)

    def rows_step(self, value, bit):
        return self.ordered(value, self.along(value, bit), bit)


class Reduction:
    def __init__(self, ring, axis):
        self.ring = ring
        self.axis = axis
        self.terms = {}
        self.level = {}

    def begin(self, side, keep, send):
        self.terms[side] = [keep, self.ring.along(send, 0)]
        self.level[side] = 1

    def value(self, side):
        out = self.terms[side][0]
        for term in self.terms[side][1:]:
            out = out + term
        return out

    def send(self, side):
        bit = self.ring.bits[self.level[side]]
        kept = []
        out = 0.0
        for term in self.terms[side]:
            shape = term.shape
            axis = self.axis
            cut = term.reshape(shape[:axis] + (shape[axis] // 2, 2) + shape[axis + 1 :])
            kept.append(pick(cut, bit, axis + 1))
            out = out + pick(cut, 1 - bit, axis + 1)
        self.terms[side] = kept
        return out

    def pass_on(self, side, value):
        self.terms[side].append(self.ring.along(value, self.level[side]))
        self.level[side] += 1

    def cross(self, value):
        self.terms["own"].append(self.ring.across(value))

    def gather(self, value):
        return lax.all_gather(value, "dp", axis=self.axis, tiled=True)

    def back(self, value, bit):
        axis = self.axis
        got = self.ring.along(value, bit)
        value, got = (v.reshape(v.shape[: axis + 1] + (1,) + v.shape[axis + 1 :]) for v in (value, got))
        out = self.ring.ordered(value, got, bit, axis + 1)
        return out.reshape(out.shape[:axis] + (-1,) + out.shape[axis + 2 :])


def body(split, *args):
    (
        tokens, cotangent, bucket, counts, first_gain, first_shift, attend_weight, time_weight, time_table,
        bias_table, output_weight, output_bias, second_gain, second_shift, hidden_weight, hidden_bias,
        return_weight, return_bias,
    ) = args
    own_images, patches, dim = tokens.shape
    images = bucket.shape[0]
    buckets = time_table.shape[0]
    heads_local = bias_table.shape[0]
    width = attend_weight.shape[2]
    units = hidden_bias.shape[0]
    group = lax.axis_index("dp")
    rank = lax.axis_index("mp")
    first_own = rank * own_images
    live = (first_own + jnp.arange(own_images) < counts[group]).astype(jnp.float32)
    inv_total = 1.0 / jnp.sum(counts).astype(jnp.float32)
    core = (group & 1).reshape(1)

    def row(vector):
        return vector.reshape(1, -1)

    def column(vector):
        return vector.reshape(-1, 1)

    tokens2 = tokens.reshape(own_images * patches, dim)
    cotangent2 = cotangent.reshape(own_images * patches, dim)
    onehot = (bucket[:, None] == jnp.arange(buckets)[None, :]).astype(jnp.float32)
    time_vec = jnp.dot(onehot, time_table, precision=HIGHEST)
    time_proj = jnp.einsum("sd,ced->sce", time_vec, time_weight.transpose(0, 2, 1), precision=HIGH)
    attend_own = attend_weight.transpose(0, 2, 1).reshape(3 * width, dim)
    norm_first = (row(first_gain), row(first_shift))
    norm_second = (row(second_gain), row(second_shift))

    def time_gradient(packed):
        d_time_all = packed[:, :-1].reshape(-1, 3, width)
        onehot_all = packed[:, -1:].astype(jnp.int32) == jnp.arange(buckets)[None, :]
        time_all = jnp.dot(onehot_all.astype(jnp.float32), time_table, precision=HIGHEST)
        grad = jnp.einsum("sce,sd->ced", d_time_all * inv_total, time_all, precision=HIGH)
        return grad.transpose(0, 2, 1)

    def absolute(own, other):
        flag = rank == 0
        return jnp.concatenate([jnp.where(flag, own, other), jnp.where(flag, other, own)], 0)

    def times_of(value):
        return value.reshape(own_images, 1, -1)

    if split:
        ring = Ring()
        less = units // BLOCK // 2
        cuts = [(0, less), (less, units // BLOCK - less)]
        table_other = ring.across(bias_table)
        bias_other = row(ring.across(hidden_bias))
        hidden_shares = [ring.share(hidden_weight, dim, first * BLOCK, blocks * BLOCK) for first, blocks in cuts]
        qk = ring.across(ring.share(attend_own, 2 * width, 0, dim))
        values_half = ring.core_half(attend_own, 2 * width, width)
        output_half = ring.core_half(output_weight, 0, width)
        qk, table_other, bias_other, values_half, output_half, time_proj, strips_own = join(
            qk, table_other, bias_other, values_half, output_half, time_proj, make_strips(bias_table)
        )
        attend_qk = ring.spread(qk)
        values_mine = ring.across(values_half)
        output_mine = ring.across(output_half)
        time_mine = lax.dynamic_slice_in_dim(time_proj, first_own, own_images, 0)
        time_theirs = lax.dynamic_slice_in_dim(time_proj, (1 - rank) * own_images, own_images, 0)
        time_other = ring.across(time_theirs)
        own = attend_forward(tokens2, *norm_first, attend_own, times_of(time_mine), strips_own)
        return_halves = [ring.core_half(return_weight, first * BLOCK, blocks * BLOCK) for first, blocks in cuts]
        own, values_mine, output_mine, time_other, return_half, share_1, share_2 = join(
            own, values_mine, output_mine, time_other, return_halves[0], *hidden_shares
        )
        hidden_other = [ring.spread(ring.across(share_1)), ring.spread(ring.across(share_2))]
        output_theirs = ring.along(output_mine, 0)
        strips_other = make_strips(table_other)
        values_full = ring.ordered(values_mine, ring.along(values_mine, 0), 0)
        attend_other = jnp.concatenate([attend_qk, values_full], 0)
        return_mine = ring.across(return_half)
        other = attend_forward(tokens2, *norm_first, attend_other, times_of(time_other), strips_other)
        attend = [attend_own, attend_other]
        other, return_mine, output_mine, output_theirs = join(other, return_mine, output_mine, output_theirs)
        output_other = ring.ordered(output_mine, output_theirs, 0)
        return_theirs = ring.along(return_mine, 0)
        output = [output_weight, output_other]
        middle, *forms = output_forward(
            live, tokens2, cotangent2, [own[3], other[3]], output, row(output_bias), *norm_second
        )
        forms, return_theirs, return_half = join(forms, return_theirs, return_halves[1])
        return_1 = ring.ordered(return_mine, return_theirs, 0)
        return_mine = ring.across(return_half)

        def feed_other(forms, index, hidden, back):
            first, blocks = cuts[index]
            bias = bias_other[:, first * BLOCK : (first + blocks) * BLOCK]
            return feed(True, core, forms, hidden, bias, back, 0, blocks)

        def feed_own(forms, index):
            return feed(True, core, forms, hidden_weight, row(hidden_bias), return_weight, *cuts[index])

        h1, h2, r1, r2, qa, qb = (Reduction(ring, axis) for axis in (1, 1, 1, 1, 0, 0))
        other_1 = feed_other(forms, 0, hidden_other[0], return_1)
        forms, other_1, return_mine = join(forms, other_1, return_mine)
        return_2 = ring.ordered(return_mine, ring.along(return_mine, 0), 0)
        forms, return_2, sent = join(forms, return_2, other_1[3:7])
        h1.begin("other", *sent[:2])
        r1.begin("other", *sent[2:])
        other_2 = feed_other(forms, 1, hidden_other[1], return_2)
        forms, other_2, a, b = join(forms, other_2, h1.value("other"), r1.send("other"))
        h1_cross, r1_y = a, b
        h2.begin("other", *other_2[3:5])
        r2.begin("other", *other_2[5:7])
        h1_crossed = ring.across(h1_cross)
        r1.pass_on("other", r1_y)
        own_1 = feed_own(forms, 0)
        forms, own_1, a, b, h1_crossed, r1.terms["other"] = join(
            forms, own_1, h2.value("other"), r2.send("other"), h1_crossed, r1.terms["other"]
        )
        h1.begin("own", *own_1[3:5])
        r1.begin("own", *own_1[5:7])
        h1.terms["own"].append(h1_crossed)
        h2_crossed = ring.across(a)
        r2.pass_on("other", b)
        own_2 = feed_own(forms, 1)
        middle, own_2, a, b, h2_crossed = join(middle, own_2, r1.send("own"), r1.value("other"), h2_crossed)
        h2.begin("own", *own_2[3:5])
        r2.begin("own", *own_2[5:7])
        h2.terms["own"].append(h2_crossed)
        r1.pass_on("own", a)
        r1.cross(b)
        fed = [other_1, own_1, other_2, own_2]
        result, d_middle, second_sums, d_mixed_own, d_mixed_other = middle_backward(
            live, middle, cotangent2, row(second_gain), row(return_bias), [f[0] for f in fed], [f[1] for f in fed], output
        )
        d_mixed_other, a, b, c = join(d_mixed_other, h1.send("own"), r2.value("other"), r1.send("own"))
        h1.pass_on("own", a)
        r2_crossed = ring.across(b)
        r1.pass_on("own", c)
        attended_other = attend_backward(*other[:4], d_mixed_other, other[5], strips_other)
        attended_other, a, b, c, r2_crossed = join(
            attended_other, h1.send("own"), r1.send("own"), h2.send("own"), r2_crossed
        )
        h1.pass_on("own", a)
        r1.pass_on("own", b)
        h2.pass_on("own", c)

        def pair_up(first, second):
            return jnp.stack([first, second]).reshape(1, -1, dim)

        def weights_a(attended, normed):
            return attend_weights(True, core, [attended[1]], [normed], [0], [2])

        def weights_b(attended, normed, flipped_mixed):
            return attend_weights(True, core, [attended[1], flipped_mixed], [normed, d_middle], [2, 0], [1, 1])

        normed_first = own[6]
        part = weights_a(attended_other, normed_first)
        part, normed_first = join(part, normed_first)
        qa.begin("other", *part)
        part = weights_b(attended_other, normed_first, other[4])
        part, d_mixed_own, a, b, c, d, e = join(
            part, d_mixed_own, qa.value("other"), h1.send("own"), r2.send("own"), h2.send("own"), r1.value("own")
        )
        qb.begin("other", *part)
        qa_first = ring.across(a[:4])
        h1.pass_on("own", b)
        r2.pass_on("own", c)
        r2.terms["own"].append(r2_crossed)
        h2.pass_on("own", d)
        return_1 = e
        attended_own = attend_backward(*own[:4], d_mixed_own, own[5], strips_own)
        attended_own, a, b, c, d, e, qa_first = join(
            attended_own, qb.send("other"), pair_up(h1.value("own"), return_1), r2.send("own"), h2.send("own"), a[4:],
            qa_first,
        )
        qb.pass_on("other", a)
        units_1 = ring.spread(b)
        r2.pass_on("own", c)
        h2.pass_on("own", d)
        qa_second = ring.across(e)
        d_time_got = ring.across(attended_other[3].reshape(own_images, 3, width))
        part = weights_b(attended_own, normed_first, own[4])
        part, normed_first, d_time_got = join(part, normed_first, d_time_got)
        d_time = absolute(attended_own[3].reshape(own_images, 3, width), d_time_got)
        packed = jnp.concatenate([d_time.reshape(images, -1), bucket.astype(jnp.float32)[:, None]], 1)
        packed = ring.rows_step(packed, 0)
        qb.begin("own", *part)
        part = weights_a(attended_own, normed_first)
        part, d_projs, a, b, c, qa_second, packed = join(
            part, [attended_own[0], attended_other[0]], qb.send("own"), qb.value("other"), r2.send("own"),
            qa_second, packed,
        )
        qa.begin("own", *part)
        qa.terms["own"].append(jnp.concatenate([qa_first, qa_second], 0))
        qb.pass_on("own", a)
        qb.cross(b)
        r2.pass_on("own", c)
        packed = ring.rows_step(packed, 1)
        half = own_images // 2
        tokens_a, sums_a = first_backward(tokens2, d_middle, row(first_gain), d_projs, attend, 0, half)
        tokens_a, d_projs, a, b, c, packed = join(
            tokens_a, d_projs, qa.send("own"), qb.send("own"), pair_up(h2.value("own"), r2.value("own")), packed
        )
        qa.pass_on("own", a)
        qb.pass_on("own", b)
        units_2 = ring.spread(c)
        packed = ring.rows_step(packed, 2)
        tokens_grad, sums_b = first_backward(
            tokens2, d_middle, row(first_gain), d_projs, attend, half, own_images - half, (tokens_a,)
        )
        tokens_grad, sums_b, a, b, packed, strips_a, strips_b, d_time = join(
            tokens_grad, sums_b, qa.send("own"), qb.send("own"), packed, attended_own[2], attended_other[2], d_time
        )
        qa.pass_on("own", a)
        qb.pass_on("own", b)
        packed = ring.rows_step(packed, 3)
        d_time_vec = jnp.einsum("sce,ced->sd", d_time, time_weight.transpose(0, 2, 1), precision=HIGH)
        time_table_part = jnp.dot(onehot.T, d_time_vec, precision=HIGHEST)
        table_full = absolute(table_gradient(strips_a), table_gradient(strips_b))
        bias_own = jnp.concatenate([own_1[2][0], own_2[2][0]])
        hidden_bias_full = absolute(bias_own, jnp.concatenate([other_1[2][0], other_2[2][0]]))
        first_sums = sums_a + sums_b
        small = [
            first_sums[0], first_sums[1], time_table_part, second_sums[2], second_sums[0], second_sums[1],
            second_sums[3], table_full, hidden_bias_full,
        ]
        flat = jnp.concatenate([v.reshape(-1) for v in small]) * inv_total
        flat = jnp.pad(flat, (0, -flat.shape[0] % 1024)).reshape(-1, 128)
        a, packed, flat = join(qa.send("own"), packed, flat)
        qa.pass_on("own", a)
        flat = flat + ring.along(flat, 0)
        time_weight_grad = time_gradient(packed)
        last = jnp.stack([qa.value("own"), qb.value("own")]).reshape(1, -1, dim)
        last, flat, time_weight_grad, units_1, units_2 = join(last, flat, time_weight_grad, units_1, units_2)
        attend_all = ring.spread(last).reshape(16, 2, -1, dim)
        flat = flat + ring.across(flat)
        scale = inv_total.reshape(1)
        hidden_grad, return_grad = settle_units(
            scale, *(g.reshape(16, 2, -1, PIECE, dim) for g in (units_1, units_2))
        )
        flat, hidden_grad, return_grad = join(flat, hidden_grad, return_grad)
        for bit in (1, 2, 3):
            flat = flat + ring.along(flat, bit)
        attend_weight_grad, output_weight_grad = settle_attend(scale, attend_all)
        attend_weight_grad = attend_weight_grad.reshape(3, width, dim).transpose(0, 2, 1)
    else:
        attend = [lax.all_gather(attend_weight, "mp", axis=2, tiled=True).transpose(0, 2, 1).reshape(-1, dim)]
        output = [lax.all_gather(output_weight, "mp", axis=0, tiled=True)]
        hidden_full = lax.all_gather(hidden_weight, "mp", axis=1, tiled=True)
        return_full = lax.all_gather(return_weight, "mp", axis=0, tiled=True)
        bias_full = lax.all_gather(hidden_bias, "mp", axis=0, tiled=True)
        strips = make_strips(lax.all_gather(bias_table, "mp", axis=0, tiled=True))
        full = lax.all_gather(time_proj, "mp", axis=2, tiled=True)
        times = times_of(lax.dynamic_slice_in_dim(full, first_own, own_images, 0))
        all_of = attend_forward(tokens2, *norm_first, attend[0], times, strips)
        middle, *forms = output_forward(
            live, tokens2, cotangent2, [all_of[3]], output, row(output_bias), *norm_second
        )
        fed = feed(False, core, forms, hidden_full, row(bias_full), return_full, 0, hidden_full.shape[1] // BLOCK)
        result, d_middle, second_sums, d_mixed = middle_backward(
            live, middle, cotangent2, row(second_gain), row(return_bias), [fed[0]], [fed[1]], output
        )
        attended = attend_backward(*all_of[:4], d_mixed, all_of[5], strips)
        (attend_full,) = attend_weights(
            False, core, [attended[1]], [all_of[6]], [0], [attended[1].shape[0] // STEP]
        )
        (output_full,) = attend_weights(False, core, [all_of[4]], [d_middle], [0], [dim // STEP])
        tokens_grad, first_sums = first_backward(
            tokens2, d_middle, row(first_gain), [attended[0]], attend, 0, own_images
        )

        def settle(value, axis):
            return lax.psum(lax.psum_scatter(value * inv_total, "mp", scatter_dimension=axis, tiled=True), "dp")

        hidden_grad = settle(fed[3], 0).T
        return_grad = settle(fed[4], 0)
        attend_weight_grad = settle(attend_full.reshape(3, -1, dim), 1).transpose(0, 2, 1)
        output_weight_grad = settle(output_full, 0)
        table_full = table_gradient(attended[2])
        hidden_bias_full = fed[2][0]
        d_time = lax.all_gather(attended[3].reshape(own_images, 3, -1), "mp", axis=0, tiled=True)
        d_time = lax.dynamic_slice_in_dim(d_time, rank * width, width, 2)

        packed = jnp.concatenate([d_time.reshape(images, -1), bucket.astype(jnp.float32)[:, None]], 1)
        time_weight_grad = time_gradient(lax.all_gather(packed, "dp", axis=0, tiled=True))
        d_time_vec = jnp.einsum("sce,ced->sd", d_time, time_weight.transpose(0, 2, 1), precision=HIGH)
        time_table_part = jnp.dot(onehot.T, d_time_vec, precision=HIGHEST)
        small = [
            first_sums[0], first_sums[1], time_table_part, second_sums[2], second_sums[0], second_sums[1],
            second_sums[3], table_full, hidden_bias_full,
        ]
        flat = lax.psum(jnp.concatenate([v.reshape(-1) for v in small]) * inv_total, ("dp", "mp"))

    flat = flat.reshape(-1)
    sums = []
    start = 0
    for s in small:
        sums.append(flat[start : start + s.size].reshape(s.shape))
        start += s.size
    bias_table_grad = lax.dynamic_slice_in_dim(sums[7], rank * heads_local, heads_local, 0)
    hidden_bias_grad = lax.dynamic_slice_in_dim(sums[8], rank * units, units, 0)
    return (
        result.reshape(tokens.shape),
        tokens_grad.reshape(tokens.shape),
        sums[0],
        sums[1],
        attend_weight_grad,
        time_weight_grad,
        sums[2],
        bias_table_grad,
        output_weight_grad,
        sums[3],
        sums[4],
        sums[5],
        hidden_grad,
        hidden_bias_grad,
        return_grad,
        sums[6],
    )


def solution(mesh):
    in_specs = (
        P(("dp", "mp"), None, None),
        P(("dp", "mp"), None, None),
        P("dp"),
        P(),
        P(),
        P(),
        P(None, None, "mp"),
        P(None, None, "mp"),
        P(),
        P("mp", None),
        P("mp", None),
        P(),
        P(),
        P(),
        P(None, "mp"),
        P("mp"),
        P("mp", None),
        P(),
    )
    out_specs = (
        P(("dp", "mp"), None, None),
        P(("dp", "mp"), None, None),
        P(),
        P(),
        P(None, None, "mp"),
        P(None, None, "mp"),
        P(),
        P("mp", None),
        P("mp", None),
        P(),
        P(),
        P(),
        P(None, "mp"),
        P("mp"),
        P("mp", None),
        P(),
    )
    split = mesh.shape["dp"] == 16 and mesh.shape["mp"] == 2
    return jax.shard_map(
        functools.partial(body, split), mesh=mesh, in_specs=in_specs, out_specs=out_specs, check_vma=False
    )
```
